512 devices in a mesh: dp: 32 (over y, z_hi, core), image: 16 (over z_lo, x).
Axes of the slice: x: 4, y: 8, z: 8 (z_hi: 2, z_lo: 4; z = z_hi * 4 + z_lo), core: 2. Of those that a mesh axis runs over, the one named last changes fastest.
Arguments:
- queries: bfloat16 [64, 1024, 4096], P('dp', 'image'), may hold values from -6 to 6
- vision: bfloat16 [64, 16, 8, 8192], P('dp', 'image'), may hold values from -40 to 40
- cotangent: bfloat16 [64, 1024, 4096], P('dp', 'image'), may hold values from -16 to 16
- assignment: int32 [32, 2], P('dp'), may hold values from 0 to 1, each once within a row
- frame_counts: int32 [64], P('dp'), may hold values from 4 to 16, as said below
- lambdas: float32 [4, 16, 128], replicated, may hold values from -2.5 to 2.5
- norm_gain: float32 [256], replicated, may hold values from 0.1 to 1.9
- gate_logit: float32 [1], replicated, may hold values from 0.3 to 1.5
Outputs:
- grad_queries: bfloat16 [64, 1024, 4096], P('dp', 'image')
- grad_vision: bfloat16 [64, 16, 8, 8192], P('dp', 'image')
- grad_lambdas: float32 [4, 16, 128], replicated
- grad_gain: float32 [256], replicated
- grad_gate: float32 [1], replicated
The draws below stay inside these ranges and needn't reach their ends.
Inputs may be any that keep to these rules, and one draw needn't show every extreme that they name: `assignment`: for each index of dp, its 2 sequences attend to its 2 videos, each video to exactly one sequence. A video's first frame_counts frames are used; some video uses all 16.
All inputs are finite; a program needn't handle non-finite values.
Results may differ from the reference program's by a relative error of at most 0.017.
Values may be sent and summed in bfloat16 or wider, within the bound.
No kernel may reach another device: no remote copies, remote signals or barrier semaphores. Data moves between devices by JAX's collectives and lax.ppermute only.
A program may use at most 64 MiB of HBM per device.

```python
import math
import jax
import jax.numpy as jnp
from jax import lax

H = 16
DH = 128
SEQS = 2
PATCH = 8
LEN = 1024
FRAMES = 16
SEQUENCES = 64
VIDEOS = 64


def draw_queries(key, part):
    key = jax.random.fold_in(key, 11)
    shape = (SEQUENCES, LEN, 2 * H * DH)
    values = jnp.clip(jax.random.normal(key, shape, jnp.float32), -6.0, 6.0)
    return values.astype(jnp.bfloat16)


def draw_vision(key, part):
    key = jax.random.fold_in(key, 23)
    column_key, value_key = jax.random.split(key)
    spread = jnp.exp(jax.random.uniform(column_key, (2 * H * DH,), jnp.float32, 0.0, math.log(10.0)))
    scales = jnp.concatenate([jnp.ones((2 * H * DH,), jnp.float32), spread])
    shape = (VIDEOS, FRAMES, PATCH, 4 * H * DH)
    values = jnp.clip(jax.random.normal(value_key, shape, jnp.float32), -4.0, 4.0) * scales
    return values.astype(jnp.bfloat16)


def draw_cotangent(key, part):
    key = jax.random.fold_in(key, 37)
    shape = (SEQUENCES, LEN, 2 * H * DH)
    ramp = (jnp.arange(SEQUENCES)[:, None] * LEN + jnp.arange(LEN)[None, :]).astype(jnp.float32)
    ramp = ramp / float(SEQUENCES * LEN - 1)
    values = jnp.clip(jax.random.normal(key, shape, jnp.float32), -4.0, 4.0) * jnp.power(3.0, ramp)[:, :, None]
    return values.astype(jnp.bfloat16)


def draw_frame_counts(key, part):
    key = jax.random.fold_in(key, 41)
    first_key, second_key = jax.random.split(key)
    lowest = max(1, FRAMES // 4)
    counts = jax.random.randint(first_key, (VIDEOS,), lowest, FRAMES + 1)
    filled = jax.random.randint(second_key, (), 0, VIDEOS)
    counts = jnp.where(jnp.arange(VIDEOS) == filled, FRAMES, counts)
    return counts.astype(jnp.int32)


def gaussian(stream_key, dims, scale, most, kind=jnp.bfloat16):
    drawn = scale * jax.random.normal(stream_key, dims, jnp.float32)
    return jnp.clip(drawn, min=-most, max=most).astype(kind)


def setup_inputs(seed: int = 0) -> dict:
    keys = jax.random.split(jax.random.key(seed), 9)
    queries = draw_queries(jax.random.fold_in(keys[8], 71), 0)
    vision = draw_vision(jax.random.fold_in(keys[8], 71), 0)
    cotangent = draw_cotangent(jax.random.fold_in(keys[8], 71), 0)
    assignment = jax.vmap(lambda own: jax.random.permutation(own, SEQS))(jax.random.split(keys[3], (VIDEOS // SEQS))).reshape((VIDEOS // SEQS, SEQS)).astype(jnp.int32)
    frame_counts = draw_frame_counts(jax.random.fold_in(keys[8], 71), 0)
    lambdas = gaussian(keys[5], (4, H, DH), 0.2, 2.5, jnp.float32)
    norm_gain = jnp.clip(1.0 + 0.18 * jax.random.normal(keys[6], (2 * DH,), jnp.float32), 0.1, 1.9)
    gate_logit = jnp.clip(jax.random.uniform(keys[7], (1,), jnp.float32, 0.3, 1.5), 0.3, 1.5)
    return dict(queries=queries, vision=vision, cotangent=cotangent, assignment=assignment, frame_counts=frame_counts, lambdas=lambdas, norm_gain=norm_gain, gate_logit=gate_logit)


rate_offset = 0.8
epsilon = 1e-05

def rates_of(lambdas):
    first_exp = jnp.exp(lax.optimization_barrier(jnp.sum(lambdas[0] * lambdas[1], axis=-1)))
    second_exp = jnp.exp(lax.optimization_barrier(jnp.sum(lambdas[2] * lambdas[3], axis=-1)))
    return (first_exp - second_exp + rate_offset, first_exp, second_exp)

def attend(query_maps, grad_out, key_rows, value_rows, count, head_rates, norm_gain, gate_tanh):
    score_scale = query_maps.shape[-1] ** (-0.5)
    query_wide = query_maps.astype(jnp.float32)
    key_wide = key_rows.astype(jnp.float32)
    value_wide = value_rows.astype(jnp.float32)
    usable = jnp.arange(key_rows.shape[0], dtype=jnp.int32) // PATCH < count
    scores = jnp.einsum('lmhd,kmhd->mhlk', query_wide, key_wide) * score_scale
    scores = jnp.where(usable[None, None, None, :], scores, -jnp.inf)
    shifted = jnp.exp(scores - lax.optimization_barrier(jnp.max(scores, axis=-1, keepdims=True)))
    probability = shifted / lax.optimization_barrier(jnp.sum(shifted, axis=-1, keepdims=True))
    mixed = (probability[0] - head_rates[:, None, None] * probability[1]).astype(jnp.bfloat16)
    attended = jnp.einsum('hlk,khe->lhe', mixed.astype(jnp.float32), value_wide)
    inverse_rms = lax.rsqrt(lax.optimization_barrier(jnp.mean(attended * attended, axis=-1, keepdims=True)) + epsilon)
    normed = attended * inverse_rms
    output_scale = gate_tanh * (1.0 - rate_offset)
    grad_wide = grad_out.astype(jnp.float32)
    grad_gate = jnp.sum(grad_wide * normed * norm_gain) * (1.0 - rate_offset) * (1.0 - gate_tanh * gate_tanh)
    grad_gain = lax.optimization_barrier(jnp.sum(grad_wide * normed, axis=(0, 1))) * output_scale
    scaled_grad = grad_wide * output_scale * norm_gain
    grad_attended = inverse_rms * (scaled_grad - normed * lax.optimization_barrier(jnp.mean(scaled_grad * normed, axis=-1, keepdims=True)))
    grad_attended = grad_attended.astype(jnp.bfloat16).astype(jnp.float32)
    grad_mixed = jnp.einsum('lhe,khe->hlk', grad_attended, value_wide)
    grad_values = jnp.einsum('hlk,lhe->khe', mixed.astype(jnp.float32), grad_attended)
    grad_rate = -lax.optimization_barrier(jnp.sum(grad_mixed * probability[1], axis=(1, 2)))
    grad_probs = jnp.stack([grad_mixed, -head_rates[:, None, None] * grad_mixed])
    grad_scores = probability * (grad_probs - lax.optimization_barrier(jnp.sum(grad_probs * probability, axis=-1, keepdims=True))) * score_scale
    grad_scores = grad_scores.astype(jnp.bfloat16).astype(jnp.float32)
    grad_query = jnp.einsum('mhlk,kmhd->lmhd', grad_scores, key_wide)
    grad_key = jnp.einsum('mhlk,lmhd->kmhd', grad_scores, query_wide)
    return (grad_query.astype(jnp.bfloat16), grad_key.astype(jnp.bfloat16), grad_values.astype(jnp.bfloat16), grad_rate, grad_gain, grad_gate)

def reference(queries, vision, cotangent, assignment, frame_counts, lambdas, norm_gain, gate_logit):
    head_rates, first_exp, second_exp = rates_of(lambdas)
    gate_tanh = jnp.tanh(gate_logit[0])
    key_all = vision[..., :2 * H * DH].reshape(VIDEOS, FRAMES * PATCH, 2, H, DH)
    value_all = vision[..., 2 * H * DH:].reshape(VIDEOS, FRAMES * PATCH, H, 2 * DH)
    video_of = jnp.arange(SEQUENCES, dtype=jnp.int32) // SEQS * SEQS + assignment.reshape(-1).astype(jnp.int32)

    def per_sequence(sequence):
        video = video_of[sequence]
        query_maps = queries[sequence].reshape(LEN, 2, H, DH)
        grad_out = cotangent[sequence].reshape(LEN, H, 2 * DH)
        return attend(query_maps, grad_out, key_all[video], value_all[video], frame_counts[video], head_rates, norm_gain, gate_tanh)
    grad_query, grad_key, grad_values, grad_rate, grad_gain, grad_gate = lax.map(per_sequence, jnp.arange(SEQUENCES, dtype=jnp.int32))
    grad_queries = grad_query.reshape(SEQUENCES, LEN, 2 * H * DH)
    per_video = jnp.concatenate([grad_key.reshape(SEQUENCES, FRAMES, PATCH, 2 * H * DH), grad_values.reshape(SEQUENCES, FRAMES, PATCH, 2 * H * DH)], axis=-1)
    grad_vision = jnp.zeros((VIDEOS, FRAMES, PATCH, 4 * H * DH), jnp.bfloat16).at[video_of].set(per_video)
    total_rate = lax.optimization_barrier(jnp.sum(grad_rate, axis=0))
    weight_one = (total_rate * first_exp)[:, None]
    weight_two = (total_rate * second_exp)[:, None]
    grad_lambdas = jnp.stack([weight_one * lambdas[1], weight_one * lambdas[0], -weight_two * lambdas[3], -weight_two * lambdas[2]])
    return (grad_queries, grad_vision, grad_lambdas, lax.optimization_barrier(jnp.sum(grad_gain, axis=0)), jnp.sum(grad_gate).reshape(1))
```

```python
import functools

import jax
import jax.numpy as jnp
from jax import lax
from jax.experimental import pallas as pl
from jax.experimental.pallas import tpu as pltpu
from jax.sharding import Mesh, PartitionSpec as P

rate_offset = 0.8
epsilon = 1e-05
DP = ("y", "zh", "core")
IMAGE = ("zl", "x")
FIRST, SECOND = 32, 16
PARTS = 4
VMEM = pl.BlockSpec(memory_space=pltpu.VMEM)
SMEM = pl.BlockSpec(memory_space=pltpu.SMEM)
ANY = pl.BlockSpec(memory_space=pl.ANY)
LIMIT = pltpu.CompilerParams(vmem_limit_bytes=32 * 2**20)
f32, bf16 = jnp.float32, jnp.bfloat16


def dot(a, b, contract):
    return lax.dot_general(
        a, b, ((contract[:1], contract[1:]), ((), ())), preferred_element_type=f32
    )


def wrap(index):
    return lax.rem(index + PARTS, PARTS)


def pack_vision_body(vision, out):
    half = vision.shape[1] // 4
    width = half // PARTS
    for g in range(PARTS):
        out[g, :, :width] = vision[:, g * width : (g + 1) * width]
        out[g, :, width : 2 * width] = vision[:, half + g * width : half + (g + 1) * width]
        out[g, :, 2 * width :] = vision[
            :, 2 * half + 2 * g * width : 2 * half + 2 * (g + 1) * width
        ]


def pack_text_body(place, queries, cotangent, *refs):
    outs, sems = refs[:PARTS], refs[PARTS]
    half = queries.shape[2] // 2
    width = half // PARTS
    copies = []
    for shift in range(PARTS):
        g = wrap(place[1] + shift)
        first = pl.multiple_of(g * width, width)
        second = pl.multiple_of(half + g * width, width)
        wide = pl.multiple_of(g * 2 * width, 2 * width)
        pieces = (
            (queries.at[:, :, pl.ds(first, width)], pl.ds(0, width)),
            (queries.at[:, :, pl.ds(second, width)], pl.ds(width, width)),
            (cotangent.at[:, :, pl.ds(wide, 2 * width)], pl.ds(2 * width, 2 * width)),
        )
        for i, (source, columns) in enumerate(pieces):
            copies.append(
                pltpu.make_async_copy(source, outs[shift].at[:, :, columns], sems.at[shift, i])
            )
    for copy in copies:
        copy.start()
    for copy in copies:
        copy.wait()


def attend_body(
    place, assignment, counts, lambdas, norm_gain, gate, *refs, heads, head_size, patch
):
    text, vision, grad_text, grad_vision = (refs[i * PARTS : (i + 1) * PARTS] for i in range(4))
    stats = refs[4 * PARTS]
    zl, x = place[0], place[1]
    seqs, toks = text[0].shape[0], text[0].shape[1]
    frames = PARTS * PARTS
    keys = frames * patch
    width = heads * head_size
    scale = head_size ** (-0.5)
    output_scale = jnp.tanh(gate[...]) * (1.0 - rate_offset)
    gain_row = norm_gain[...] * output_scale
    first_exp = jnp.exp(jnp.sum(lambdas[0] * lambdas[1], axis=-1, keepdims=True))
    second_exp = jnp.exp(jnp.sum(lambdas[2] * lambdas[3], axis=-1, keepdims=True))
    all_rates = first_exp - second_exp + rate_offset
    head_index = lax.broadcasted_iota(jnp.int32, all_rates.shape, 0)
    spot = lax.broadcasted_iota(jnp.int32, (1, keys), 1) // patch
    part = spot // PARTS
    frame = wrap(zl - part) * PARTS + spot - part * PARTS
    raw_gain = jnp.zeros((1, 2 * head_size), f32)
    lane = lax.broadcasted_iota(jnp.int32, (1, head_size), 1)
    rate_row = jnp.zeros((1, head_size), f32)

    def block(columns):
        wide = jnp.concatenate([part[:, :, columns] for part in vision], axis=0)
        return wide.astype(f32).reshape(frames, seqs, patch, -1)

    def of_video(wide, v):
        return wide[:, v].reshape(keys, -1).astype(bf16)

    for h in range(heads):
        rate = jnp.sum(
            jnp.where(head_index == x * heads + h, all_rates, 0.0), axis=0, keepdims=True
        )
        map_columns = [pl.ds(m * width + h * head_size, head_size) for m in range(2)]
        value_columns = pl.ds(2 * width + 2 * h * head_size, 2 * head_size)
        wide_keys = [block(c) for c in map_columns]
        wide_values = block(value_columns)
        grad_keys, grad_values = ([[], []], [])
        total_rate = jnp.zeros((1, 1), f32)
        for v in range(seqs):
            s = jnp.where(assignment[0, 0] == v, 0, 1)
            usable = frame < counts[v]
            value_rows = of_video(wide_values, v)
            key_rows, query_rows, probs = [], [], []
            for m in range(2):
                k = of_video(wide_keys[m], v)
                q = jnp.concatenate([t[s, :, map_columns[m]] for t in text], axis=0)
                scores = dot(q, k, (1, 1)) * scale
                scores = jnp.where(usable, scores, -jnp.inf)
                shifted = jnp.exp(scores - jnp.max(scores, axis=-1, keepdims=True))
                probs.append(shifted / jnp.sum(shifted, axis=-1, keepdims=True))
                key_rows.append(k)
                query_rows.append(q)
            mixed = (probs[0] - rate * probs[1]).astype(bf16)
            attended = dot(mixed, value_rows, (1, 0))
            inverse_rms = lax.rsqrt(
                jnp.mean(attended * attended, axis=-1, keepdims=True) + epsilon
            )
            normed = attended * inverse_rms
            grad_out = jnp.concatenate([t[s, :, value_columns] for t in text], axis=0).astype(f32)
            raw_gain = raw_gain + jnp.sum(grad_out * normed, axis=0, keepdims=True)
            scaled = grad_out * gain_row
            grad_attended = (
                inverse_rms
                * (scaled - normed * jnp.mean(scaled * normed, axis=-1, keepdims=True))
            ).astype(bf16)
            grad_mixed = dot(grad_attended, value_rows, (1, 1))
            grad_values.append(dot(mixed, grad_attended, (0, 0)).reshape(frames, patch, -1))
            sums = [jnp.sum(grad_mixed * p, axis=-1, keepdims=True) for p in probs]
            total_rate = total_rate - jnp.sum(sums[1], axis=0, keepdims=True)
            factors = (scale, -rate * scale)
            for m in range(2):
                grad_scores = (probs[m] * (grad_mixed - sums[m]) * factors[m]).astype(bf16)
                grad_query = dot(grad_scores, key_rows[m], (1, 0)).astype(bf16)
                for i in range(PARTS):
                    grad_text[i][s, :, map_columns[m]] = grad_query[i * toks : (i + 1) * toks]
                grad_key = dot(grad_scores, query_rows[m], (0, 0))
                grad_keys[m].append(grad_key.reshape(frames, patch, -1))
        for columns, parts in (
            (map_columns[0], grad_keys[0]),
            (map_columns[1], grad_keys[1]),
            (value_columns, grad_values),
        ):
            joined = jnp.concatenate(parts, axis=1).astype(bf16)
            for j in range(PARTS):
                grad_vision[j][:, :, columns] = joined[j * PARTS : (j + 1) * PARTS]
        rate_row = jnp.where(lane == x * heads + h, total_rate, rate_row)
    row = lax.broadcasted_iota(jnp.int32, stats.shape[1:], 0)
    tile = jnp.where(row == 0, raw_gain[:, :head_size], 0.0)
    tile = jnp.where(row == 1, raw_gain[:, head_size:], tile)
    tile = jnp.where(row == 2, rate_row, tile)
    for i in range(stats.shape[0]):
        stats[i] = tile


def sum_parts(refs):
    total = refs[0][...].astype(f32)
    for part in refs[1:]:
        total = total + part[...].astype(f32)
    return total


def sum_vision_body(*refs):
    refs[PARTS][...] = sum_parts(refs[:PARTS]).astype(bf16)


def spread_sum_body(tiles, out):
    total = jnp.sum(tiles[...], axis=0)
    for i in range(out.shape[0]):
        out[i] = total


def finish_body(tiles, lambdas, norm_gain, gate, grad_lambdas, grad_gain, grad_gate):
    total = jnp.sum(tiles[...], axis=0)
    head_count, head_size = lambdas.shape[1:]
    gate_tanh = jnp.tanh(gate[...])
    grad_gain[...] = total[:2] * (gate_tanh * (1.0 - rate_offset))
    weighed = jnp.sum(total[:2] * norm_gain[...], axis=-1, keepdims=True)
    grad_gate[...] = (
        jnp.sum(weighed, axis=0, keepdims=True)
        * (1.0 - rate_offset)
        * (1.0 - gate_tanh * gate_tanh)
    )
    shape = (head_count, head_size)
    own = lax.broadcasted_iota(jnp.int32, shape, 0) == lax.broadcasted_iota(jnp.int32, shape, 1)
    grad_rate = jnp.sum(jnp.where(own, total[2:3], 0.0), axis=-1, keepdims=True)
    first_exp = jnp.exp(jnp.sum(lambdas[0] * lambdas[1], axis=-1, keepdims=True))
    second_exp = jnp.exp(jnp.sum(lambdas[2] * lambdas[3], axis=-1, keepdims=True))
    weight_one, weight_two = grad_rate * first_exp, grad_rate * second_exp
    grad_lambdas[0] = weight_one * lambdas[1]
    grad_lambdas[1] = weight_one * lambdas[0]
    grad_lambdas[2] = -weight_two * lambdas[3]
    grad_lambdas[3] = -weight_two * lambdas[2]


def unpack_vision_body(received, out):
    half = out.shape[1] // 4
    width = half // PARTS
    for g in range(PARTS):
        out[:, g * width : (g + 1) * width] = received[g, :, :width]
        out[:, half + g * width : half + (g + 1) * width] = received[g, :, width : 2 * width]
        out[:, 2 * half + 2 * g * width : 2 * half + 2 * (g + 1) * width] = received[
            g, :, 2 * width :
        ]


def unpack_text_body(place, *refs):
    parts, out, sems = refs[:PARTS], refs[PARTS], refs[PARTS + 1]
    half = out.shape[2] // 2
    width = half // PARTS
    copies = []
    for shift in range(PARTS):
        g = wrap(place[1] + shift)
        for m in range(2):
            columns = pl.ds(pl.multiple_of(m * half + g * width, width), width)
            copies.append(
                pltpu.make_async_copy(
                    parts[shift].at[:, :, pl.ds(m * width, width)],
                    out.at[:, :, columns],
                    sems.at[shift, m],
                )
            )
    for copy in copies:
        copy.start()
    for copy in copies:
        copy.wait()


def along(shift):
    return [(i, (i + shift) % PARTS) for i in range(PARTS)]


def kernel(body, out_shape, in_specs, out_specs, **more):
    return pl.pallas_call(
        body,
        out_shape=out_shape,
        in_specs=in_specs,
        out_specs=out_specs,
        compiler_params=LIMIT,
        **more,
    )


def shaped(shape, dtype=bf16):
    return jax.ShapeDtypeStruct(shape, dtype)


def exchange(value, axes):
    return lax.all_to_all(value, axes, 0, 0, tiled=True)


def shards(queries, vision, cotangent, assignment, frame_counts, lambdas, norm_gain, gate_logit):
    seqs, toks, text_columns = queries.shape
    frames_dev, patch, vision_columns = vision.shape[1:]
    head_count, head_size = lambdas.shape[1:]
    heads = head_count // PARTS
    rows = seqs * frames_dev * patch
    place = jnp.stack([lax.axis_index("zl"), lax.axis_index("x")]).astype(jnp.int32)
    slab = shaped((PARTS, rows, vision_columns // PARTS))
    gain_rows = norm_gain.reshape(-1, head_size)
    gate = gate_logit.reshape(1, 1)

    sent_vision = kernel(pack_vision_body, slab, [VMEM], VMEM)(
        vision.reshape(rows, vision_columns)
    )
    row_vision = exchange(sent_vision, "x")
    sent_text = kernel(
        pack_text_body,
        [shaped((seqs, toks, 2 * text_columns // PARTS))] * PARTS,
        [SMEM, ANY, ANY],
        [ANY] * PARTS,
        scratch_shapes=[pltpu.SemaphoreType.DMA((PARTS, 3))],
    )(place, queries, cotangent)
    held_text = [sent_text[0]] + [
        lax.ppermute(sent_text[k], "x", along(k)) for k in range(1, PARTS)
    ]
    held_vision = [row_vision] + [
        lax.ppermute(row_vision, "zl", along(k)) for k in range(1, PARTS)
    ]

    grads = kernel(
        functools.partial(attend_body, heads=heads, head_size=head_size, patch=patch),
        [shaped((seqs, toks, text_columns // PARTS))] * PARTS
        + [slab] * PARTS
        + [shaped((FIRST, 4, head_size), f32)],
        [SMEM] * 3 + [VMEM] * (3 + 2 * PARTS),
        [VMEM] * (2 * PARTS + 1),
    )(
        place,
        assignment,
        frame_counts,
        lambdas,
        norm_gain.reshape(1, -1),
        gate,
        *held_text,
        *held_vision,
    )
    grad_text, grad_vision, stats = grads[:PARTS], grads[PARTS : 2 * PARTS], grads[2 * PARTS]

    stats = exchange(stats, ("y", "x"))
    back_vision = [grad_vision[0]] + [
        lax.ppermute(grad_vision[k], "zl", along(-k)) for k in range(1, PARTS)
    ]
    stats = kernel(spread_sum_body, shaped((SECOND, 4, head_size), f32), [VMEM], VMEM)(stats)
    stats = exchange(stats, ("zh", "core", "zl"))
    back_text = [grad_text[0]] + [
        lax.ppermute(grad_text[k], "x", along(-k)) for k in range(1, PARTS)
    ]
    row_vision = kernel(sum_vision_body, slab, [VMEM] * PARTS, VMEM)(*back_vision)
    row_vision = exchange(row_vision, "x")

    grad_queries = kernel(
        unpack_text_body,
        shaped(queries.shape),
        [SMEM] + [ANY] * PARTS,
        ANY,
        scratch_shapes=[pltpu.SemaphoreType.DMA((PARTS, 2))],
    )(place, *back_text)
    grad_lambdas, grad_gain, grad_gate = kernel(
        finish_body,
        [shaped(lambdas.shape, f32), shaped(gain_rows.shape, f32), shaped((1, 1), f32)],
        [VMEM] * 4,
        [VMEM] * 3,
    )(stats, lambdas, gain_rows, gate)
    grad_vision = kernel(unpack_vision_body, shaped((rows, vision_columns)), [VMEM], VMEM)(
        row_vision
    )
    return (
        grad_queries,
        grad_vision.reshape(vision.shape),
        grad_lambdas,
        grad_gain.reshape(norm_gain.shape),
        grad_gate.reshape(gate_logit.shape),
    )


def solution(mesh):
    fine = Mesh(mesh.devices.reshape(8, 2, 2, PARTS, PARTS), DP + IMAGE)
    placed = (
        P(DP, IMAGE, None),
        P(DP, IMAGE, None, None),
        P(DP, IMAGE, None),
        P(DP, None),
        P(DP),
        P(),
        P(),
        P(),
    )
    return jax.shard_map(
        shards,
        mesh=fine,
        in_specs=placed,
        out_specs=(P(DP, IMAGE, None), P(DP, IMAGE, None, None), P(), P(), P()),
        check_vma=False,
    )
```

```python
import functools

import jax
import jax.numpy as jnp
from jax import lax
from jax.experimental import pallas as pl
from jax.experimental.pallas import tpu as pltpu
from jax.sharding import Mesh, PartitionSpec as P

rate_offset = 0.8
epsilon = 1e-05
DP = ("y", "zh", "core")
IMAGE = ("zl", "x")
FIRST, SECOND = 32, 16
PARTS = 4
ORDER, LATE = (0, 2, 1, 3), (0, 3, 1, 2)
VMEM = pl.BlockSpec(memory_space=pltpu.VMEM)
SMEM = pl.BlockSpec(memory_space=pltpu.SMEM)
ANY = pl.BlockSpec(memory_space=pl.ANY)
LIMIT = pltpu.CompilerParams(vmem_limit_bytes=32 * 2**20)
f32, bf16 = jnp.float32, jnp.bfloat16


def dot(a, b, contract):
    return lax.dot_general(
        a, b, ((contract[:1], contract[1:]), ((), ())), preferred_element_type=f32
    )


def wrap(index):
    return lax.rem(index + PARTS, PARTS)


def pack_vision_body(vision, out):
    half = vision.shape[1] // 4
    width = half // PARTS
    for g in range(PARTS):
        out[g, :, :width] = vision[:, g * width : (g + 1) * width]
        out[g, :, width : 2 * width] = vision[:, half + g * width : half + (g + 1) * width]
        out[g, :, 2 * width :] = vision[
            :, 2 * half + 2 * g * width : 2 * half + 2 * (g + 1) * width
        ]


def pack_text_body(place, queries, cotangent, *refs):
    outs, sems = refs[:-1], refs[-1]
    half = queries.shape[2] // 2
    width = half // PARTS
    copies = []
    for n, shift in enumerate(ORDER):
        g = wrap(place[1] + shift)
        first = pl.multiple_of(g * width, width)
        second = pl.multiple_of(half + g * width, width)
        wide = pl.multiple_of(g * 2 * width, 2 * width)
        pieces = (
            (queries.at[:, :, pl.ds(first, width)], pl.ds(0, width)),
            (queries.at[:, :, pl.ds(second, width)], pl.ds(width, width)),
            (cotangent.at[:, :, pl.ds(wide, 2 * width)], pl.ds(2 * width, 2 * width)),
        )
        for i, (source, columns) in enumerate(pieces):
            copies.append(
                pltpu.make_async_copy(source, outs[n].at[:, :, columns], sems.at[n, i])
            )
    for copy in copies:
        copy.start()
    for copy in copies:
        copy.wait()


def attend_body(
    place, assignment, counts, lambdas, norm_gain, gate, *refs, heads, head_size, patch
):
    text, vision, payload, grad_vision = (refs[i * PARTS : (i + 1) * PARTS] for i in range(4))
    vision = [vision[LATE.index(k)] for k in range(PARTS)]
    stats = refs[4 * PARTS]
    zl, x = place[0], place[1]
    seqs, toks = text[0].shape[0], text[0].shape[1]
    frames = PARTS * PARTS
    keys = frames * patch
    width = heads * head_size
    scale = head_size ** (-0.5)
    output_scale = jnp.tanh(gate[...]) * (1.0 - rate_offset)
    gain_row = norm_gain[...] * output_scale
    first_exp = jnp.exp(jnp.sum(lambdas[0] * lambdas[1], axis=-1, keepdims=True))
    second_exp = jnp.exp(jnp.sum(lambdas[2] * lambdas[3], axis=-1, keepdims=True))
    all_rates = first_exp - second_exp + rate_offset
    head_index = lax.broadcasted_iota(jnp.int32, all_rates.shape, 0)
    spot = lax.broadcasted_iota(jnp.int32, (1, keys), 1) // patch
    part = spot // PARTS
    frame = wrap(zl - part) * PARTS + spot - part * PARTS
    raw_gain = jnp.zeros((1, 2 * head_size), f32)
    lane = lax.broadcasted_iota(jnp.int32, (1, head_size), 1)
    rate_row = jnp.zeros((1, head_size), f32)

    def block(columns):
        wide = jnp.concatenate([part[:, :, columns] for part in vision], axis=0)
        return wide.astype(f32).reshape(frames, seqs, patch, -1)

    def of_video(wide, v):
        return wide[:, v].reshape(keys, -1).astype(bf16)

    for h in range(heads):
        rate = jnp.sum(
            jnp.where(head_index == x * heads + h, all_rates, 0.0), axis=0, keepdims=True
        )
        map_columns = [pl.ds(m * width + h * head_size, head_size) for m in range(2)]
        value_columns = pl.ds(2 * width + 2 * h * head_size, 2 * head_size)
        wide_keys = [block(c) for c in map_columns]
        wide_values = block(value_columns)
        grad_keys, grad_values = ([[], []], [])
        total_rate = jnp.zeros((1, 1), f32)
        for v in range(seqs):
            s = jnp.where(assignment[0, 0] == v, 0, 1)
            usable = frame < counts[v]
            value_rows = of_video(wide_values, v)
            key_rows, query_rows, probs = [], [], []
            for m in range(2):
                k = of_video(wide_keys[m], v)
                q = jnp.concatenate([t[s, :, map_columns[m]] for t in text], axis=0)
                scores = dot(q, k, (1, 1)) * scale
                scores = jnp.where(usable, scores, -jnp.inf)
                shifted = jnp.exp(scores - jnp.max(scores, axis=-1, keepdims=True))
                probs.append(shifted / jnp.sum(shifted, axis=-1, keepdims=True))
                key_rows.append(k)
                query_rows.append(q)
            mixed = (probs[0] - rate * probs[1]).astype(bf16)
            attended = dot(mixed, value_rows, (1, 0))
            inverse_rms = lax.rsqrt(
                jnp.mean(attended * attended, axis=-1, keepdims=True) + epsilon
            )
            normed = attended * inverse_rms
            grad_out = jnp.concatenate([t[s, :, value_columns] for t in text], axis=0).astype(f32)
            raw_gain = raw_gain + jnp.sum(grad_out * normed, axis=0, keepdims=True)
            scaled = grad_out * gain_row
            grad_attended = (
                inverse_rms
                * (scaled - normed * jnp.mean(scaled * normed, axis=-1, keepdims=True))
            ).astype(bf16)
            grad_mixed = dot(grad_attended, value_rows, (1, 1))
            grad_values.append(dot(mixed, grad_attended, (0, 0)).reshape(frames, patch, -1))
            sums = [jnp.sum(grad_mixed * p, axis=-1, keepdims=True) for p in probs]
            total_rate = total_rate - jnp.sum(sums[1], axis=0, keepdims=True)
            factors = (scale, -rate * scale)
            for m in range(2):
                grad_scores = (probs[m] * (grad_mixed - sums[m]) * factors[m]).astype(bf16)
                grad_query = dot(grad_scores, key_rows[m], (1, 0)).astype(bf16)
                own_rows = pl.ds(pl.multiple_of(s * toks, toks), toks)
                for i in range(PARTS):
                    payload[i][own_rows, map_columns[m]] = grad_query[i * toks : (i + 1) * toks]
                grad_key = dot(grad_scores, query_rows[m], (0, 0))
                grad_keys[m].append(grad_key.reshape(frames, patch, -1))
        for columns, parts in (
            (map_columns[0], grad_keys[0]),
            (map_columns[1], grad_keys[1]),
            (value_columns, grad_values),
        ):
            joined = jnp.concatenate(parts, axis=1).astype(bf16)
            for j in range(PARTS):
                grad_vision[j][:, :, columns] = joined[j * PARTS : (j + 1) * PARTS]
        rate_row = jnp.where(lane == x * heads + h, total_rate, rate_row)
    row = lax.broadcasted_iota(jnp.int32, stats.shape[1:], 0)
    tile = jnp.where(row == 0, raw_gain[:, :head_size], 0.0)
    tile = jnp.where(row == 1, raw_gain[:, head_size:], tile)
    tile = jnp.where(row == 2, rate_row, tile)
    for i in range(stats.shape[0]):
        stats[i] = tile


def sum_vision_body(place, after, *refs):
    del after
    parts, outs, total, sems = (
        refs[:PARTS],
        refs[2 * PARTS : 3 * PARTS],
        refs[3 * PARTS],
        refs[3 * PARTS + 1],
    )
    rows, columns = total.shape[1] // 2, total.shape[2]
    copies = []
    for k in range(PARTS):
        x = wrap(place[1] - ORDER[k])
        value = parts[0][x].astype(f32)
        for part in parts[1:]:
            value = value + part[x].astype(f32)
        value = value.astype(bf16)
        total[k, :rows] = value[:, :columns]
        total[k, rows:] = value[:, columns:]
        base = outs[k].shape[0] - 2 * rows
        copies.append(
            pltpu.make_async_copy(total.at[k], outs[k].at[pl.ds(base, 2 * rows)], sems.at[k])
        )
        copies[k].start()
    for copy in copies:
        copy.wait()


def spread_sum_body(tiles, after, out):
    del after
    total = jnp.sum(tiles[...], axis=0)
    for i in range(out.shape[0]):
        out[i] = total


def finish_body(tiles, lambdas, norm_gain, gate, grad_lambdas, grad_gain, grad_gate):
    total = jnp.sum(tiles[...], axis=0)
    head_count, head_size = lambdas.shape[1:]
    gate_tanh = jnp.tanh(gate[...])
    grad_gain[...] = total[:2] * (gate_tanh * (1.0 - rate_offset))
    weighed = jnp.sum(total[:2] * norm_gain[...], axis=-1, keepdims=True)
    grad_gate[...] = (
        jnp.sum(weighed, axis=0, keepdims=True)
        * (1.0 - rate_offset)
        * (1.0 - gate_tanh * gate_tanh)
    )
    shape = (head_count, head_size)
    own = lax.broadcasted_iota(jnp.int32, shape, 0) == lax.broadcasted_iota(jnp.int32, shape, 1)
    grad_rate = jnp.sum(jnp.where(own, total[2:3], 0.0), axis=-1, keepdims=True)
    first_exp = jnp.exp(jnp.sum(lambdas[0] * lambdas[1], axis=-1, keepdims=True))
    second_exp = jnp.exp(jnp.sum(lambdas[2] * lambdas[3], axis=-1, keepdims=True))
    weight_one, weight_two = grad_rate * first_exp, grad_rate * second_exp
    grad_lambdas[0] = weight_one * lambdas[1]
    grad_lambdas[1] = weight_one * lambdas[0]
    grad_lambdas[2] = -weight_two * lambdas[3]
    grad_lambdas[3] = -weight_two * lambdas[2]


def unpack_body(place, *refs):
    parts, grad_queries, grad_vision, sems = refs[:PARTS], refs[PARTS], refs[PARTS + 1], refs[-1]
    text_rows, rows = grad_queries.shape[0], grad_vision.shape[0]
    half = grad_queries.shape[1] // 2
    width = half // PARTS
    copies = []
    for k in range(PARTS):
        g = wrap(place[1] + ORDER[k])
        first = pl.multiple_of(g * width, width)
        second = pl.multiple_of(half + g * width, width)
        wide = pl.multiple_of(2 * half + 2 * g * width, 2 * width)
        text, keys = pl.ds(0, text_rows), pl.ds(text_rows, rows)
        values = pl.ds(text_rows + rows, rows)
        left, right, both = pl.ds(0, width), pl.ds(width, width), pl.ds(0, 2 * width)
        pieces = (
            (text, left, grad_queries, pl.ds(first, width)),
            (text, right, grad_queries, pl.ds(second, width)),
            (keys, left, grad_vision, pl.ds(first, width)),
            (keys, right, grad_vision, pl.ds(second, width)),
            (values, both, grad_vision, pl.ds(wide, 2 * width)),
        )
        for i, (own_rows, columns, out, to) in enumerate(pieces):
            copies.append(
                pltpu.make_async_copy(
                    parts[k].at[own_rows, columns], out.at[:, to], sems.at[k, i]
                )
            )
    for copy in copies:
        copy.start()
    for copy in copies:
        copy.wait()


def shift_all(parts, axis, order, way):
    return [
        lax.ppermute(part, axis, [(i, (i + way * k) % PARTS) for i in range(PARTS)]) if k else part
        for part, k in zip(parts, order)
    ]


def kernel(body, out_shape, in_specs, out_specs, **more):
    return pl.pallas_call(
        body,
        out_shape=out_shape,
        in_specs=in_specs,
        out_specs=out_specs,
        compiler_params=LIMIT,
        **more,
    )


def shaped(shape, dtype=bf16):
    return jax.ShapeDtypeStruct(shape, dtype)


def exchange(value, axes):
    return lax.all_to_all(value, axes, 0, 0, tiled=True)


def shards(queries, vision, cotangent, assignment, frame_counts, lambdas, norm_gain, gate_logit):
    seqs, toks, text_columns = queries.shape
    frames_dev, patch, vision_columns = vision.shape[1:]
    head_count, head_size = lambdas.shape[1:]
    heads = head_count // PARTS
    rows = seqs * frames_dev * patch
    place = jnp.stack([lax.axis_index("zl"), lax.axis_index("x")]).astype(jnp.int32)
    slab = shaped((PARTS, rows, vision_columns // PARTS))
    gain_rows = norm_gain.reshape(-1, head_size)
    gate = gate_logit.reshape(1, 1)

    sent_vision = kernel(pack_vision_body, slab, [VMEM], VMEM)(
        vision.reshape(rows, vision_columns)
    )
    row_vision = exchange(sent_vision, "x")
    sent_text = kernel(
        pack_text_body,
        [shaped((seqs, toks, 2 * text_columns // PARTS))] * PARTS,
        [SMEM, ANY, ANY],
        [ANY] * PARTS,
        scratch_shapes=[pltpu.SemaphoreType.DMA((PARTS, 3))],
    )(place, queries, cotangent)
    held_text = shift_all(sent_text, "x", ORDER, 1)
    held_vision = shift_all([row_vision] * PARTS, "zl", LATE, 1)

    grads = kernel(
        functools.partial(attend_body, heads=heads, head_size=head_size, patch=patch),
        [shaped((seqs * toks + 2 * rows, text_columns // PARTS))] * PARTS
        + [slab] * PARTS
        + [shaped((FIRST, 4, head_size), f32)],
        [SMEM] * 3 + [VMEM] * (3 + 2 * PARTS),
        [VMEM] * (2 * PARTS + 1),
    )(
        place,
        assignment,
        frame_counts,
        lambdas,
        norm_gain.reshape(1, -1),
        gate,
        *held_text,
        *held_vision,
    )
    payload, grad_vision, stats = grads[:PARTS], grads[PARTS : 2 * PARTS], grads[2 * PARTS]

    back_vision = shift_all([grad_vision[k] for k in ORDER], "zl", ORDER, -1)
    stats = exchange(stats, ("y", "x"))
    payload = kernel(
        sum_vision_body,
        [shaped(payload[0].shape)] * PARTS,
        [SMEM, ANY] + [VMEM] * PARTS + [ANY] * PARTS,
        [ANY] * PARTS,
        scratch_shapes=[
            pltpu.VMEM((PARTS, 2 * rows, text_columns // PARTS), bf16),
            pltpu.SemaphoreType.DMA((PARTS,)),
        ],
        input_output_aliases={2 + PARTS + k: k for k in range(PARTS)},
    )(place, stats, *back_vision, *payload)
    back = shift_all(payload, "x", ORDER, -1)
    stats = kernel(spread_sum_body, shaped((SECOND, 4, head_size), f32), [VMEM, ANY], VMEM)(
        stats, payload[0]
    )
    stats = exchange(stats, ("zh", "core", "zl"))
    grad_queries, grad_vision = kernel(
        unpack_body,
        [shaped((seqs * toks, text_columns)), shaped((rows, vision_columns))],
        [SMEM] + [ANY] * PARTS,
        [ANY] * 2,
        scratch_shapes=[pltpu.SemaphoreType.DMA((PARTS, 5))],
    )(place, *back)

    grad_lambdas, grad_gain, grad_gate = kernel(
        finish_body,
        [shaped(lambdas.shape, f32), shaped(gain_rows.shape, f32), shaped((1, 1), f32)],
        [VMEM] * 4,
        [VMEM] * 3,
    )(stats, lambdas, gain_rows, gate)
    return (
        grad_queries.reshape(queries.shape),
        grad_vision.reshape(vision.shape),
        grad_lambdas,
        grad_gain.reshape(norm_gain.shape),
        grad_gate.reshape(gate_logit.shape),
    )


def solution(mesh):
    fine = Mesh(mesh.devices.reshape(8, 2, 2, PARTS, PARTS), DP + IMAGE)
    placed = (
        P(DP, IMAGE, None),
        P(DP, IMAGE, None, None),
        P(DP, IMAGE, None),
        P(DP, None),
        P(DP),
        P(),
        P(),
        P(),
    )
    return jax.shard_map(
        shards,
        mesh=fine,
        in_specs=placed,
        out_specs=(P(DP, IMAGE, None), P(DP, IMAGE, None, None), P(), P(), P()),
        check_vma=False,
    )
```

```python
import functools

import jax
import jax.numpy as jnp
from jax import lax
from jax.experimental import pallas as pl
from jax.experimental.pallas import tpu as pltpu
from jax.sharding import Mesh, PartitionSpec as P

rate_offset = 0.8
epsilon = 1e-05
DP = ("y", "zh", "core")
IMAGE = ("zl", "x")
FIRST, SECOND = 32, 16
PARTS = 4
ORDER, LATE = (0, 2, 1, 3), (0, 3, 1, 2)
VMEM = pl.BlockSpec(memory_space=pltpu.VMEM)
SMEM = pl.BlockSpec(memory_space=pltpu.SMEM)
ANY = pl.BlockSpec(memory_space=pl.ANY)
LIMIT = pltpu.CompilerParams(vmem_limit_bytes=32 * 2**20)
f32, bf16 = jnp.float32, jnp.bfloat16


def dot(a, b, contract):
    return lax.dot_general(
        a, b, ((contract[:1], contract[1:]), ((), ())), preferred_element_type=f32
    )


def wrap(index):
    return lax.rem(index + PARTS, PARTS)


def pack_vision_body(vision, out):
    half = vision.shape[1] // 4
    width = half // PARTS
    for g in range(PARTS):
        out[g, :, :width] = vision[:, g * width : (g + 1) * width]
        out[g, :, width : 2 * width] = vision[:, half + g * width : half + (g + 1) * width]
        out[g, :, 2 * width :] = vision[
            :, 2 * half + 2 * g * width : 2 * half + 2 * (g + 1) * width
        ]


def pack_text_body(queries, cotangent, out, sems):
    half = queries.shape[2] // 2
    width = half // PARTS
    copies = []
    for g in range(PARTS):
        pieces = (
            (queries, g * width, 0, width),
            (queries, half + g * width, width, width),
            (cotangent, 2 * g * width, 2 * width, 2 * width),
        )
        for i, (source, first, to, size) in enumerate(pieces):
            copies.append(
                pltpu.make_async_copy(
                    source.at[:, :, pl.ds(first, size)],
                    out.at[g, :, :, pl.ds(to, size)],
                    sems.at[g, i],
                )
            )
    for copy in copies:
        copy.start()
    for copy in copies:
        copy.wait()


def attend_body(
    place, assignment, counts, lambdas, norm_gain, gate, *refs, heads, head_size, patch
):
    text = refs[0]
    vision, payload, grad_vision = (refs[1 + i * PARTS : 1 + (i + 1) * PARTS] for i in range(3))
    vision = [vision[LATE.index(k)] for k in range(PARTS)]
    stats = refs[1 + 3 * PARTS]
    zl, x = place[0], place[1]
    seqs, toks = text.shape[1:3]
    sources = [wrap(x - k) for k in ORDER]
    frames = PARTS * PARTS
    keys = frames * patch
    width = heads * head_size
    scale = head_size ** (-0.5)
    output_scale = jnp.tanh(gate[...]) * (1.0 - rate_offset)
    gain_row = norm_gain[...] * output_scale
    first_exp = jnp.exp(jnp.sum(lambdas[0] * lambdas[1], axis=-1, keepdims=True))
    second_exp = jnp.exp(jnp.sum(lambdas[2] * lambdas[3], axis=-1, keepdims=True))
    all_rates = first_exp - second_exp + rate_offset
    head_index = lax.broadcasted_iota(jnp.int32, all_rates.shape, 0)
    spot = lax.broadcasted_iota(jnp.int32, (1, keys), 1) // patch
    part = spot // PARTS
    frame = wrap(zl - part) * PARTS + spot - part * PARTS
    raw_gain = jnp.zeros((1, 2 * head_size), f32)
    lane = lax.broadcasted_iota(jnp.int32, (1, head_size), 1)
    rate_row = jnp.zeros((1, head_size), f32)

    def block(columns):
        wide = jnp.concatenate([part[:, :, columns] for part in vision], axis=0)
        return wide.astype(f32).reshape(frames, seqs, patch, -1)

    def of_video(wide, v):
        return wide[:, v].reshape(keys, -1).astype(bf16)

    for h in range(heads):
        rate = jnp.sum(
            jnp.where(head_index == x * heads + h, all_rates, 0.0), axis=0, keepdims=True
        )
        map_columns = [pl.ds(m * width + h * head_size, head_size) for m in range(2)]
        value_columns = pl.ds(2 * width + 2 * h * head_size, 2 * head_size)
        wide_keys = [block(c) for c in map_columns]
        wide_values = block(value_columns)
        grad_keys, grad_values = ([[], []], [])
        total_rate = jnp.zeros((1, 1), f32)
        for v in range(seqs):
            s = jnp.where(assignment[0, 0] == v, 0, 1)
            usable = frame < counts[v]
            value_rows = of_video(wide_values, v)
            key_rows, query_rows, probs = [], [], []
            for m in range(2):
                k = of_video(wide_keys[m], v)
                q = jnp.concatenate([text[i, s, :, map_columns[m]] for i in sources], axis=0)
                scores = dot(q, k, (1, 1)) * scale
                scores = jnp.where(usable, scores, -jnp.inf)
                shifted = jnp.exp(scores - jnp.max(scores, axis=-1, keepdims=True))
                probs.append(shifted / jnp.sum(shifted, axis=-1, keepdims=True))
                key_rows.append(k)
                query_rows.append(q)
            mixed = (probs[0] - rate * probs[1]).astype(bf16)
            attended = dot(mixed, value_rows, (1, 0))
            inverse_rms = lax.rsqrt(
                jnp.mean(attended * attended, axis=-1, keepdims=True) + epsilon
            )
            normed = attended * inverse_rms
            grad_out = jnp.concatenate(
                [text[i, s, :, value_columns] for i in sources], axis=0
            ).astype(f32)
            raw_gain = raw_gain + jnp.sum(grad_out * normed, axis=0, keepdims=True)
            scaled = grad_out * gain_row
            grad_attended = (
                inverse_rms
                * (scaled - normed * jnp.mean(scaled * normed, axis=-1, keepdims=True))
            ).astype(bf16)
            grad_mixed = dot(grad_attended, value_rows, (1, 1))
            grad_values.append(dot(mixed, grad_attended, (0, 0)).reshape(frames, patch, -1))
            sums = [jnp.sum(grad_mixed * p, axis=-1, keepdims=True) for p in probs]
            total_rate = total_rate - jnp.sum(sums[1], axis=0, keepdims=True)
            factors = (scale, -rate * scale)
            for m in range(2):
                grad_scores = (probs[m] * (grad_mixed - sums[m]) * factors[m]).astype(bf16)
                grad_query = dot(grad_scores, key_rows[m], (1, 0)).astype(bf16)
                own_rows = pl.ds(pl.multiple_of(s * toks, toks), toks)
                for i in range(PARTS):
                    payload[i][own_rows, map_columns[m]] = grad_query[i * toks : (i + 1) * toks]
                grad_key = dot(grad_scores, query_rows[m], (0, 0))
                grad_keys[m].append(grad_key.reshape(frames, patch, -1))
        for columns, parts in (
            (map_columns[0], grad_keys[0]),
            (map_columns[1], grad_keys[1]),
            (value_columns, grad_values),
        ):
            joined = jnp.concatenate(parts, axis=1).astype(bf16)
            for j in range(PARTS):
                grad_vision[j][:, :, columns] = joined[j * PARTS : (j + 1) * PARTS]
        rate_row = jnp.where(lane == x * heads + h, total_rate, rate_row)
    row = lax.broadcasted_iota(jnp.int32, stats.shape[1:], 0)
    tile = jnp.where(row == 0, raw_gain[:, :head_size], 0.0)
    tile = jnp.where(row == 1, raw_gain[:, head_size:], tile)
    tile = jnp.where(row == 2, rate_row, tile)
    for i in range(stats.shape[0]):
        stats[i] = tile


def sum_vision_body(place, after, *refs):
    del after
    parts, outs, total, sems = (
        refs[:PARTS],
        refs[2 * PARTS : 3 * PARTS],
        refs[3 * PARTS],
        refs[3 * PARTS + 1],
    )
    rows, columns = total.shape[1] // 2, total.shape[2]
    copies = []
    for k in range(PARTS):
        x = wrap(place[1] - ORDER[k])
        value = parts[0][x].astype(f32)
        for part in parts[1:]:
            value = value + part[x].astype(f32)
        value = value.astype(bf16)
        total[k, :rows] = value[:, :columns]
        total[k, rows:] = value[:, columns:]
        base = outs[k].shape[0] - 2 * rows
        copies.append(
            pltpu.make_async_copy(total.at[k], outs[k].at[pl.ds(base, 2 * rows)], sems.at[k])
        )
        copies[k].start()
    for copy in copies:
        copy.wait()


def spread_sum_body(tiles, after, out):
    del after
    total = jnp.sum(tiles[...], axis=0)
    for i in range(out.shape[0]):
        out[i] = total


def finish_body(place, tiles, lambdas, norm_gain, gate, *refs):
    parts, grad_queries, grad_vision, grad_lambdas, grad_gain, grad_gate, sems = (
        refs[:PARTS],
        *refs[PARTS:],
    )
    text_rows, rows = grad_queries.shape[0], grad_vision.shape[0]
    half = grad_queries.shape[1] // 2
    width = half // PARTS
    copies = []
    for k in range(PARTS):
        g = wrap(place[1] + ORDER[k])
        first = pl.multiple_of(g * width, width)
        second = pl.multiple_of(half + g * width, width)
        wide = pl.multiple_of(2 * half + 2 * g * width, 2 * width)
        text, keys = pl.ds(0, text_rows), pl.ds(text_rows, rows)
        values = pl.ds(text_rows + rows, rows)
        left, right, both = pl.ds(0, width), pl.ds(width, width), pl.ds(0, 2 * width)
        pieces = (
            (text, left, grad_queries, pl.ds(first, width)),
            (text, right, grad_queries, pl.ds(second, width)),
            (keys, left, grad_vision, pl.ds(first, width)),
            (keys, right, grad_vision, pl.ds(second, width)),
            (values, both, grad_vision, pl.ds(wide, 2 * width)),
        )
        for i, (own_rows, columns, out, to) in enumerate(pieces):
            copies.append(
                pltpu.make_async_copy(
                    parts[k].at[own_rows, columns], out.at[:, to], sems.at[k, i]
                )
            )
    for copy in copies:
        copy.start()
    total = jnp.sum(tiles[...], axis=0)
    head_count, head_size = lambdas.shape[1:]
    gate_tanh = jnp.tanh(gate[...])
    grad_gain[...] = total[:2] * (gate_tanh * (1.0 - rate_offset))
    weighed = jnp.sum(total[:2] * norm_gain[...], axis=-1, keepdims=True)
    grad_gate[...] = (
        jnp.sum(weighed, axis=0, keepdims=True)
        * (1.0 - rate_offset)
        * (1.0 - gate_tanh * gate_tanh)
    )
    shape = (head_count, head_size)
    own = lax.broadcasted_iota(jnp.int32, shape, 0) == lax.broadcasted_iota(jnp.int32, shape, 1)
    grad_rate = jnp.sum(jnp.where(own, total[2:3], 0.0), axis=-1, keepdims=True)
    first_exp = jnp.exp(jnp.sum(lambdas[0] * lambdas[1], axis=-1, keepdims=True))
    second_exp = jnp.exp(jnp.sum(lambdas[2] * lambdas[3], axis=-1, keepdims=True))
    weight_one, weight_two = grad_rate * first_exp, grad_rate * second_exp
    grad_lambdas[0] = weight_one * lambdas[1]
    grad_lambdas[1] = weight_one * lambdas[0]
    grad_lambdas[2] = -weight_two * lambdas[3]
    grad_lambdas[3] = -weight_two * lambdas[2]
    for copy in copies:
        copy.wait()


def shift_all(parts, axis, order, way):
    return [
        lax.ppermute(part, axis, [(i, (i + way * k) % PARTS) for i in range(PARTS)]) if k else part
        for part, k in zip(parts, order)
    ]


def kernel(body, out_shape, in_specs, out_specs, **more):
    return pl.pallas_call(
        body,
        out_shape=out_shape,
        in_specs=in_specs,
        out_specs=out_specs,
        compiler_params=LIMIT,
        **more,
    )


def shaped(shape, dtype=bf16):
    return jax.ShapeDtypeStruct(shape, dtype)


def exchange(value, axes):
    return lax.all_to_all(value, axes, 0, 0, tiled=True)


def shards(queries, vision, cotangent, assignment, frame_counts, lambdas, norm_gain, gate_logit):
    seqs, toks, text_columns = queries.shape
    frames_dev, patch, vision_columns = vision.shape[1:]
    head_count, head_size = lambdas.shape[1:]
    heads = head_count // PARTS
    rows = seqs * frames_dev * patch
    place = jnp.stack([lax.axis_index("zl"), lax.axis_index("x")]).astype(jnp.int32)
    slab = shaped((PARTS, rows, vision_columns // PARTS))
    gain_rows = norm_gain.reshape(-1, head_size)
    gate = gate_logit.reshape(1, 1)

    sent_vision = kernel(pack_vision_body, slab, [VMEM], VMEM)(
        vision.reshape(rows, vision_columns)
    )
    row_vision = exchange(sent_vision, "x")
    sent_text = kernel(
        pack_text_body,
        shaped((PARTS, seqs, toks, 2 * text_columns // PARTS)),
        [ANY] * 2,
        ANY,
        scratch_shapes=[pltpu.SemaphoreType.DMA((PARTS, 3))],
    )(queries, cotangent)
    held_text = exchange(sent_text, "x")
    held_vision = shift_all([row_vision] * PARTS, "zl", LATE, 1)

    grads = kernel(
        functools.partial(attend_body, heads=heads, head_size=head_size, patch=patch),
        [shaped((seqs * toks + 2 * rows, text_columns // PARTS))] * PARTS
        + [slab] * PARTS
        + [shaped((FIRST, 4, head_size), f32)],
        [SMEM] * 3 + [VMEM] * (4 + PARTS),
        [VMEM] * (2 * PARTS + 1),
    )(
        place,
        assignment,
        frame_counts,
        lambdas,
        norm_gain.reshape(1, -1),
        gate,
        held_text,
        *held_vision,
    )
    payload, grad_vision, stats = grads[:PARTS], grads[PARTS : 2 * PARTS], grads[2 * PARTS]

    back_vision = shift_all(grad_vision, "zl", range(PARTS), -1)
    stats = exchange(stats, ("y", "x"))
    payload = kernel(
        sum_vision_body,
        [shaped(payload[0].shape)] * PARTS,
        [SMEM, ANY] + [VMEM] * PARTS + [ANY] * PARTS,
        [ANY] * PARTS,
        scratch_shapes=[
            pltpu.VMEM((PARTS, 2 * rows, text_columns // PARTS), bf16),
            pltpu.SemaphoreType.DMA((PARTS,)),
        ],
        input_output_aliases={2 + PARTS + k: k for k in range(PARTS)},
    )(place, stats, *back_vision, *payload)
    back = shift_all(payload, "x", ORDER, -1)
    stats = kernel(spread_sum_body, shaped((SECOND, 4, head_size), f32), [VMEM, ANY], VMEM)(
        stats, payload[0]
    )
    stats = exchange(stats, ("zh", "core", "zl"))
    grad_queries, grad_vision, grad_lambdas, grad_gain, grad_gate = kernel(
        finish_body,
        [
            shaped((seqs * toks, text_columns)),
            shaped((rows, vision_columns)),
            shaped(lambdas.shape, f32),
            shaped(gain_rows.shape, f32),
            shaped((1, 1), f32),
        ],
        [SMEM] + [VMEM] * 4 + [ANY] * PARTS,
        [ANY] * 2 + [VMEM] * 3,
        scratch_shapes=[pltpu.SemaphoreType.DMA((PARTS, 5))],
    )(place, stats, lambdas, gain_rows, gate, *back)
    return (
        grad_queries.reshape(queries.shape),
        grad_vision.reshape(vision.shape),
        grad_lambdas,
        grad_gain.reshape(norm_gain.shape),
        grad_gate.reshape(gate_logit.shape),
    )


def solution(mesh):
    fine = Mesh(mesh.devices.reshape(8, 2, 2, PARTS, PARTS), DP + IMAGE)
    placed = (
        P(DP, IMAGE, None),
        P(DP, IMAGE, None, None),
        P(DP, IMAGE, None),
        P(DP, None),
        P(DP),
        P(),
        P(),
        P(),
    )
    return jax.shard_map(
        shards,
        mesh=fine,
        in_specs=placed,
        out_specs=(P(DP, IMAGE, None), P(DP, IMAGE, None, None), P(), P(), P()),
        check_vma=False,
    )
```

```python
import functools

import jax
import jax.numpy as jnp
from jax import lax
from jax.experimental import pallas as pl
from jax.experimental.pallas import tpu as pltpu
from jax.sharding import Mesh, PartitionSpec as P

rate_offset = 0.8
epsilon = 1e-05
DP = ("y", "zh", "core")
IMAGE = ("zl", "x")
FIRST, SECOND = 16, 32
PARTS = 4
GROUP = 2
ORDER, LATE = (0, 2, 1, 3), (0, 3, 1, 2)
VMEM = pl.BlockSpec(memory_space=pltpu.VMEM)
SMEM = pl.BlockSpec(memory_space=pltpu.SMEM)
ANY = pl.BlockSpec(memory_space=pl.ANY)
LIMIT = pltpu.CompilerParams(vmem_limit_bytes=32 * 2**20)
f32, bf16 = jnp.float32, jnp.bfloat16


def dot(a, b, contract):
    return lax.dot_general(
        a, b, ((contract[:1], contract[1:]), ((), ())), preferred_element_type=f32
    )


def wrap(index):
    return lax.rem(index + PARTS, PARTS)


def pack_vision_body(vision, out):
    half = vision.shape[1] // 4
    width = half // PARTS
    for g in range(PARTS):
        out[g, :, :width] = vision[:, g * width : (g + 1) * width]
        out[g, :, width : 2 * width] = vision[:, half + g * width : half + (g + 1) * width]
        out[g, :, 2 * width :] = vision[
            :, 2 * half + 2 * g * width : 2 * half + 2 * (g + 1) * width
        ]


def pack_text_body(queries, cotangent, out, sems):
    half = queries.shape[2] // 2
    width = half // PARTS
    copies = []
    for g in range(PARTS):
        pieces = (
            (queries, g * width, 0, width),
            (queries, half + g * width, width, width),
            (cotangent, 2 * g * width, 2 * width, 2 * width),
        )
        for i, (source, first, to, size) in enumerate(pieces):
            copies.append(
                pltpu.make_async_copy(
                    source.at[:, :, pl.ds(first, size)],
                    out.at[g, :, :, pl.ds(to, size)],
                    sems.at[g, i],
                )
            )
    for copy in copies:
        copy.start()
    for copy in copies:
        copy.wait()


def attend_body(
    place, assignment, counts, lambdas, norm_gain, gate, *refs, heads, head_size, patch
):
    text = refs[0]
    vision, payload, grad_vision = (refs[1 + i * PARTS : 1 + (i + 1) * PARTS] for i in range(3))
    vision = [vision[LATE.index(k)] for k in range(PARTS)]
    stats, gain, bias, raw_gain = refs[1 + 3 * PARTS :]
    zl, x = place[0], place[1]
    seqs, toks = text.shape[1:3]
    sources = [wrap(x - k) for k in ORDER]
    rows = PARTS * toks
    frames = PARTS * PARTS
    keys = frames * patch
    width = heads * head_size
    wide = 2 * head_size
    scale = head_size ** (-0.5)
    first_exp = jnp.exp(jnp.sum(lambdas[0] * lambdas[1], axis=-1, keepdims=True))
    second_exp = jnp.exp(jnp.sum(lambdas[2] * lambdas[3], axis=-1, keepdims=True))
    all_rates = first_exp - second_exp + rate_offset
    head_index = lax.broadcasted_iota(jnp.int32, all_rates.shape, 0)
    shape = (wide, wide)
    diagonal = lax.broadcasted_iota(jnp.int32, shape, 0) == lax.broadcasted_iota(
        jnp.int32, shape, 1
    )
    eye = jnp.where(diagonal, 1.0, 0.0).astype(bf16)
    gain_row = norm_gain[...] * (jnp.tanh(gate[...]) * (1.0 - rate_offset))
    gain[...] = jnp.broadcast_to(
        jnp.sum(jnp.where(diagonal, gain_row, 0.0), axis=1, keepdims=True), gain.shape
    )
    spot = lax.broadcasted_iota(jnp.int32, (keys, rows), 0) // patch
    part = spot // PARTS
    frame = wrap(zl - part) * PARTS + spot - part * PARTS
    for v in range(seqs):
        bias[v] = jnp.where(frame < counts[v], 0.0, -jnp.inf)
    lane = lax.broadcasted_iota(jnp.int32, (1, head_size), 1)
    rate_row = jnp.zeros((1, head_size), f32)

    def map_columns(h, m):
        return pl.ds(m * width + h * head_size, head_size)

    def value_columns(h):
        return pl.ds(2 * width + h * wide, wide)

    def block(columns):
        joined = jnp.concatenate([part[:, :, columns] for part in vision], axis=0)
        return joined.astype(f32).reshape(frames, seqs, patch, -1)

    def of_video(joined, v):
        return joined[:, v].reshape(keys, -1).astype(bf16)

    place_of = [jnp.where(assignment[0, 0] == v, 0, 1) for v in range(seqs)]
    for first in range(0, heads, GROUP):
        chains = [(h, v) for h in range(first, first + GROUP) for v in range(seqs)]
        both = [(h, v, m) for h, v in chains for m in range(2)]
        rates, joined = {}, {}
        for h in range(first, first + GROUP):
            rates[h] = jnp.sum(
                jnp.where(head_index == x * heads + h, all_rates, 0.0), axis=0, keepdims=True
            )
            joined[h] = block(value_columns(h))
            for m in range(2):
                joined[h, m] = block(map_columns(h, m))
        values = {(h, v): of_video(joined[h], v) for h, v in chains}
        key_rows = {(h, v, m): of_video(joined[h, m], v) for h, v, m in both}
        queries = {
            (h, v, m): jnp.concatenate(
                [text[i, place_of[v], :, map_columns(h, m)] for i in sources], axis=0
            )
            for h, v, m in both
        }
        scores = {c: dot(key_rows[c], queries[c], (1, 1)) + bias[c[1]] for c in both}
        shifted = {
            c: jnp.exp((scores[c] - jnp.max(scores[c], axis=0, keepdims=True)) * scale)
            for c in both
        }
        probs = {
            c: shifted[c] * (1.0 / jnp.sum(shifted[c], axis=0, keepdims=True)) for c in both
        }
        rated = {c: rates[c[0]] * probs[(*c, 1)] for c in chains}
        mixed = {c: (probs[(*c, 0)] - rated[c]).astype(bf16) for c in chains}
        attended = {c: dot(values[c], mixed[c], (0, 0)) for c in chains}
        grad_out = {
            (h, v): dot(
                eye,
                jnp.concatenate(
                    [text[i, place_of[v], :, value_columns(h)] for i in sources], axis=0
                ),
                (1, 1),
            )
            for h, v in chains
        }
        inverse_rms = {
            c: lax.rsqrt(jnp.mean(attended[c] * attended[c], axis=0, keepdims=True) + epsilon)
            for c in chains
        }
        grad_attended = {}
        for c in chains:
            normed = attended[c] * inverse_rms[c]
            product = grad_out[c] * normed
            halves = product[:, :head_size] + product[:, head_size:]
            raw_gain[...] = halves if c == (0, 0) else raw_gain[...] + halves
            middle = jnp.mean(product * gain[...], axis=0, keepdims=True)
            grad_attended[c] = (
                inverse_rms[c] * (grad_out[c] * gain[...] - normed * middle)
            ).astype(bf16)
        grad_mixed = {c: dot(values[c], grad_attended[c], (1, 0)) * scale for c in chains}
        grad_values = {c: dot(mixed[c], grad_attended[c], (1, 1)) for c in chains}
        sums = {
            c: jnp.sum(grad_mixed[c[:2]] * probs[c], axis=0, keepdims=True) for c in both
        }
        grad_scores = {}
        for c in chains:
            grad_scores[(*c, 0)] = (probs[(*c, 0)] * (grad_mixed[c] - sums[(*c, 0)])).astype(bf16)
            grad_scores[(*c, 1)] = (rated[c] * (sums[(*c, 1)] - grad_mixed[c])).astype(bf16)
        grad_keys = {c: dot(grad_scores[c], queries[c], (1, 0)) for c in both}
        for h, v, m in both:
            grad_query = dot(grad_scores[h, v, m], key_rows[h, v, m], (0, 0)).astype(bf16)
            own_rows = pl.ds(pl.multiple_of(place_of[v] * toks, toks), toks)
            for i in range(PARTS):
                payload[i][own_rows, map_columns(h, m)] = grad_query[i * toks : (i + 1) * toks]
        for h in range(first, first + GROUP):
            for columns, parts in (
                (map_columns(h, 0), [grad_keys[h, v, 0] for v in range(seqs)]),
                (map_columns(h, 1), [grad_keys[h, v, 1] for v in range(seqs)]),
                (value_columns(h), [grad_values[h, v] for v in range(seqs)]),
            ):
                parts = [p.reshape(frames, patch, -1) for p in parts]
                total = jnp.concatenate(parts, axis=1).astype(bf16)
                for j in range(PARTS):
                    grad_vision[j][:, :, columns] = total[j * PARTS : (j + 1) * PARTS]
            total_rate = sum(sums[h, v, 1] for v in range(seqs))
            own_rate = jnp.sum(total_rate, axis=1, keepdims=True) * (-1.0 / scale)
            rate_row = jnp.where(lane == x * heads + h, own_rate, rate_row)
    gains = jnp.sum(raw_gain[...].T, axis=0, keepdims=True)
    row = lax.broadcasted_iota(jnp.int32, stats.shape[1:], 0)
    tile = jnp.where(row == 0, gains[:, :head_size], 0.0)
    tile = jnp.where(row == 1, gains[:, head_size:], tile)
    tile = jnp.where(row == 2, rate_row, tile)
    for i in range(stats.shape[0]):
        stats[i] = tile


def sum_vision_body(place, after, *refs):
    del after
    parts, outs, total, sems = (
        refs[:PARTS],
        refs[2 * PARTS : 3 * PARTS],
        refs[3 * PARTS],
        refs[3 * PARTS + 1],
    )
    rows, columns = total.shape[1] // 2, total.shape[2]
    copies = []
    for k in range(PARTS):
        x = wrap(place[1] - ORDER[k])
        value = parts[0][x].astype(f32)
        for part in parts[1:]:
            value = value + part[x].astype(f32)
        value = value.astype(bf16)
        total[k, :rows] = value[:, :columns]
        total[k, rows:] = value[:, columns:]
        base = outs[k].shape[0] - 2 * rows
        copies.append(
            pltpu.make_async_copy(total.at[k], outs[k].at[pl.ds(base, 2 * rows)], sems.at[k])
        )
        copies[k].start()
    for copy in copies:
        copy.wait()


def spread_sum_body(tiles, after, out):
    del after
    total = jnp.sum(tiles[...], axis=0)
    for i in range(out.shape[0]):
        out[i] = total


def finish_body(place, tiles, lambdas, norm_gain, gate, *refs):
    parts, grad_queries, grad_vision, grad_lambdas, grad_gain, grad_gate, sems = (
        refs[:PARTS],
        *refs[PARTS:],
    )
    text_rows, rows = grad_queries.shape[0], grad_vision.shape[0]
    half = grad_queries.shape[1] // 2
    width = half // PARTS
    copies = []
    for k in range(PARTS):
        g = wrap(place[1] + ORDER[k])
        first = pl.multiple_of(g * width, width)
        second = pl.multiple_of(half + g * width, width)
        wide = pl.multiple_of(2 * half + 2 * g * width, 2 * width)
        text, keys = pl.ds(0, text_rows), pl.ds(text_rows, rows)
        values = pl.ds(text_rows + rows, rows)
        left, right, both = pl.ds(0, width), pl.ds(width, width), pl.ds(0, 2 * width)
        pieces = (
            (text, left, grad_queries, pl.ds(first, width)),
            (text, right, grad_queries, pl.ds(second, width)),
            (keys, left, grad_vision, pl.ds(first, width)),
            (keys, right, grad_vision, pl.ds(second, width)),
            (values, both, grad_vision, pl.ds(wide, 2 * width)),
        )
        for i, (own_rows, columns, out, to) in enumerate(pieces):
            copies.append(
                pltpu.make_async_copy(
                    parts[k].at[own_rows, columns], out.at[:, to], sems.at[k, i]
                )
            )
    for copy in copies:
        copy.start()
    total = jnp.sum(tiles[...], axis=0)
    head_count, head_size = lambdas.shape[1:]
    gate_tanh = jnp.tanh(gate[...])
    grad_gain[...] = total[:2] * (gate_tanh * (1.0 - rate_offset))
    weighed = jnp.sum(total[:2] * norm_gain[...], axis=-1, keepdims=True)
    grad_gate[...] = (
        jnp.sum(weighed, axis=0, keepdims=True)
        * (1.0 - rate_offset)
        * (1.0 - gate_tanh * gate_tanh)
    )
    shape = (head_count, head_size)
    own = lax.broadcasted_iota(jnp.int32, shape, 0) == lax.broadcasted_iota(jnp.int32, shape, 1)
    grad_rate = jnp.sum(jnp.where(own, total[2:3], 0.0), axis=-1, keepdims=True)
    first_exp = jnp.exp(jnp.sum(lambdas[0] * lambdas[1], axis=-1, keepdims=True))
    second_exp = jnp.exp(jnp.sum(lambdas[2] * lambdas[3], axis=-1, keepdims=True))
    weight_one, weight_two = grad_rate * first_exp, grad_rate * second_exp
    grad_lambdas[0] = weight_one * lambdas[1]
    grad_lambdas[1] = weight_one * lambdas[0]
    grad_lambdas[2] = -weight_two * lambdas[3]
    grad_lambdas[3] = -weight_two * lambdas[2]
    for copy in copies:
        copy.wait()


def shift_all(parts, axis, order, way):
    return [
        lax.ppermute(part, axis, [(i, (i + way * k) % PARTS) for i in range(PARTS)]) if k else part
        for part, k in zip(parts, order)
    ]


def kernel(body, out_shape, in_specs, out_specs, **more):
    return pl.pallas_call(
        body,
        out_shape=out_shape,
        in_specs=in_specs,
        out_specs=out_specs,
        compiler_params=LIMIT,
        **more,
    )


def shaped(shape, dtype=bf16):
    return jax.ShapeDtypeStruct(shape, dtype)


def exchange(value, axes):
    return lax.all_to_all(value, axes, 0, 0, tiled=True)


def attend_call(place, assignment, counts, lambdas, norm_gain, gate, text, *vision):
    seqs, toks, columns = text.shape[1:]
    head_count, head_size = lambdas.shape[1:]
    heads = head_count // PARTS
    slab = vision[0].shape
    rows = slab[1]
    return kernel(
        functools.partial(
            attend_body, heads=heads, head_size=head_size, patch=rows // seqs
        ),
        [shaped((seqs * toks + 2 * rows, columns // 2))] * PARTS
        + [shaped(slab)] * PARTS
        + [shaped((FIRST, 4, head_size), f32)],
        [SMEM] * 3 + [VMEM] * (4 + PARTS),
        [VMEM] * (2 * PARTS + 1),
        scratch_shapes=[
            pltpu.VMEM((2 * head_size, PARTS * toks), f32),
            pltpu.VMEM((seqs, PARTS * PARTS * rows // seqs, PARTS * toks), f32),
            pltpu.VMEM((2 * head_size, head_size), f32),
        ],
    )(place, assignment, counts, lambdas, norm_gain, gate, text, *vision)


def shards(queries, vision, cotangent, assignment, frame_counts, lambdas, norm_gain, gate_logit):
    seqs, toks, text_columns = queries.shape
    frames_dev, patch, vision_columns = vision.shape[1:]
    head_count, head_size = lambdas.shape[1:]
    heads = head_count // PARTS
    rows = seqs * frames_dev * patch
    place = jnp.stack([lax.axis_index("zl"), lax.axis_index("x")]).astype(jnp.int32)
    slab = shaped((PARTS, rows, vision_columns // PARTS))
    gain_rows = norm_gain.reshape(-1, head_size)
    gate = gate_logit.reshape(1, 1)

    sent_vision = kernel(pack_vision_body, slab, [VMEM], VMEM)(
        vision.reshape(rows, vision_columns)
    )
    row_vision = exchange(sent_vision, "x")
    sent_text = kernel(
        pack_text_body,
        shaped((PARTS, seqs, toks, 2 * text_columns // PARTS)),
        [ANY] * 2,
        ANY,
        scratch_shapes=[pltpu.SemaphoreType.DMA((PARTS, 3))],
    )(queries, cotangent)
    held_text = exchange(sent_text, "x")
    held_vision = shift_all([row_vision] * PARTS, "zl", LATE, 1)

    grads = attend_call(
        place,
        assignment,
        frame_counts,
        lambdas,
        norm_gain.reshape(1, -1),
        gate,
        held_text,
        *held_vision,
    )
    payload, grad_vision, stats = grads[:PARTS], grads[PARTS : 2 * PARTS], grads[2 * PARTS]

    back_vision = shift_all(grad_vision, "zl", range(PARTS), -1)
    stats = exchange(stats, ("y", "core"))
    payload = kernel(
        sum_vision_body,
        [shaped(payload[0].shape)] * PARTS,
        [SMEM, ANY] + [VMEM] * PARTS + [ANY] * PARTS,
        [ANY] * PARTS,
        scratch_shapes=[
            pltpu.VMEM((PARTS, 2 * rows, text_columns // PARTS), bf16),
            pltpu.SemaphoreType.DMA((PARTS,)),
        ],
        input_output_aliases={2 + PARTS + k: k for k in range(PARTS)},
    )(place, stats, *back_vision, *payload)
    back = shift_all(payload, "x", ORDER, -1)
    stats = kernel(spread_sum_body, shaped((SECOND, 4, head_size), f32), [VMEM, ANY], VMEM)(
        stats, payload[0]
    )
    stats = exchange(stats, ("zh", "zl", "x"))
    grad_queries, grad_vision, grad_lambdas, grad_gain, grad_gate = kernel(
        finish_body,
        [
            shaped((seqs * toks, text_columns)),
            shaped((rows, vision_columns)),
            shaped(lambdas.shape, f32),
            shaped(gain_rows.shape, f32),
            shaped((1, 1), f32),
        ],
        [SMEM] + [VMEM] * 4 + [ANY] * PARTS,
        [ANY] * 2 + [VMEM] * 3,
        scratch_shapes=[pltpu.SemaphoreType.DMA((PARTS, 5))],
    )(place, stats, lambdas, gain_rows, gate, *back)
    return (
        grad_queries.reshape(queries.shape),
        grad_vision.reshape(vision.shape),
        grad_lambdas,
        grad_gain.reshape(norm_gain.shape),
        grad_gate.reshape(gate_logit.shape),
    )


def solution(mesh):
    fine = Mesh(mesh.devices.reshape(8, 2, 2, PARTS, PARTS), DP + IMAGE)
    placed = (
        P(DP, IMAGE, None),
        P(DP, IMAGE, None, None),
        P(DP, IMAGE, None),
        P(DP, None),
        P(DP),
        P(),
        P(),
        P(),
    )
    return jax.shard_map(
        shards,
        mesh=fine,
        in_specs=placed,
        out_specs=(P(DP, IMAGE, None), P(DP, IMAGE, None, None), P(), P(), P()),
        check_vma=False,
    )
```

```python
import functools

import jax
import jax.numpy as jnp
from jax import lax
from jax.experimental import pallas as pl
from jax.experimental.pallas import tpu as pltpu
from jax.sharding import Mesh, PartitionSpec as P

rate_offset = 0.8
epsilon = 1e-05
DP = ("y", "zh", "core")
IMAGE = ("zl", "x")
FIRST, SECOND = 32, 16
PARTS = 4
GROUP = 2
ORDER, LATE = (0, 2, 1, 3), (0, 3, 1, 2)
VMEM = pl.BlockSpec(memory_space=pltpu.VMEM)
SMEM = pl.BlockSpec(memory_space=pltpu.SMEM)
ANY = pl.BlockSpec(memory_space=pl.ANY)
LIMIT = pltpu.CompilerParams(vmem_limit_bytes=32 * 2**20)
f32, bf16 = jnp.float32, jnp.bfloat16


def dot(a, b, contract):
    return lax.dot_general(
        a, b, ((contract[:1], contract[1:]), ((), ())), preferred_element_type=f32
    )


def wrap(index):
    return lax.rem(index + PARTS, PARTS)


def pack_vision_body(vision, out):
    half = vision.shape[1] // 4
    width = half // PARTS
    for g in range(PARTS):
        out[g, :, :width] = vision[:, g * width : (g + 1) * width]
        out[g, :, width : 2 * width] = vision[:, half + g * width : half + (g + 1) * width]
        out[g, :, 2 * width :] = vision[
            :, 2 * half + 2 * g * width : 2 * half + 2 * (g + 1) * width
        ]


def pack_text_body(queries, cotangent, out, sems):
    half = queries.shape[2] // 2
    width = half // PARTS
    copies = []
    for g in range(PARTS):
        pieces = (
            (queries, g * width, 0, width),
            (queries, half + g * width, width, width),
            (cotangent, 2 * g * width, 2 * width, 2 * width),
        )
        for i, (source, first, to, size) in enumerate(pieces):
            copies.append(
                pltpu.make_async_copy(
                    source.at[:, :, pl.ds(first, size)],
                    out.at[g, :, :, pl.ds(to, size)],
                    sems.at[g, i],
                )
            )
    for copy in copies:
        copy.start()
    for copy in copies:
        copy.wait()


def attend_body(
    place, assignment, counts, lambdas, norm_gain, gate, *refs, heads, head_size, patch
):
    text = refs[0]
    vision, payload, grad_vision = (refs[1 + i * PARTS : 1 + (i + 1) * PARTS] for i in range(3))
    vision = [vision[LATE.index(k)] for k in range(PARTS)]
    stats, gain, bias, raw_gain = refs[1 + 3 * PARTS :]
    zl, x = place[0], place[1]
    seqs, toks = text.shape[1:3]
    sources = [wrap(x - k) for k in ORDER]
    rows = PARTS * toks
    frames = PARTS * PARTS
    keys = frames * patch
    width = heads * head_size
    wide = 2 * head_size
    scale = head_size ** (-0.5)
    first_exp = jnp.exp(jnp.sum(lambdas[0] * lambdas[1], axis=-1, keepdims=True))
    second_exp = jnp.exp(jnp.sum(lambdas[2] * lambdas[3], axis=-1, keepdims=True))
    all_rates = first_exp - second_exp + rate_offset
    head_index = lax.broadcasted_iota(jnp.int32, all_rates.shape, 0)
    shape = (wide, wide)
    diagonal = lax.broadcasted_iota(jnp.int32, shape, 0) == lax.broadcasted_iota(
        jnp.int32, shape, 1
    )
    eye = jnp.where(diagonal, 1.0, 0.0).astype(bf16)
    gain_row = norm_gain[...] * (jnp.tanh(gate[...]) * (1.0 - rate_offset))
    gain[...] = jnp.broadcast_to(
        jnp.sum(jnp.where(diagonal, gain_row, 0.0), axis=1, keepdims=True), gain.shape
    )
    spot = lax.broadcasted_iota(jnp.int32, (keys, rows), 0) // patch
    part = spot // PARTS
    frame = wrap(zl - part) * PARTS + spot - part * PARTS
    for v in range(seqs):
        bias[v] = jnp.where(frame < counts[v], 0.0, -jnp.inf)
    lane = lax.broadcasted_iota(jnp.int32, (1, head_size), 1)
    rate_row = jnp.zeros((1, head_size), f32)

    def map_columns(h, m):
        return pl.ds(m * width + h * head_size, head_size)

    def value_columns(h):
        return pl.ds(2 * width + h * wide, wide)

    def block(columns):
        joined = jnp.concatenate([part[:, :, columns] for part in vision], axis=0)
        return joined.astype(f32).reshape(frames, seqs, patch, -1)

    def of_video(joined, v):
        return joined[:, v].reshape(keys, -1).astype(bf16)

    place_of = [jnp.where(assignment[0, 0] == v, 0, 1) for v in range(seqs)]
    for first in range(0, heads, GROUP):
        chains = [(h, v) for h in range(first, first + GROUP) for v in range(seqs)]
        both = [(h, v, m) for h, v in chains for m in range(2)]
        rates, joined = {}, {}
        for h in range(first, first + GROUP):
            rates[h] = jnp.sum(
                jnp.where(head_index == x * heads + h, all_rates, 0.0), axis=0, keepdims=True
            )
            joined[h] = block(value_columns(h))
            for m in range(2):
                joined[h, m] = block(map_columns(h, m))
        values = {(h, v): of_video(joined[h], v) for h, v in chains}
        key_rows = {(h, v, m): of_video(joined[h, m], v) for h, v, m in both}
        queries = {
            (h, v, m): jnp.concatenate(
                [text[i, place_of[v], :, map_columns(h, m)] for i in sources], axis=0
            )
            for h, v, m in both
        }
        scores = {c: dot(key_rows[c], queries[c], (1, 1)) + bias[c[1]] for c in both}
        shifted = {
            c: jnp.exp((scores[c] - jnp.max(scores[c], axis=0, keepdims=True)) * scale)
            for c in both
        }
        probs = {
            c: shifted[c] * (1.0 / jnp.sum(shifted[c], axis=0, keepdims=True)) for c in both
        }
        rated = {c: rates[c[0]] * probs[(*c, 1)] for c in chains}
        mixed = {c: (probs[(*c, 0)] - rated[c]).astype(bf16) for c in chains}
        attended = {c: dot(values[c], mixed[c], (0, 0)) for c in chains}
        grad_out = {
            (h, v): dot(
                eye,
                jnp.concatenate(
                    [text[i, place_of[v], :, value_columns(h)] for i in sources], axis=0
                ),
                (1, 1),
            )
            for h, v in chains
        }
        inverse_rms = {
            c: lax.rsqrt(jnp.mean(attended[c] * attended[c], axis=0, keepdims=True) + epsilon)
            for c in chains
        }
        grad_attended = {}
        for c in chains:
            normed = attended[c] * inverse_rms[c]
            product = grad_out[c] * normed
            halves = product[:, :head_size] + product[:, head_size:]
            raw_gain[...] = halves if c == (0, 0) else raw_gain[...] + halves
            middle = jnp.mean(product * gain[...], axis=0, keepdims=True)
            grad_attended[c] = (
                inverse_rms[c] * (grad_out[c] * gain[...] - normed * middle)
            ).astype(bf16)
        grad_mixed = {c: dot(values[c], grad_attended[c], (1, 0)) * scale for c in chains}
        grad_values = {c: dot(mixed[c], grad_attended[c], (1, 1)) for c in chains}
        sums = {
            c: jnp.sum(grad_mixed[c[:2]] * probs[c], axis=0, keepdims=True) for c in both
        }
        grad_scores = {}
        for c in chains:
            grad_scores[(*c, 0)] = (probs[(*c, 0)] * (grad_mixed[c] - sums[(*c, 0)])).astype(bf16)
            grad_scores[(*c, 1)] = (rated[c] * (sums[(*c, 1)] - grad_mixed[c])).astype(bf16)
        grad_keys = {c: dot(grad_scores[c], queries[c], (1, 0)) for c in both}
        for h, v, m in both:
            grad_query = dot(grad_scores[h, v, m], key_rows[h, v, m], (0, 0)).astype(bf16)
            own_rows = pl.ds(pl.multiple_of(place_of[v] * toks, toks), toks)
            for i in range(PARTS):
                payload[i][own_rows, map_columns(h, m)] = grad_query[i * toks : (i + 1) * toks]
        for h in range(first, first + GROUP):
            for columns, parts in (
                (map_columns(h, 0), [grad_keys[h, v, 0] for v in range(seqs)]),
                (map_columns(h, 1), [grad_keys[h, v, 1] for v in range(seqs)]),
                (value_columns(h), [grad_values[h, v] for v in range(seqs)]),
            ):
                parts = [p.reshape(frames, patch, -1) for p in parts]
                total = jnp.concatenate(parts, axis=1).astype(bf16)
                for j in range(PARTS):
                    grad_vision[j][:, :, columns] = total[j * PARTS : (j + 1) * PARTS]
            total_rate = sum(sums[h, v, 1] for v in range(seqs))
            own_rate = jnp.sum(total_rate, axis=1, keepdims=True) * (-1.0 / scale)
            rate_row = jnp.where(lane == x * heads + h, own_rate, rate_row)
    gains = jnp.sum(raw_gain[...].T, axis=0, keepdims=True)
    row = lax.broadcasted_iota(jnp.int32, stats.shape[1:], 0)
    tile = jnp.where(row == 0, gains[:, :head_size], 0.0)
    tile = jnp.where(row == 1, gains[:, head_size:], tile)
    tile = jnp.where(row == 2, rate_row, tile)
    for i in range(stats.shape[0]):
        stats[i] = tile


def sum_vision_body(place, after, *refs):
    del after
    parts, outs, total, sems = (
        refs[:PARTS],
        refs[2 * PARTS : 3 * PARTS],
        refs[3 * PARTS],
        refs[3 * PARTS + 1],
    )
    rows, columns = total.shape[1] // 2, total.shape[2]
    copies = []
    for k in range(PARTS):
        x = wrap(place[1] - ORDER[k])
        value = parts[0][x].astype(f32)
        for part in parts[1:]:
            value = value + part[x].astype(f32)
        value = value.astype(bf16)
        total[k, :rows] = value[:, :columns]
        total[k, rows:] = value[:, columns:]
        base = outs[k].shape[0] - 2 * rows
        copies.append(
            pltpu.make_async_copy(total.at[k], outs[k].at[pl.ds(base, 2 * rows)], sems.at[k])
        )
        copies[k].start()
    for copy in copies:
        copy.wait()


def spread_sum_body(tiles, after, out):
    del after
    total = jnp.sum(tiles[...], axis=0)
    for i in range(out.shape[0]):
        out[i] = total


def finish_body(place, tiles, lambdas, norm_gain, gate, *refs):
    parts, grad_queries, grad_vision, grad_lambdas, grad_gain, grad_gate = (
        refs[:PARTS],
        *refs[PARTS:],
    )
    text_rows, rows = grad_queries.shape[0], grad_vision.shape[0]
    half = grad_queries.shape[1] // 2
    width = half // PARTS
    for k in range(PARTS):
        g = wrap(place[1] + ORDER[k])
        first = pl.multiple_of(g * width, width)
        second = pl.multiple_of(half + g * width, width)
        wide = pl.multiple_of(2 * half + 2 * g * width, 2 * width)
        own = parts[k]
        grad_queries[:, pl.ds(first, width)] = own[:text_rows, :width]
        grad_queries[:, pl.ds(second, width)] = own[:text_rows, width:]
        grad_vision[:, pl.ds(first, width)] = own[text_rows : text_rows + rows, :width]
        grad_vision[:, pl.ds(second, width)] = own[text_rows : text_rows + rows, width:]
        grad_vision[:, pl.ds(wide, 2 * width)] = own[text_rows + rows :, :]
    total = jnp.sum(tiles[...], axis=0)
    head_count, head_size = lambdas.shape[1:]
    gate_tanh = jnp.tanh(gate[...])
    grad_gain[...] = total[:2] * (gate_tanh * (1.0 - rate_offset))
    weighed = jnp.sum(total[:2] * norm_gain[...], axis=-1, keepdims=True)
    grad_gate[...] = (
        jnp.sum(weighed, axis=0, keepdims=True)
        * (1.0 - rate_offset)
        * (1.0 - gate_tanh * gate_tanh)
    )
    shape = (head_count, head_size)
    own = lax.broadcasted_iota(jnp.int32, shape, 0) == lax.broadcasted_iota(jnp.int32, shape, 1)
    grad_rate = jnp.sum(jnp.where(own, total[2:3], 0.0), axis=-1, keepdims=True)
    first_exp = jnp.exp(jnp.sum(lambdas[0] * lambdas[1], axis=-1, keepdims=True))
    second_exp = jnp.exp(jnp.sum(lambdas[2] * lambdas[3], axis=-1, keepdims=True))
    weight_one, weight_two = grad_rate * first_exp, grad_rate * second_exp
    grad_lambdas[0] = weight_one * lambdas[1]
    grad_lambdas[1] = weight_one * lambdas[0]
    grad_lambdas[2] = -weight_two * lambdas[3]
    grad_lambdas[3] = -weight_two * lambdas[2]


def shift_all(parts, axis, order, way):
    return [
        lax.ppermute(part, axis, [(i, (i + way * k) % PARTS) for i in range(PARTS)]) if k else part
        for part, k in zip(parts, order)
    ]


def kernel(body, out_shape, in_specs, out_specs, **more):
    return pl.pallas_call(
        body,
        out_shape=out_shape,
        in_specs=in_specs,
        out_specs=out_specs,
        compiler_params=LIMIT,
        **more,
    )


def shaped(shape, dtype=bf16):
    return jax.ShapeDtypeStruct(shape, dtype)


def exchange(value, axes):
    return lax.all_to_all(value, axes, 0, 0, tiled=True)


def attend_call(place, assignment, counts, lambdas, norm_gain, gate, text, *vision):
    seqs, toks, columns = text.shape[1:]
    head_count, head_size = lambdas.shape[1:]
    heads = head_count // PARTS
    slab = vision[0].shape
    rows = slab[1]
    return kernel(
        functools.partial(
            attend_body, heads=heads, head_size=head_size, patch=rows // seqs
        ),
        [shaped((seqs * toks + 2 * rows, columns // 2))] * PARTS
        + [shaped(slab)] * PARTS
        + [shaped((FIRST, 4, head_size), f32)],
        [SMEM] * 3 + [VMEM] * (4 + PARTS),
        [VMEM] * (2 * PARTS + 1),
        scratch_shapes=[
            pltpu.VMEM((2 * head_size, PARTS * toks), f32),
            pltpu.VMEM((seqs, PARTS * PARTS * rows // seqs, PARTS * toks), f32),
            pltpu.VMEM((2 * head_size, head_size), f32),
        ],
    )(place, assignment, counts, lambdas, norm_gain, gate, text, *vision)


def shards(queries, vision, cotangent, assignment, frame_counts, lambdas, norm_gain, gate_logit):
    seqs, toks, text_columns = queries.shape
    frames_dev, patch, vision_columns = vision.shape[1:]
    head_count, head_size = lambdas.shape[1:]
    heads = head_count // PARTS
    rows = seqs * frames_dev * patch
    place = jnp.stack([lax.axis_index("zl"), lax.axis_index("x")]).astype(jnp.int32)
    slab = shaped((PARTS, rows, vision_columns // PARTS))
    gain_rows = norm_gain.reshape(-1, head_size)
    gate = gate_logit.reshape(1, 1)

    sent_vision = kernel(pack_vision_body, slab, [VMEM], VMEM)(
        vision.reshape(rows, vision_columns)
    )
    row_vision = exchange(sent_vision, "x")
    sent_text = kernel(
        pack_text_body,
        shaped((PARTS, seqs, toks, 2 * text_columns // PARTS)),
        [ANY] * 2,
        ANY,
        scratch_shapes=[pltpu.SemaphoreType.DMA((PARTS, 3))],
    )(queries, cotangent)
    held_text = exchange(sent_text, "x")
    held_vision = shift_all([row_vision] * PARTS, "zl", LATE, 1)

    grads = attend_call(
        place,
        assignment,
        frame_counts,
        lambdas,
        norm_gain.reshape(1, -1),
        gate,
        held_text,
        *held_vision,
    )
    payload, grad_vision, stats = grads[:PARTS], grads[PARTS : 2 * PARTS], grads[2 * PARTS]

    back_vision = shift_all(grad_vision, "zl", range(PARTS), -1)
    stats = exchange(stats, ("y", "x"))
    payload = kernel(
        sum_vision_body,
        [shaped(payload[0].shape)] * PARTS,
        [SMEM, ANY] + [VMEM] * PARTS + [ANY] * PARTS,
        [ANY] * PARTS,
        scratch_shapes=[
            pltpu.VMEM((PARTS, 2 * rows, text_columns // PARTS), bf16),
            pltpu.SemaphoreType.DMA((PARTS,)),
        ],
        input_output_aliases={2 + PARTS + k: k for k in range(PARTS)},
    )(place, stats, *back_vision, *payload)
    back = shift_all(payload, "x", ORDER, -1)
    stats = kernel(spread_sum_body, shaped((SECOND, 4, head_size), f32), [VMEM, ANY], VMEM)(
        stats, payload[0]
    )
    stats = exchange(stats, ("zh", "core", "zl"))
    grad_queries, grad_vision, grad_lambdas, grad_gain, grad_gate = kernel(
        finish_body,
        [
            shaped((seqs * toks, text_columns)),
            shaped((rows, vision_columns)),
            shaped(lambdas.shape, f32),
            shaped(gain_rows.shape, f32),
            shaped((1, 1), f32),
        ],
        [SMEM] + [VMEM] * (4 + PARTS),
        [VMEM] * 5,
    )(place, stats, lambdas, gain_rows, gate, *back)
    return (
        grad_queries.reshape(queries.shape),
        grad_vision.reshape(vision.shape),
        grad_lambdas,
        grad_gain.reshape(norm_gain.shape),
        grad_gate.reshape(gate_logit.shape),
    )


def solution(mesh):
    fine = Mesh(mesh.devices.reshape(8, 2, 2, PARTS, PARTS), DP + IMAGE)
    placed = (
        P(DP, IMAGE, None),
        P(DP, IMAGE, None, None),
        P(DP, IMAGE, None),
        P(DP, None),
        P(DP),
        P(),
        P(),
        P(),
    )
    return jax.shard_map(
        shards,
        mesh=fine,
        in_specs=placed,
        out_specs=(P(DP, IMAGE, None), P(DP, IMAGE, None, None), P(), P(), P()),
        check_vma=False,
    )
```

```python
import functools

import jax
import jax.numpy as jnp
from jax import lax
from jax.experimental import pallas as pl
from jax.experimental.pallas import tpu as pltpu
from jax.sharding import Mesh, PartitionSpec as P

rate_offset = 0.8
epsilon = 1e-05
DP = ("y", "zh", "core")
IMAGE = ("zl", "x")
FIRST, SECOND = 32, 16
PARTS = 4
GROUP = 2
ORDER, LATE = (0, 2, 1, 3), (0, 3, 1, 2)
VMEM = pl.BlockSpec(memory_space=pltpu.VMEM)
SMEM = pl.BlockSpec(memory_space=pltpu.SMEM)
ANY = pl.BlockSpec(memory_space=pl.ANY)
LIMIT = pltpu.CompilerParams(vmem_limit_bytes=32 * 2**20)
f32, bf16 = jnp.float32, jnp.bfloat16


def dot(a, b, contract):
    return lax.dot_general(
        a, b, ((contract[:1], contract[1:]), ((), ())), preferred_element_type=f32
    )


def wrap(index):
    return lax.rem(index + PARTS, PARTS)


def pack_vision_body(vision, out):
    half = vision.shape[1] // 4
    width = half // PARTS
    for g in range(PARTS):
        out[g, :, :width] = vision[:, g * width : (g + 1) * width]
        out[g, :, width : 2 * width] = vision[:, half + g * width : half + (g + 1) * width]
        out[g, :, 2 * width :] = vision[
            :, 2 * half + 2 * g * width : 2 * half + 2 * (g + 1) * width
        ]


def pack_text_body(place, queries, cotangent, after, *refs, shifts):
    del after
    outs, sems = refs[:-1], refs[-1]
    half = queries.shape[2] // 2
    width = half // PARTS
    copies = []
    for n, shift in enumerate(shifts):
        g = wrap(place[1] + shift)
        first = pl.multiple_of(g * width, width)
        second = pl.multiple_of(half + g * width, width)
        wide = pl.multiple_of(2 * g * width, 2 * width)
        pieces = (
            (queries.at[:, :, pl.ds(first, width)], pl.ds(0, width)),
            (queries.at[:, :, pl.ds(second, width)], pl.ds(width, width)),
            (cotangent.at[:, :, pl.ds(wide, 2 * width)], pl.ds(2 * width, 2 * width)),
        )
        for i, (source, columns) in enumerate(pieces):
            copies.append(
                pltpu.make_async_copy(source, outs[n].at[:, :, columns], sems.at[n, i])
            )
    for copy in copies:
        copy.start()
    for copy in copies:
        copy.wait()


def attend_body(
    place, assignment, counts, lambdas, norm_gain, gate, *refs, heads, head_size, patch
):
    text, vision, payload, grad_vision = (refs[i * PARTS : (i + 1) * PARTS] for i in range(4))
    vision = [vision[LATE.index(k)] for k in range(PARTS)]
    stats, gain, bias, raw_gain = refs[4 * PARTS :]
    zl, x = place[0], place[1]
    seqs, toks = text[0].shape[:2]
    rows = PARTS * toks
    frames = PARTS * PARTS
    keys = frames * patch
    width = heads * head_size
    wide = 2 * head_size
    scale = head_size ** (-0.5)
    first_exp = jnp.exp(jnp.sum(lambdas[0] * lambdas[1], axis=-1, keepdims=True))
    second_exp = jnp.exp(jnp.sum(lambdas[2] * lambdas[3], axis=-1, keepdims=True))
    all_rates = first_exp - second_exp + rate_offset
    head_index = lax.broadcasted_iota(jnp.int32, all_rates.shape, 0)
    shape = (wide, wide)
    diagonal = lax.broadcasted_iota(jnp.int32, shape, 0) == lax.broadcasted_iota(
        jnp.int32, shape, 1
    )
    eye = jnp.where(diagonal, 1.0, 0.0).astype(bf16)
    gain_row = norm_gain[...] * (jnp.tanh(gate[...]) * (1.0 - rate_offset))
    gain[...] = jnp.broadcast_to(
        jnp.sum(jnp.where(diagonal, gain_row, 0.0), axis=1, keepdims=True), gain.shape
    )
    spot = lax.broadcasted_iota(jnp.int32, (keys, rows), 0) // patch
    part = spot // PARTS
    frame = wrap(zl - part) * PARTS + spot - part * PARTS
    for v in range(seqs):
        bias[v] = jnp.where(frame < counts[v], 0.0, -jnp.inf)
    lane = lax.broadcasted_iota(jnp.int32, (1, head_size), 1)
    rate_row = jnp.zeros((1, head_size), f32)

    def map_columns(h, m):
        return pl.ds(m * width + h * head_size, head_size)

    def value_columns(h):
        return pl.ds(2 * width + h * wide, wide)

    def block(columns):
        joined = jnp.concatenate([part[:, :, columns] for part in vision], axis=0)
        return joined.astype(f32).reshape(frames, seqs, patch, -1)

    def of_video(joined, v):
        return joined[:, v].reshape(keys, -1).astype(bf16)

    place_of = [jnp.where(assignment[0, 0] == v, 0, 1) for v in range(seqs)]
    for first in range(0, heads, GROUP):
        chains = [(h, v) for h in range(first, first + GROUP) for v in range(seqs)]
        both = [(h, v, m) for h, v in chains for m in range(2)]
        rates, joined = {}, {}
        for h in range(first, first + GROUP):
            rates[h] = jnp.sum(
                jnp.where(head_index == x * heads + h, all_rates, 0.0), axis=0, keepdims=True
            )
            joined[h] = block(value_columns(h))
            for m in range(2):
                joined[h, m] = block(map_columns(h, m))
        values = {(h, v): of_video(joined[h], v) for h, v in chains}
        key_rows = {(h, v, m): of_video(joined[h, m], v) for h, v, m in both}
        queries = {
            (h, v, m): jnp.concatenate(
                [part[place_of[v], :, map_columns(h, m)] for part in text], axis=0
            )
            for h, v, m in both
        }
        scores = {c: dot(key_rows[c], queries[c], (1, 1)) + bias[c[1]] for c in both}
        shifted = {
            c: jnp.exp((scores[c] - jnp.max(scores[c], axis=0, keepdims=True)) * scale)
            for c in both
        }
        probs = {
            c: shifted[c] * (1.0 / jnp.sum(shifted[c], axis=0, keepdims=True)) for c in both
        }
        rated = {c: rates[c[0]] * probs[(*c, 1)] for c in chains}
        mixed = {c: (probs[(*c, 0)] - rated[c]).astype(bf16) for c in chains}
        attended = {c: dot(values[c], mixed[c], (0, 0)) for c in chains}
        grad_out = {
            (h, v): dot(
                eye,
                jnp.concatenate(
                    [part[place_of[v], :, value_columns(h)] for part in text], axis=0
                ),
                (1, 1),
            )
            for h, v in chains
        }
        inverse_rms = {
            c: lax.rsqrt(jnp.mean(attended[c] * attended[c], axis=0, keepdims=True) + epsilon)
            for c in chains
        }
        grad_attended = {}
        for c in chains:
            normed = attended[c] * inverse_rms[c]
            product = grad_out[c] * normed
            halves = product[:, :head_size] + product[:, head_size:]
            raw_gain[...] = halves if c == (0, 0) else raw_gain[...] + halves
            middle = jnp.mean(product * gain[...], axis=0, keepdims=True)
            grad_attended[c] = (
                inverse_rms[c] * (grad_out[c] * gain[...] - normed * middle)
            ).astype(bf16)
        grad_mixed = {c: dot(values[c], grad_attended[c], (1, 0)) * scale for c in chains}
        grad_values = {c: dot(mixed[c], grad_attended[c], (1, 1)) for c in chains}
        sums = {
            c: jnp.sum(grad_mixed[c[:2]] * probs[c], axis=0, keepdims=True) for c in both
        }
        grad_scores = {}
        for c in chains:
            grad_scores[(*c, 0)] = (probs[(*c, 0)] * (grad_mixed[c] - sums[(*c, 0)])).astype(bf16)
            grad_scores[(*c, 1)] = (rated[c] * (sums[(*c, 1)] - grad_mixed[c])).astype(bf16)
        grad_keys = {c: dot(grad_scores[c], queries[c], (1, 0)) for c in both}
        for h, v, m in both:
            grad_query = dot(grad_scores[h, v, m], key_rows[h, v, m], (0, 0)).astype(bf16)
            own_rows = pl.ds(pl.multiple_of(place_of[v] * toks, toks), toks)
            for i in range(PARTS):
                payload[i][own_rows, map_columns(h, m)] = grad_query[i * toks : (i + 1) * toks]
        for h in range(first, first + GROUP):
            for columns, parts in (
                (map_columns(h, 0), [grad_keys[h, v, 0] for v in range(seqs)]),
                (map_columns(h, 1), [grad_keys[h, v, 1] for v in range(seqs)]),
                (value_columns(h), [grad_values[h, v] for v in range(seqs)]),
            ):
                parts = [p.reshape(frames, patch, -1) for p in parts]
                total = jnp.concatenate(parts, axis=1).astype(bf16)
                for j in range(PARTS):
                    grad_vision[j][:, :, columns] = total[j * PARTS : (j + 1) * PARTS]
            total_rate = sum(sums[h, v, 1] for v in range(seqs))
            own_rate = jnp.sum(total_rate, axis=1, keepdims=True) * (-1.0 / scale)
            rate_row = jnp.where(lane == x * heads + h, own_rate, rate_row)
    gains = jnp.sum(raw_gain[...].T, axis=0, keepdims=True)
    row = lax.broadcasted_iota(jnp.int32, stats.shape[1:], 0)
    tile = jnp.where(row == 0, gains[:, :head_size], 0.0)
    tile = jnp.where(row == 1, gains[:, head_size:], tile)
    tile = jnp.where(row == 2, rate_row, tile)
    for i in range(stats.shape[0]):
        stats[i] = tile


def sum_vision_body(place, after, *refs):
    del after
    parts, outs, total, sems = (
        refs[:PARTS],
        refs[2 * PARTS : 3 * PARTS],
        refs[3 * PARTS],
        refs[3 * PARTS + 1],
    )
    rows, columns = total.shape[1] // 2, total.shape[2]
    copies = []
    for k in range(PARTS):
        x = wrap(place[1] - ORDER[k])
        value = parts[0][x].astype(f32)
        for part in parts[1:]:
            value = value + part[x].astype(f32)
        value = value.astype(bf16)
        total[k, :rows] = value[:, :columns]
        total[k, rows:] = value[:, columns:]
        base = outs[k].shape[0] - 2 * rows
        copies.append(
            pltpu.make_async_copy(total.at[k], outs[k].at[pl.ds(base, 2 * rows)], sems.at[k])
        )
        copies[k].start()
    for copy in copies:
        copy.wait()


def spread_sum_body(tiles, after, out):
    del after
    total = jnp.sum(tiles[...], axis=0)
    for i in range(out.shape[0]):
        out[i] = total


def finish_body(place, tiles, lambdas, norm_gain, gate, *refs):
    parts, grad_queries, grad_vision, grad_lambdas, grad_gain, grad_gate = (
        refs[:PARTS],
        *refs[PARTS:],
    )
    text_rows, rows = grad_queries.shape[0], grad_vision.shape[0]
    half = grad_queries.shape[1] // 2
    width = half // PARTS
    for k in range(PARTS):
        g = wrap(place[1] + ORDER[k])
        first = pl.multiple_of(g * width, width)
        second = pl.multiple_of(half + g * width, width)
        wide = pl.multiple_of(2 * half + 2 * g * width, 2 * width)
        own = parts[k]
        grad_queries[:, pl.ds(first, width)] = own[:text_rows, :width]
        grad_queries[:, pl.ds(second, width)] = own[:text_rows, width:]
        grad_vision[:, pl.ds(first, width)] = own[text_rows : text_rows + rows, :width]
        grad_vision[:, pl.ds(second, width)] = own[text_rows : text_rows + rows, width:]
        grad_vision[:, pl.ds(wide, 2 * width)] = own[text_rows + rows :, :]
    total = jnp.sum(tiles[...], axis=0)
    head_count, head_size = lambdas.shape[1:]
    gate_tanh = jnp.tanh(gate[...])
    grad_gain[...] = total[:2] * (gate_tanh * (1.0 - rate_offset))
    weighed = jnp.sum(total[:2] * norm_gain[...], axis=-1, keepdims=True)
    grad_gate[...] = (
        jnp.sum(weighed, axis=0, keepdims=True)
        * (1.0 - rate_offset)
        * (1.0 - gate_tanh * gate_tanh)
    )
    shape = (head_count, head_size)
    own = lax.broadcasted_iota(jnp.int32, shape, 0) == lax.broadcasted_iota(jnp.int32, shape, 1)
    grad_rate = jnp.sum(jnp.where(own, total[2:3], 0.0), axis=-1, keepdims=True)
    first_exp = jnp.exp(jnp.sum(lambdas[0] * lambdas[1], axis=-1, keepdims=True))
    second_exp = jnp.exp(jnp.sum(lambdas[2] * lambdas[3], axis=-1, keepdims=True))
    weight_one, weight_two = grad_rate * first_exp, grad_rate * second_exp
    grad_lambdas[0] = weight_one * lambdas[1]
    grad_lambdas[1] = weight_one * lambdas[0]
    grad_lambdas[2] = -weight_two * lambdas[3]
    grad_lambdas[3] = -weight_two * lambdas[2]


def shift_all(parts, axis, order, way):
    return [
        lax.ppermute(part, axis, [(i, (i + way * k) % PARTS) for i in range(PARTS)]) if k else part
        for part, k in zip(parts, order)
    ]


def kernel(body, out_shape, in_specs, out_specs, **more):
    return pl.pallas_call(
        body,
        out_shape=out_shape,
        in_specs=in_specs,
        out_specs=out_specs,
        compiler_params=LIMIT,
        **more,
    )


def shaped(shape, dtype=bf16):
    return jax.ShapeDtypeStruct(shape, dtype)


def exchange(value, axes):
    return lax.all_to_all(value, axes, 0, 0, tiled=True)


def attend_call(place, assignment, counts, lambdas, norm_gain, gate, text, vision):
    seqs, toks, columns = text[0].shape
    head_count, head_size = lambdas.shape[1:]
    heads = head_count // PARTS
    slab = vision[0].shape
    rows = slab[1]
    return kernel(
        functools.partial(
            attend_body, heads=heads, head_size=head_size, patch=rows // seqs
        ),
        [shaped((seqs * toks + 2 * rows, columns // 2))] * PARTS
        + [shaped(slab)] * PARTS
        + [shaped((FIRST, 4, head_size), f32)],
        [SMEM] * 3 + [VMEM] * (3 + 2 * PARTS),
        [VMEM] * (2 * PARTS + 1),
        scratch_shapes=[
            pltpu.VMEM((2 * head_size, PARTS * toks), f32),
            pltpu.VMEM((seqs, PARTS * PARTS * rows // seqs, PARTS * toks), f32),
            pltpu.VMEM((2 * head_size, head_size), f32),
        ],
    )(place, assignment, counts, lambdas, norm_gain, gate, *text, *vision)


def shards(queries, vision, cotangent, assignment, frame_counts, lambdas, norm_gain, gate_logit):
    seqs, toks, text_columns = queries.shape
    frames_dev, patch, vision_columns = vision.shape[1:]
    head_count, head_size = lambdas.shape[1:]
    heads = head_count // PARTS
    rows = seqs * frames_dev * patch
    place = jnp.stack([lax.axis_index("zl"), lax.axis_index("x")]).astype(jnp.int32)
    slab = shaped((PARTS, rows, vision_columns // PARTS))
    gain_rows = norm_gain.reshape(-1, head_size)
    gate = gate_logit.reshape(1, 1)

    sent_vision = kernel(pack_vision_body, slab, [VMEM], VMEM)(
        vision.reshape(rows, vision_columns)
    )
    row_vision = exchange(sent_vision, "x")
    sent_text = {}
    for shifts, after in (((2,), place), ((0, 1, 3), row_vision)):
        packed = kernel(
            functools.partial(pack_text_body, shifts=shifts),
            [shaped((seqs, toks, 2 * text_columns // PARTS))] * len(shifts),
            [SMEM, ANY, ANY, ANY],
            [ANY] * len(shifts),
            scratch_shapes=[pltpu.SemaphoreType.DMA((len(shifts), 3))],
        )(place, queries, cotangent, after)
        sent_text.update(zip(shifts, packed))
    held_text = shift_all([sent_text[k] for k in ORDER], "x", ORDER, 1)
    held_vision = shift_all([row_vision] * PARTS, "zl", LATE, 1)

    grads = attend_call(
        place,
        assignment,
        frame_counts,
        lambdas,
        norm_gain.reshape(1, -1),
        gate,
        held_text,
        held_vision,
    )
    payload, grad_vision, stats = grads[:PARTS], grads[PARTS : 2 * PARTS], grads[2 * PARTS]

    back_vision = shift_all(grad_vision, "zl", range(PARTS), -1)
    stats = exchange(stats, ("y", "x"))
    payload = kernel(
        sum_vision_body,
        [shaped(payload[0].shape)] * PARTS,
        [SMEM, ANY] + [VMEM] * PARTS + [ANY] * PARTS,
        [ANY] * PARTS,
        scratch_shapes=[
            pltpu.VMEM((PARTS, 2 * rows, text_columns // PARTS), bf16),
            pltpu.SemaphoreType.DMA((PARTS,)),
        ],
        input_output_aliases={2 + PARTS + k: k for k in range(PARTS)},
    )(place, stats, *back_vision, *payload)
    back = shift_all(payload, "x", ORDER, -1)
    stats = kernel(spread_sum_body, shaped((SECOND, 4, head_size), f32), [VMEM, ANY], VMEM)(
        stats, payload[0]
    )
    stats = exchange(stats, ("zh", "core", "zl"))
    grad_queries, grad_vision, grad_lambdas, grad_gain, grad_gate = kernel(
        finish_body,
        [
            shaped((seqs * toks, text_columns)),
            shaped((rows, vision_columns)),
            shaped(lambdas.shape, f32),
            shaped(gain_rows.shape, f32),
            shaped((1, 1), f32),
        ],
        [SMEM] + [VMEM] * (4 + PARTS),
        [VMEM] * 5,
    )(place, stats, lambdas, gain_rows, gate, *back)
    return (
        grad_queries.reshape(queries.shape),
        grad_vision.reshape(vision.shape),
        grad_lambdas,
        grad_gain.reshape(norm_gain.shape),
        grad_gate.reshape(gate_logit.shape),
    )


def solution(mesh):
    fine = Mesh(mesh.devices.reshape(8, 2, 2, PARTS, PARTS), DP + IMAGE)
    placed = (
        P(DP, IMAGE, None),
        P(DP, IMAGE, None, None),
        P(DP, IMAGE, None),
        P(DP, None),
        P(DP),
        P(),
        P(),
        P(),
    )
    return jax.shard_map(
        shards,
        mesh=fine,
        in_specs=placed,
        out_specs=(P(DP, IMAGE, None), P(DP, IMAGE, None, None), P(), P(), P()),
        check_vma=False,
    )
```

```python
import functools

import jax
import jax.numpy as jnp
from jax import lax
from jax.experimental import pallas as pl
from jax.experimental.pallas import tpu as pltpu
from jax.sharding import Mesh, PartitionSpec as P

rate_offset = 0.8
epsilon = 1e-05
DP = ("y", "zh", "core")
IMAGE = ("zl", "x")
FIRST, SECOND = 32, 16
PARTS = 4
GROUP = 2
ORDER = (0, 2, 1, 3)
LATE = (0, 1, 3, 2)
VMEM = pl.BlockSpec(memory_space=pltpu.VMEM)
SMEM = pl.BlockSpec(memory_space=pltpu.SMEM)
ANY = pl.BlockSpec(memory_space=pl.ANY)
LIMIT = pltpu.CompilerParams(vmem_limit_bytes=32 * 2**20)
f32, bf16 = jnp.float32, jnp.bfloat16


def dot(a, b, contract):
    return lax.dot_general(
        a, b, ((contract[:1], contract[1:]), ((), ())), preferred_element_type=f32
    )


def wrap(index):
    return lax.rem(index + PARTS, PARTS)


def pack_vision_body(vision, out):
    half = vision.shape[1] // 4
    width = half // PARTS
    for g in range(PARTS):
        out[g, :, :width] = vision[:, g * width : (g + 1) * width]
        out[g, :, width : 2 * width] = vision[:, half + g * width : half + (g + 1) * width]
        out[g, :, 2 * width :] = vision[
            :, 2 * half + 2 * g * width : 2 * half + 2 * (g + 1) * width
        ]


def pack_text_body(place, queries, cotangent, *refs, shifts):
    outs, sems = refs[-1 - len(shifts) : -1], refs[-1]
    half = queries.shape[2] // 2
    width = half // PARTS
    copies = []
    for n, shift in enumerate(shifts):
        g = wrap(place[1] + shift)
        first = pl.multiple_of(g * width, width)
        second = pl.multiple_of(half + g * width, width)
        wide = pl.multiple_of(2 * g * width, 2 * width)
        pieces = (
            (queries.at[:, :, pl.ds(first, width)], pl.ds(0, width)),
            (queries.at[:, :, pl.ds(second, width)], pl.ds(width, width)),
            (cotangent.at[:, :, pl.ds(wide, 2 * width)], pl.ds(2 * width, 2 * width)),
        )
        for i, (source, columns) in enumerate(pieces):
            copies.append(
                pltpu.make_async_copy(source, outs[n].at[:, :, columns], sems.at[n, i])
            )
    for copy in copies:
        copy.start()
    for copy in copies:
        copy.wait()


def attend_body(
    place, assignment, counts, lambdas, norm_gain, gate, *refs, heads, head_size, patch
):
    text, vision, payload, grad_vision = (refs[i * PARTS : (i + 1) * PARTS] for i in range(4))
    vision = [vision[LATE.index(k)] for k in range(PARTS)]
    stats, gain, bias, raw_gain = refs[4 * PARTS :]
    zl, x = place[0], place[1]
    seqs, toks = text[0].shape[:2]
    rows = PARTS * toks
    frames = PARTS * PARTS
    keys = frames * patch
    width = heads * head_size
    wide = 2 * head_size
    scale = head_size ** (-0.5)
    first_exp = jnp.exp(jnp.sum(lambdas[0] * lambdas[1], axis=-1, keepdims=True))
    second_exp = jnp.exp(jnp.sum(lambdas[2] * lambdas[3], axis=-1, keepdims=True))
    all_rates = first_exp - second_exp + rate_offset
    head_index = lax.broadcasted_iota(jnp.int32, all_rates.shape, 0)
    shape = (wide, wide)
    diagonal = lax.broadcasted_iota(jnp.int32, shape, 0) == lax.broadcasted_iota(
        jnp.int32, shape, 1
    )
    eye = jnp.where(diagonal, 1.0, 0.0).astype(bf16)
    gain_row = norm_gain[...] * (jnp.tanh(gate[...]) * (1.0 - rate_offset))
    gain[...] = jnp.broadcast_to(
        jnp.sum(jnp.where(diagonal, gain_row, 0.0), axis=1, keepdims=True), gain.shape
    )
    spot = lax.broadcasted_iota(jnp.int32, (keys, rows), 0) // patch
    part = spot // PARTS
    frame = (zl ^ part) * PARTS + spot - part * PARTS
    for v in range(seqs):
        bias[v] = jnp.where(frame < counts[v], 0.0, -jnp.inf)
    lane = lax.broadcasted_iota(jnp.int32, (1, head_size), 1)
    rate_row = jnp.zeros((1, head_size), f32)

    def map_columns(h, m):
        return pl.ds(m * width + h * head_size, head_size)

    def value_columns(h):
        return pl.ds(2 * width + h * wide, wide)

    def block(columns):
        joined = jnp.concatenate([part[:, :, columns] for part in vision], axis=0)
        return joined.astype(f32).reshape(frames, seqs, patch, -1)

    def of_video(joined, v):
        return joined[:, v].reshape(keys, -1).astype(bf16)

    place_of = [jnp.where(assignment[0, 0] == v, 0, 1) for v in range(seqs)]
    for first in range(0, heads, GROUP):
        chains = [(h, v) for h in range(first, first + GROUP) for v in range(seqs)]
        both = [(h, v, m) for h, v in chains for m in range(2)]
        rates, joined = {}, {}
        for h in range(first, first + GROUP):
            rates[h] = jnp.sum(
                jnp.where(head_index == x * heads + h, all_rates, 0.0), axis=0, keepdims=True
            )
            joined[h] = block(value_columns(h))
            for m in range(2):
                joined[h, m] = block(map_columns(h, m))
        values = {(h, v): of_video(joined[h], v) for h, v in chains}
        key_rows = {(h, v, m): of_video(joined[h, m], v) for h, v, m in both}
        queries = {
            (h, v, m): jnp.concatenate(
                [part[place_of[v], :, map_columns(h, m)] for part in text], axis=0
            )
            for h, v, m in both
        }
        scores = {c: dot(key_rows[c], queries[c], (1, 1)) + bias[c[1]] for c in both}
        shifted = {
            c: jnp.exp((scores[c] - jnp.max(scores[c], axis=0, keepdims=True)) * scale)
            for c in both
        }
        probs = {
            c: shifted[c] * (1.0 / jnp.sum(shifted[c], axis=0, keepdims=True)) for c in both
        }
        rated = {c: rates[c[0]] * probs[(*c, 1)] for c in chains}
        mixed = {c: (probs[(*c, 0)] - rated[c]).astype(bf16) for c in chains}
        attended = {c: dot(values[c], mixed[c], (0, 0)) for c in chains}
        grad_out = {
            (h, v): dot(
                eye,
                jnp.concatenate(
                    [part[place_of[v], :, value_columns(h)] for part in text], axis=0
                ),
                (1, 1),
            )
            for h, v in chains
        }
        inverse_rms = {
            c: lax.rsqrt(jnp.mean(attended[c] * attended[c], axis=0, keepdims=True) + epsilon)
            for c in chains
        }
        grad_attended = {}
        for c in chains:
            normed = attended[c] * inverse_rms[c]
            product = grad_out[c] * normed
            halves = product[:, :head_size] + product[:, head_size:]
            raw_gain[...] = halves if c == (0, 0) else raw_gain[...] + halves
            middle = jnp.mean(product * gain[...], axis=0, keepdims=True)
            grad_attended[c] = (
                inverse_rms[c] * (grad_out[c] * gain[...] - normed * middle)
            ).astype(bf16)
        grad_mixed = {c: dot(values[c], grad_attended[c], (1, 0)) * scale for c in chains}
        grad_values = {c: dot(mixed[c], grad_attended[c], (1, 1)) for c in chains}
        sums = {
            c: jnp.sum(grad_mixed[c[:2]] * probs[c], axis=0, keepdims=True) for c in both
        }
        grad_scores = {}
        for c in chains:
            grad_scores[(*c, 0)] = (probs[(*c, 0)] * (grad_mixed[c] - sums[(*c, 0)])).astype(bf16)
            grad_scores[(*c, 1)] = (rated[c] * (sums[(*c, 1)] - grad_mixed[c])).astype(bf16)
        grad_keys = {c: dot(grad_scores[c], queries[c], (1, 0)) for c in both}
        for h, v, m in both:
            grad_query = dot(grad_scores[h, v, m], key_rows[h, v, m], (0, 0)).astype(bf16)
            own_rows = pl.ds(pl.multiple_of(place_of[v] * toks, toks), toks)
            for i in range(PARTS):
                payload[i][own_rows, map_columns(h, m)] = grad_query[i * toks : (i + 1) * toks]
        for h in range(first, first + GROUP):
            for columns, parts in (
                (map_columns(h, 0), [grad_keys[h, v, 0] for v in range(seqs)]),
                (map_columns(h, 1), [grad_keys[h, v, 1] for v in range(seqs)]),
                (value_columns(h), [grad_values[h, v] for v in range(seqs)]),
            ):
                parts = [p.reshape(frames, patch, -1) for p in parts]
                total = jnp.concatenate(parts, axis=1).astype(bf16)
                for j in range(PARTS):
                    grad_vision[j][:, :, columns] = total[j * PARTS : (j + 1) * PARTS]
            total_rate = sum(sums[h, v, 1] for v in range(seqs))
            own_rate = jnp.sum(total_rate, axis=1, keepdims=True) * (-1.0 / scale)
            rate_row = jnp.where(lane == x * heads + h, own_rate, rate_row)
    gains = jnp.sum(raw_gain[...].T, axis=0, keepdims=True)
    row = lax.broadcasted_iota(jnp.int32, stats.shape[1:], 0)
    tile = jnp.where(row == 0, gains[:, :head_size], 0.0)
    tile = jnp.where(row == 1, gains[:, head_size:], tile)
    tile = jnp.where(row == 2, rate_row, tile)
    for i in range(stats.shape[0]):
        stats[i] = tile


def sum_vision_body(place, after, *refs):
    del after
    parts, outs, total, sems = (
        refs[:PARTS],
        refs[2 * PARTS : 3 * PARTS],
        refs[3 * PARTS],
        refs[3 * PARTS + 1],
    )
    rows, columns = total.shape[1] // 2, total.shape[2]
    copies = []
    for k in range(PARTS):
        x = wrap(place[1] - ORDER[k])
        value = parts[0][x].astype(f32)
        for part in parts[1:]:
            value = value + part[x].astype(f32)
        value = value.astype(bf16)
        total[k, :rows] = value[:, :columns]
        total[k, rows:] = value[:, columns:]
        base = outs[k].shape[0] - 2 * rows
        copies.append(
            pltpu.make_async_copy(total.at[k], outs[k].at[pl.ds(base, 2 * rows)], sems.at[k])
        )
        copies[k].start()
    for copy in copies:
        copy.wait()


def spread_sum_body(tiles, after, out):
    del after
    total = jnp.sum(tiles[...], axis=0)
    for i in range(out.shape[0]):
        out[i] = total


def finish_body(place, tiles, lambdas, norm_gain, gate, *refs):
    parts, grad_queries, grad_vision, grad_lambdas, grad_gain, grad_gate = (
        refs[:PARTS],
        *refs[PARTS:],
    )
    text_rows, rows = grad_queries.shape[0], grad_vision.shape[0]
    half = grad_queries.shape[1] // 2
    width = half // PARTS
    for k in range(PARTS):
        g = wrap(place[1] + ORDER[k])
        first = pl.multiple_of(g * width, width)
        second = pl.multiple_of(half + g * width, width)
        wide = pl.multiple_of(2 * half + 2 * g * width, 2 * width)
        own = parts[k]
        grad_queries[:, pl.ds(first, width)] = own[:text_rows, :width]
        grad_queries[:, pl.ds(second, width)] = own[:text_rows, width:]
        grad_vision[:, pl.ds(first, width)] = own[text_rows : text_rows + rows, :width]
        grad_vision[:, pl.ds(second, width)] = own[text_rows : text_rows + rows, width:]
        grad_vision[:, pl.ds(wide, 2 * width)] = own[text_rows + rows :, :]
    total = jnp.sum(tiles[...], axis=0)
    head_count, head_size = lambdas.shape[1:]
    gate_tanh = jnp.tanh(gate[...])
    grad_gain[...] = total[:2] * (gate_tanh * (1.0 - rate_offset))
    weighed = jnp.sum(total[:2] * norm_gain[...], axis=-1, keepdims=True)
    grad_gate[...] = (
        jnp.sum(weighed, axis=0, keepdims=True)
        * (1.0 - rate_offset)
        * (1.0 - gate_tanh * gate_tanh)
    )
    shape = (head_count, head_size)
    own = lax.broadcasted_iota(jnp.int32, shape, 0) == lax.broadcasted_iota(jnp.int32, shape, 1)
    grad_rate = jnp.sum(jnp.where(own, total[2:3], 0.0), axis=-1, keepdims=True)
    first_exp = jnp.exp(jnp.sum(lambdas[0] * lambdas[1], axis=-1, keepdims=True))
    second_exp = jnp.exp(jnp.sum(lambdas[2] * lambdas[3], axis=-1, keepdims=True))
    weight_one, weight_two = grad_rate * first_exp, grad_rate * second_exp
    grad_lambdas[0] = weight_one * lambdas[1]
    grad_lambdas[1] = weight_one * lambdas[0]
    grad_lambdas[2] = -weight_two * lambdas[3]
    grad_lambdas[3] = -weight_two * lambdas[2]


def send_all(parts, axis, targets):
    return [
        part if target is None else lax.ppermute(part, axis, [(i, target(i)) for i in range(PARTS)])
        for part, target in zip(parts, targets)
    ]


def shifts(order, way):
    return [(lambda i, k=k: (i + way * k) % PARTS) if k else None for k in order]


def partners(order):
    return [(lambda i, k=k: i ^ k) if k else None for k in order]


def kernel(body, out_shape, in_specs, out_specs, **more):
    return pl.pallas_call(
        body,
        out_shape=out_shape,
        in_specs=in_specs,
        out_specs=out_specs,
        compiler_params=LIMIT,
        **more,
    )


def shaped(shape, dtype=bf16):
    return jax.ShapeDtypeStruct(shape, dtype)


def exchange(value, axes):
    return lax.all_to_all(value, axes, 0, 0, tiled=True)


def attend_call(place, assignment, counts, lambdas, norm_gain, gate, text, vision):
    seqs, toks, columns = text[0].shape
    head_count, head_size = lambdas.shape[1:]
    heads = head_count // PARTS
    slab = vision[0].shape
    rows = slab[1]
    return kernel(
        functools.partial(
            attend_body, heads=heads, head_size=head_size, patch=rows // seqs
        ),
        [shaped((seqs * toks + 2 * rows, columns // 2))] * PARTS
        + [shaped(slab)] * PARTS
        + [shaped((FIRST, 4, head_size), f32)],
        [SMEM] * 3 + [VMEM] * (3 + 2 * PARTS),
        [VMEM] * (2 * PARTS + 1),
        scratch_shapes=[
            pltpu.VMEM((2 * head_size, PARTS * toks), f32),
            pltpu.VMEM((seqs, PARTS * PARTS * rows // seqs, PARTS * toks), f32),
            pltpu.VMEM((2 * head_size, head_size), f32),
        ],
    )(place, assignment, counts, lambdas, norm_gain, gate, *text, *vision)


def shards(queries, vision, cotangent, assignment, frame_counts, lambdas, norm_gain, gate_logit):
    seqs, toks, text_columns = queries.shape
    frames_dev, patch, vision_columns = vision.shape[1:]
    head_count, head_size = lambdas.shape[1:]
    heads = head_count // PARTS
    rows = seqs * frames_dev * patch
    place = jnp.stack([lax.axis_index("zl"), lax.axis_index("x")]).astype(jnp.int32)
    slab = shaped((PARTS, rows, vision_columns // PARTS))
    gain_rows = norm_gain.reshape(-1, head_size)
    gate = gate_logit.reshape(1, 1)

    sent_vision = kernel(pack_vision_body, slab, [VMEM], VMEM)(
        vision.reshape(rows, vision_columns)
    )
    row_vision = exchange(sent_vision, "x")
    sent_text = {}
    early = (row_vision, norm_gain.reshape(1, -1), assignment, frame_counts)
    for held, others in (((2,), ()), ((0, 1, 3), early)):
        packed = kernel(
            functools.partial(pack_text_body, shifts=held),
            [shaped((seqs, toks, 2 * text_columns // PARTS))] * len(held),
            [SMEM, ANY, ANY] + [ANY, VMEM, SMEM, SMEM][: len(others)],
            [ANY] * len(held),
            scratch_shapes=[pltpu.SemaphoreType.DMA((len(held), 3))],
        )(place, queries, cotangent, *others)
        sent_text.update(zip(held, packed))
    held_text = send_all([sent_text[k] for k in ORDER], "x", shifts(ORDER, 1))
    held_vision = send_all([row_vision] * PARTS, "zl", partners(LATE))

    grads = attend_call(
        place,
        assignment,
        frame_counts,
        lambdas,
        norm_gain.reshape(1, -1),
        gate,
        held_text,
        held_vision,
    )
    payload, grad_vision, stats = grads[:PARTS], grads[PARTS : 2 * PARTS], grads[2 * PARTS]

    back_vision = send_all(grad_vision, "zl", partners(range(PARTS)))
    stats = exchange(stats, ("y", "x"))
    payload = kernel(
        sum_vision_body,
        [shaped(payload[0].shape)] * PARTS,
        [SMEM, ANY] + [VMEM] * PARTS + [ANY] * PARTS,
        [ANY] * PARTS,
        scratch_shapes=[
            pltpu.VMEM((PARTS, 2 * rows, text_columns // PARTS), bf16),
            pltpu.SemaphoreType.DMA((PARTS,)),
        ],
        input_output_aliases={2 + PARTS + k: k for k in range(PARTS)},
    )(place, stats, *back_vision, *payload)
    back = send_all(payload, "x", shifts(ORDER, -1))
    stats = kernel(spread_sum_body, shaped((SECOND, 4, head_size), f32), [VMEM, ANY], VMEM)(
        stats, payload[0]
    )
    stats = exchange(stats, ("zh", "core", "zl"))
    grad_queries, grad_vision, grad_lambdas, grad_gain, grad_gate = kernel(
        finish_body,
        [
            shaped((seqs * toks, text_columns)),
            shaped((rows, vision_columns)),
            shaped(lambdas.shape, f32),
            shaped(gain_rows.shape, f32),
            shaped((1, 1), f32),
        ],
        [SMEM] + [VMEM] * (4 + PARTS),
        [VMEM] * 5,
    )(place, stats, lambdas, gain_rows, gate, *back)
    return (
        grad_queries.reshape(queries.shape),
        grad_vision.reshape(vision.shape),
        grad_lambdas,
        grad_gain.reshape(norm_gain.shape),
        grad_gate.reshape(gate_logit.shape),
    )


def solution(mesh):
    fine = Mesh(mesh.devices.reshape(8, 2, 2, PARTS, PARTS), DP + IMAGE)
    placed = (
        P(DP, IMAGE, None),
        P(DP, IMAGE, None, None),
        P(DP, IMAGE, None),
        P(DP, None),
        P(DP),
        P(),
        P(),
        P(),
    )
    return jax.shard_map(
        shards,
        mesh=fine,
        in_specs=placed,
        out_specs=(P(DP, IMAGE, None), P(DP, IMAGE, None, None), P(), P(), P()),
        check_vma=False,
    )
```

```python
import functools

import jax
import jax.numpy as jnp
from jax import lax
from jax.experimental import pallas as pl
from jax.experimental.pallas import tpu as pltpu
from jax.sharding import Mesh, PartitionSpec as P

rate_offset = 0.8
epsilon = 1e-05
DP = ("y", "zh", "core")
IMAGE = ("zl", "x")
FIRST, SECOND = 32, 16
PARTS = 4
GROUP = 2
ORDER, LATE = (0, 2, 1, 3), (0, 3, 1, 2)
VMEM = pl.BlockSpec(memory_space=pltpu.VMEM)
SMEM = pl.BlockSpec(memory_space=pltpu.SMEM)
ANY = pl.BlockSpec(memory_space=pl.ANY)
f32, bf16 = jnp.float32, jnp.bfloat16


def dot(a, b, contract):
    return lax.dot_general(
        a, b, ((contract[:1], contract[1:]), ((), ())), preferred_element_type=f32
    )


def wrap(index):
    return lax.rem(index + PARTS, PARTS)


def pack_vision_body(vision, out, sems):
    half = vision.shape[1] // 4
    width = half // PARTS
    copies = []
    for g in range(PARTS):
        pieces = (
            (g * width, 0, width),
            (half + g * width, width, width),
            (2 * half + 2 * g * width, 2 * width, 2 * width),
        )
        for i, (first, to, size) in enumerate(pieces):
            copies.append(
                pltpu.make_async_copy(
                    vision.at[:, pl.ds(first, size)], out.at[g, :, pl.ds(to, size)], sems.at[g, i]
                )
            )
    for copy in copies:
        copy.start()
    for copy in copies:
        copy.wait()


def pack_text_body(place, queries, cotangent, *refs, shifts):
    outs, sems = refs[-1 - len(shifts) : -1], refs[-1]
    half = queries.shape[2] // 2
    width = half // PARTS
    copies = []
    for n, shift in enumerate(shifts):
        g = wrap(place[1] + shift)
        first = pl.multiple_of(g * width, width)
        second = pl.multiple_of(half + g * width, width)
        wide = pl.multiple_of(2 * g * width, 2 * width)
        pieces = (
            (queries.at[:, :, pl.ds(first, width)], pl.ds(0, width)),
            (queries.at[:, :, pl.ds(second, width)], pl.ds(width, width)),
            (cotangent.at[:, :, pl.ds(wide, 2 * width)], pl.ds(2 * width, 2 * width)),
        )
        for i, (source, columns) in enumerate(pieces):
            copies.append(
                pltpu.make_async_copy(source, outs[n].at[:, :, columns], sems.at[n, i])
            )
    for copy in copies:
        copy.start()
    for copy in copies:
        copy.wait()


def attend_body(
    place, assignment, counts, lambdas, norm_gain, gate, *refs, heads, head_size, patch
):
    text, vision, payload, grad_vision = (refs[i * PARTS : (i + 1) * PARTS] for i in range(4))
    vision = [vision[LATE.index(k)] for k in range(PARTS)]
    stats, gain, bias, raw_gain = refs[4 * PARTS :]
    zl, x = place[0], place[1]
    seqs, toks = text[0].shape[:2]
    rows = PARTS * toks
    frames = PARTS * PARTS
    keys = frames * patch
    width = heads * head_size
    wide = 2 * head_size
    scale = head_size ** (-0.5)
    first_exp = jnp.exp(jnp.sum(lambdas[0] * lambdas[1], axis=-1, keepdims=True))
    second_exp = jnp.exp(jnp.sum(lambdas[2] * lambdas[3], axis=-1, keepdims=True))
    all_rates = first_exp - second_exp + rate_offset
    head_index = lax.broadcasted_iota(jnp.int32, all_rates.shape, 0)
    shape = (wide, wide)
    diagonal = lax.broadcasted_iota(jnp.int32, shape, 0) == lax.broadcasted_iota(
        jnp.int32, shape, 1
    )
    eye = jnp.where(diagonal, 1.0, 0.0).astype(bf16)
    gain_row = norm_gain[...] * (jnp.tanh(gate[...]) * (1.0 - rate_offset))
    gain[...] = jnp.broadcast_to(
        jnp.sum(jnp.where(diagonal, gain_row, 0.0), axis=1, keepdims=True), gain.shape
    )
    spot = lax.broadcasted_iota(jnp.int32, (keys, rows), 0) // patch
    part = spot // PARTS
    frame = wrap(zl - part) * PARTS + spot - part * PARTS
    for v in range(seqs):
        bias[v] = jnp.where(frame < counts[v], 0.0, -jnp.inf)
    lane = lax.broadcasted_iota(jnp.int32, (1, head_size), 1)
    rate_row = jnp.zeros((1, head_size), f32)

    def map_columns(h, m):
        return pl.ds(m * width + h * head_size, head_size)

    def value_columns(h):
        return pl.ds(2 * width + h * wide, wide)

    def block(columns):
        joined = jnp.concatenate([part[:, :, columns] for part in vision], axis=0)
        return joined.astype(f32).reshape(frames, seqs, patch, -1)

    def of_video(joined, v):
        return joined[:, v].reshape(keys, -1).astype(bf16)

    place_of = [jnp.where(assignment[0, 0] == v, 0, 1) for v in range(seqs)]
    for first in range(0, heads, GROUP):
        chains = [(h, v) for h in range(first, first + GROUP) for v in range(seqs)]
        both = [(h, v, m) for h, v in chains for m in range(2)]
        rates, joined = {}, {}
        for h in range(first, first + GROUP):
            rates[h] = jnp.sum(
                jnp.where(head_index == x * heads + h, all_rates, 0.0), axis=0, keepdims=True
            )
            joined[h] = block(value_columns(h))
            for m in range(2):
                joined[h, m] = block(map_columns(h, m))
        values = {(h, v): of_video(joined[h], v) for h, v in chains}
        key_rows = {(h, v, m): of_video(joined[h, m], v) for h, v, m in both}
        queries = {
            (h, v, m): jnp.concatenate(
                [part[place_of[v], :, map_columns(h, m)] for part in text], axis=0
            )
            for h, v, m in both
        }
        scores = {c: dot(key_rows[c], queries[c], (1, 1)) + bias[c[1]] for c in both}
        shifted = {
            c: jnp.exp((scores[c] - jnp.max(scores[c], axis=0, keepdims=True)) * scale)
            for c in both
        }
        probs = {
            c: shifted[c] * (1.0 / jnp.sum(shifted[c], axis=0, keepdims=True)) for c in both
        }
        rated = {c: rates[c[0]] * probs[(*c, 1)] for c in chains}
        mixed = {c: (probs[(*c, 0)] - rated[c]).astype(bf16) for c in chains}
        attended = {c: dot(values[c], mixed[c], (0, 0)) for c in chains}
        grad_out = {
            (h, v): dot(
                eye,
                jnp.concatenate(
                    [part[place_of[v], :, value_columns(h)] for part in text], axis=0
                ),
                (1, 1),
            )
            for h, v in chains
        }
        inverse_rms = {
            c: lax.rsqrt(jnp.mean(attended[c] * attended[c], axis=0, keepdims=True) + epsilon)
            for c in chains
        }
        grad_attended = {}
        for c in chains:
            normed = attended[c] * inverse_rms[c]
            product = grad_out[c] * normed
            halves = product[:, :head_size] + product[:, head_size:]
            raw_gain[...] = halves if c == (0, 0) else raw_gain[...] + halves
            middle = jnp.mean(product * gain[...], axis=0, keepdims=True)
            grad_attended[c] = (
                inverse_rms[c] * (grad_out[c] * gain[...] - normed * middle)
            ).astype(bf16)
        grad_mixed = {c: dot(values[c], grad_attended[c], (1, 0)) * scale for c in chains}
        grad_values = {c: dot(mixed[c], grad_attended[c], (1, 1)) for c in chains}
        sums = {
            c: jnp.sum(grad_mixed[c[:2]] * probs[c], axis=0, keepdims=True) for c in both
        }
        grad_scores = {}
        for c in chains:
            grad_scores[(*c, 0)] = (probs[(*c, 0)] * (grad_mixed[c] - sums[(*c, 0)])).astype(bf16)
            grad_scores[(*c, 1)] = (rated[c] * (sums[(*c, 1)] - grad_mixed[c])).astype(bf16)
        grad_keys = {c: dot(grad_scores[c], queries[c], (1, 0)) for c in both}
        for h, v, m in both:
            grad_query = dot(grad_scores[h, v, m], key_rows[h, v, m], (0, 0)).astype(bf16)
            own_rows = pl.ds(pl.multiple_of(place_of[v] * toks, toks), toks)
            for i in range(PARTS):
                payload[i][own_rows, map_columns(h, m)] = grad_query[i * toks : (i + 1) * toks]
        for h in range(first, first + GROUP):
            for columns, parts in (
                (map_columns(h, 0), [grad_keys[h, v, 0] for v in range(seqs)]),
                (map_columns(h, 1), [grad_keys[h, v, 1] for v in range(seqs)]),
                (value_columns(h), [grad_values[h, v] for v in range(seqs)]),
            ):
                parts = [p.reshape(frames, patch, -1) for p in parts]
                total = jnp.concatenate(parts, axis=1).astype(bf16)
                for j in range(PARTS):
                    grad_vision[j][:, :, columns] = total[j * PARTS : (j + 1) * PARTS]
            total_rate = sum(sums[h, v, 1] for v in range(seqs))
            own_rate = jnp.sum(total_rate, axis=1, keepdims=True) * (-1.0 / scale)
            rate_row = jnp.where(lane == x * heads + h, own_rate, rate_row)
    gains = jnp.sum(raw_gain[...].T, axis=0, keepdims=True)
    row = lax.broadcasted_iota(jnp.int32, stats.shape[1:], 0)
    tile = jnp.where(row == 0, gains[:, :head_size], 0.0)
    tile = jnp.where(row == 1, gains[:, head_size:], tile)
    tile = jnp.where(row == 2, rate_row, tile)
    for i in range(stats.shape[0]):
        stats[i] = tile


def sum_vision_body(place, after, *refs):
    del after
    parts, outs, total, sems = (
        refs[:PARTS],
        refs[2 * PARTS : 3 * PARTS],
        refs[3 * PARTS],
        refs[3 * PARTS + 1],
    )
    rows, columns = total.shape[1] // 2, total.shape[2]
    copies = []
    for k in range(PARTS):
        x = wrap(place[1] - ORDER[k])
        value = parts[0][x].astype(f32)
        for part in parts[1:]:
            value = value + part[x].astype(f32)
        value = value.astype(bf16)
        total[k, :rows] = value[:, :columns]
        total[k, rows:] = value[:, columns:]
        base = outs[k].shape[0] - 2 * rows
        copies.append(
            pltpu.make_async_copy(total.at[k], outs[k].at[pl.ds(base, 2 * rows)], sems.at[k])
        )
        copies[k].start()
    for copy in copies:
        copy.wait()


def spread_sum_body(tiles, after, out):
    del after
    total = jnp.sum(tiles[...], axis=0)
    for i in range(out.shape[0]):
        out[i] = total


def finish_body(place, tiles, lambdas, norm_gain, gate, *refs):
    parts, grad_queries, grad_vision, grad_lambdas, grad_gain, grad_gate = (
        refs[:PARTS],
        *refs[PARTS:],
    )
    text_rows, rows = grad_queries.shape[0], grad_vision.shape[0]
    half = grad_queries.shape[1] // 2
    width = half // PARTS
    for k in range(PARTS):
        g = wrap(place[1] + ORDER[k])
        first = pl.multiple_of(g * width, width)
        second = pl.multiple_of(half + g * width, width)
        wide = pl.multiple_of(2 * half + 2 * g * width, 2 * width)
        own = parts[k]
        grad_queries[:, pl.ds(first, width)] = own[:text_rows, :width]
        grad_queries[:, pl.ds(second, width)] = own[:text_rows, width:]
        grad_vision[:, pl.ds(first, width)] = own[text_rows : text_rows + rows, :width]
        grad_vision[:, pl.ds(second, width)] = own[text_rows : text_rows + rows, width:]
        grad_vision[:, pl.ds(wide, 2 * width)] = own[text_rows + rows :, :]
    total = jnp.sum(tiles[...], axis=0)
    head_count, head_size = lambdas.shape[1:]
    gate_tanh = jnp.tanh(gate[...])
    grad_gain[...] = total[:2] * (gate_tanh * (1.0 - rate_offset))
    weighed = jnp.sum(total[:2] * norm_gain[...], axis=-1, keepdims=True)
    grad_gate[...] = (
        jnp.sum(weighed, axis=0, keepdims=True)
        * (1.0 - rate_offset)
        * (1.0 - gate_tanh * gate_tanh)
    )
    shape = (head_count, head_size)
    own = lax.broadcasted_iota(jnp.int32, shape, 0) == lax.broadcasted_iota(jnp.int32, shape, 1)
    grad_rate = jnp.sum(jnp.where(own, total[2:3], 0.0), axis=-1, keepdims=True)
    first_exp = jnp.exp(jnp.sum(lambdas[0] * lambdas[1], axis=-1, keepdims=True))
    second_exp = jnp.exp(jnp.sum(lambdas[2] * lambdas[3], axis=-1, keepdims=True))
    weight_one, weight_two = grad_rate * first_exp, grad_rate * second_exp
    grad_lambdas[0] = weight_one * lambdas[1]
    grad_lambdas[1] = weight_one * lambdas[0]
    grad_lambdas[2] = -weight_two * lambdas[3]
    grad_lambdas[3] = -weight_two * lambdas[2]


def shift_all(parts, axis, order, way):
    return [
        lax.ppermute(part, axis, [(i, (i + way * k) % PARTS) for i in range(PARTS)]) if k else part
        for part, k in zip(parts, order)
    ]


def kernel(body, out_shape, in_specs, out_specs, limit=20 * 2**20, **more):
    return pl.pallas_call(
        body,
        out_shape=out_shape,
        in_specs=in_specs,
        out_specs=out_specs,
        compiler_params=pltpu.CompilerParams(vmem_limit_bytes=limit),
        **more,
    )


def shaped(shape, dtype=bf16):
    return jax.ShapeDtypeStruct(shape, dtype)


def exchange(value, axes):
    return lax.all_to_all(value, axes, 0, 0, tiled=True)


def attend_call(place, assignment, counts, lambdas, norm_gain, gate, text, vision):
    seqs, toks, columns = text[0].shape
    head_count, head_size = lambdas.shape[1:]
    heads = head_count // PARTS
    slab = vision[0].shape
    rows = slab[1]
    return kernel(
        functools.partial(
            attend_body, heads=heads, head_size=head_size, patch=rows // seqs
        ),
        [shaped((seqs * toks + 2 * rows, columns // 2))] * PARTS
        + [shaped(slab)] * PARTS
        + [shaped((FIRST, 4, head_size), f32)],
        [SMEM] * 3 + [VMEM] * (3 + 2 * PARTS),
        [VMEM] * (2 * PARTS + 1),
        scratch_shapes=[
            pltpu.VMEM((2 * head_size, PARTS * toks), f32),
            pltpu.VMEM((seqs, PARTS * PARTS * rows // seqs, PARTS * toks), f32),
            pltpu.VMEM((2 * head_size, head_size), f32),
        ],
    )(place, assignment, counts, lambdas, norm_gain, gate, *text, *vision)


def shards(queries, vision, cotangent, assignment, frame_counts, lambdas, norm_gain, gate_logit):
    seqs, toks, text_columns = queries.shape
    frames_dev, patch, vision_columns = vision.shape[1:]
    head_count, head_size = lambdas.shape[1:]
    heads = head_count // PARTS
    rows = seqs * frames_dev * patch
    place = jnp.stack([lax.axis_index("zl"), lax.axis_index("x")]).astype(jnp.int32)
    slab = shaped((PARTS, rows, vision_columns // PARTS))
    gain_rows = norm_gain.reshape(-1, head_size)
    gate = gate_logit.reshape(1, 1)

    sent_vision = kernel(
        pack_vision_body,
        slab,
        [ANY],
        ANY,
        limit=62 * 2**20,
        scratch_shapes=[pltpu.SemaphoreType.DMA((PARTS, 3))],
    )(vision.reshape(rows, vision_columns))
    row_vision = exchange(sent_vision, "x")
    sent_text = {}
    early = (row_vision, norm_gain.reshape(1, -1), assignment, frame_counts)
    for held, others in (((2,), ()), ((0, 1, 3), early)):
        packed = kernel(
            functools.partial(pack_text_body, shifts=held),
            [shaped((seqs, toks, 2 * text_columns // PARTS))] * len(held),
            [SMEM, ANY, ANY] + [ANY, VMEM, SMEM, SMEM][: len(others)],
            [ANY] * len(held),
            scratch_shapes=[pltpu.SemaphoreType.DMA((len(held), 3))],
        )(place, queries, cotangent, *others)
        sent_text.update(zip(held, packed))
    held_text = shift_all([sent_text[k] for k in ORDER], "x", ORDER, 1)
    held_vision = shift_all([row_vision] * PARTS, "zl", LATE, 1)

    grads = attend_call(
        place,
        assignment,
        frame_counts,
        lambdas,
        norm_gain.reshape(1, -1),
        gate,
        held_text,
        held_vision,
    )
    payload, grad_vision, stats = grads[:PARTS], grads[PARTS : 2 * PARTS], grads[2 * PARTS]

    back_vision = shift_all(grad_vision, "zl", range(PARTS), -1)
    stats = exchange(stats, ("y", "x"))
    payload = kernel(
        sum_vision_body,
        [shaped(payload[0].shape)] * PARTS,
        [SMEM, ANY] + [VMEM] * PARTS + [ANY] * PARTS,
        [ANY] * PARTS,
        scratch_shapes=[
            pltpu.VMEM((PARTS, 2 * rows, text_columns // PARTS), bf16),
            pltpu.SemaphoreType.DMA((PARTS,)),
        ],
        input_output_aliases={2 + PARTS + k: k for k in range(PARTS)},
    )(place, stats, *back_vision, *payload)
    back = shift_all(payload, "x", ORDER, -1)
    stats = kernel(spread_sum_body, shaped((SECOND, 4, head_size), f32), [VMEM, ANY], VMEM)(
        stats, payload[0]
    )
    stats = exchange(stats, ("zh", "core", "zl"))
    grad_queries, grad_vision, grad_lambdas, grad_gain, grad_gate = kernel(
        finish_body,
        [
            shaped((seqs * toks, text_columns)),
            shaped((rows, vision_columns)),
            shaped(lambdas.shape, f32),
            shaped(gain_rows.shape, f32),
            shaped((1, 1), f32),
        ],
        [SMEM] + [VMEM] * (4 + PARTS),
        [VMEM] * 5,
    )(place, stats, lambdas, gain_rows, gate, *back)
    return (
        grad_queries.reshape(queries.shape),
        grad_vision.reshape(vision.shape),
        grad_lambdas,
        grad_gain.reshape(norm_gain.shape),
        grad_gate.reshape(gate_logit.shape),
    )


def solution(mesh):
    fine = Mesh(mesh.devices.reshape(8, 2, 2, PARTS, PARTS), DP + IMAGE)
    placed = (
        P(DP, IMAGE, None),
        P(DP, IMAGE, None, None),
        P(DP, IMAGE, None),
        P(DP, None),
        P(DP),
        P(),
        P(),
        P(),
    )
    return jax.shard_map(
        shards,
        mesh=fine,
        in_specs=placed,
        out_specs=(P(DP, IMAGE, None), P(DP, IMAGE, None, None), P(), P(), P()),
        check_vma=False,
    )
```

```python
import functools

import jax
import jax.numpy as jnp
from jax import lax
from jax.experimental import pallas as pl
from jax.experimental.pallas import tpu as pltpu
from jax.sharding import Mesh, PartitionSpec as P

rate_offset = 0.8
epsilon = 1e-05
DP = ("y", "zh", "core")
IMAGE = ("zl", "x")
FIRST, SECOND = 32, 16
PARTS = 4
GROUP = 2
ORDER, LATE = (0, 2, 1, 3), (0, 3, 1, 2)
VMEM = pl.BlockSpec(memory_space=pltpu.VMEM)
SMEM = pl.BlockSpec(memory_space=pltpu.SMEM)
ANY = pl.BlockSpec(memory_space=pl.ANY)
LIMIT = pltpu.CompilerParams(vmem_limit_bytes=32 * 2**20)
f32, bf16 = jnp.float32, jnp.bfloat16


def dot(a, b, contract):
    return lax.dot_general(
        a, b, ((contract[:1], contract[1:]), ((), ())), preferred_element_type=f32
    )


def wrap(index):
    return lax.rem(index + PARTS, PARTS)


def pack_vision_body(vision, out):
    half = vision.shape[1] // 4
    width = half // PARTS
    for g in range(PARTS):
        out[g, :, :width] = vision[:, g * width : (g + 1) * width]
        out[g, :, width : 2 * width] = vision[:, half + g * width : half + (g + 1) * width]
        out[g, :, 2 * width :] = vision[
            :, 2 * half + 2 * g * width : 2 * half + 2 * (g + 1) * width
        ]


def pack_text_body(place, queries, cotangent, *refs, shifts):
    outs, sems = refs[-1 - len(shifts) : -1], refs[-1]
    half = queries.shape[2] // 2
    width = half // PARTS
    copies = []
    for n, shift in enumerate(shifts):
        g = wrap(place[1] + shift)
        first = pl.multiple_of(g * width, width)
        second = pl.multiple_of(half + g * width, width)
        wide = pl.multiple_of(2 * g * width, 2 * width)
        pieces = (
            (queries.at[:, :, pl.ds(first, width)], pl.ds(0, width)),
            (queries.at[:, :, pl.ds(second, width)], pl.ds(width, width)),
            (cotangent.at[:, :, pl.ds(wide, 2 * width)], pl.ds(2 * width, 2 * width)),
        )
        for i, (source, columns) in enumerate(pieces):
            copies.append(
                pltpu.make_async_copy(source, outs[n].at[:, :, columns], sems.at[n, i])
            )
    for copy in copies:
        copy.start()
    for copy in copies:
        copy.wait()


def attend_body(
    place, assignment, counts, lambdas, norm_gain, gate, *refs, heads, head_size, patch
):
    text, vision, payload, grad_vision = (refs[i * PARTS : (i + 1) * PARTS] for i in range(4))
    vision = [vision[LATE.index(k)] for k in range(PARTS)]
    stats, gain, bias, raw_gain = refs[4 * PARTS :]
    zl, x = place[0], place[1]
    seqs, toks = text[0].shape[:2]
    rows = PARTS * toks
    frames = PARTS * PARTS
    keys = frames * patch
    width = heads * head_size
    wide = 2 * head_size
    scale = head_size ** (-0.5)
    first_exp = jnp.exp(jnp.sum(lambdas[0] * lambdas[1], axis=-1, keepdims=True))
    second_exp = jnp.exp(jnp.sum(lambdas[2] * lambdas[3], axis=-1, keepdims=True))
    all_rates = first_exp - second_exp + rate_offset
    head_index = lax.broadcasted_iota(jnp.int32, all_rates.shape, 0)
    shape = (wide, wide)
    diagonal = lax.broadcasted_iota(jnp.int32, shape, 0) == lax.broadcasted_iota(
        jnp.int32, shape, 1
    )
    eye = jnp.where(diagonal, 1.0, 0.0).astype(bf16)
    gain_row = norm_gain[...] * (jnp.tanh(gate[...]) * (1.0 - rate_offset))
    gain[...] = jnp.broadcast_to(
        jnp.sum(jnp.where(diagonal, gain_row, 0.0), axis=1, keepdims=True), gain.shape
    )
    spot = lax.broadcasted_iota(jnp.int32, (keys, rows), 0) // patch
    part = spot // PARTS
    frame = wrap(zl - part) * PARTS + spot - part * PARTS
    for v in range(seqs):
        bias[v] = jnp.where(frame < counts[v], 0.0, -jnp.inf)
    lane = lax.broadcasted_iota(jnp.int32, (1, head_size), 1)
    rate_row = jnp.zeros((1, head_size), f32)

    def map_columns(h, m):
        return pl.ds(m * width + h * head_size, head_size)

    def value_columns(h):
        return pl.ds(2 * width + h * wide, wide)

    def block(columns):
        joined = jnp.concatenate([part[:, :, columns] for part in vision], axis=0)
        return joined.astype(f32).reshape(frames, seqs, patch, -1)

    def of_video(joined, v):
        return joined[:, v].reshape(keys, -1).astype(bf16)

    place_of = [jnp.where(assignment[0, 0] == v, 0, 1) for v in range(seqs)]
    for first in range(0, heads, GROUP):
        chains = [(h, v) for h in range(first, first + GROUP) for v in range(seqs)]
        both = [(h, v, m) for h, v in chains for m in range(2)]
        rates, joined = {}, {}
        for h in range(first, first + GROUP):
            rates[h] = jnp.sum(
                jnp.where(head_index == x * heads + h, all_rates, 0.0), axis=0, keepdims=True
            )
            joined[h] = block(value_columns(h))
            for m in range(2):
                joined[h, m] = block(map_columns(h, m))
        values = {(h, v): of_video(joined[h], v) for h, v in chains}
        key_rows = {(h, v, m): of_video(joined[h, m], v) for h, v, m in both}
        queries = {
            (h, v, m): jnp.concatenate(
                [part[place_of[v], :, map_columns(h, m)] for part in text], axis=0
            )
            for h, v, m in both
        }
        scores = {c: dot(key_rows[c], queries[c], (1, 1)) + bias[c[1]] for c in both}
        shifted = {
            c: jnp.exp((scores[c] - jnp.max(scores[c], axis=0, keepdims=True)) * scale)
            for c in both
        }
        probs = {
            c: shifted[c] * (1.0 / jnp.sum(shifted[c], axis=0, keepdims=True)) for c in both
        }
        rated = {c: rates[c[0]] * probs[(*c, 1)] for c in chains}
        mixed = {c: (probs[(*c, 0)] - rated[c]).astype(bf16) for c in chains}
        attended = {c: dot(values[c], mixed[c], (0, 0)) for c in chains}
        grad_out = {
            (h, v): dot(
                eye,
                jnp.concatenate(
                    [part[place_of[v], :, value_columns(h)] for part in text], axis=0
                ),
                (1, 1),
            )
            for h, v in chains
        }
        inverse_rms = {
            c: lax.rsqrt(jnp.mean(attended[c] * attended[c], axis=0, keepdims=True) + epsilon)
            for c in chains
        }
        grad_attended = {}
        for c in chains:
            normed = attended[c] * inverse_rms[c]
            product = grad_out[c] * normed
            halves = product[:, :head_size] + product[:, head_size:]
            raw_gain[...] = halves if c == (0, 0) else raw_gain[...] + halves
            middle = jnp.mean(product * gain[...], axis=0, keepdims=True)
            grad_attended[c] = (
                inverse_rms[c] * (grad_out[c] * gain[...] - normed * middle)
            ).astype(bf16)
        grad_mixed = {c: dot(values[c], grad_attended[c], (1, 0)) * scale for c in chains}
        grad_values = {c: dot(mixed[c], grad_attended[c], (1, 1)) for c in chains}
        sums = {
            c: jnp.sum(grad_mixed[c[:2]] * probs[c], axis=0, keepdims=True) for c in both
        }
        grad_scores = {}
        for c in chains:
            grad_scores[(*c, 0)] = (probs[(*c, 0)] * (grad_mixed[c] - sums[(*c, 0)])).astype(bf16)
            grad_scores[(*c, 1)] = (rated[c] * (sums[(*c, 1)] - grad_mixed[c])).astype(bf16)
        grad_keys = {c: dot(grad_scores[c], queries[c], (1, 0)) for c in both}
        for h, v, m in both:
            grad_query = dot(grad_scores[h, v, m], key_rows[h, v, m], (0, 0)).astype(bf16)
            own_rows = pl.ds(pl.multiple_of(place_of[v] * toks, toks), toks)
            for i in range(PARTS):
                payload[i][own_rows, map_columns(h, m)] = grad_query[i * toks : (i + 1) * toks]
        for h in range(first, first + GROUP):
            for columns, parts in (
                (map_columns(h, 0), [grad_keys[h, v, 0] for v in range(seqs)]),
                (map_columns(h, 1), [grad_keys[h, v, 1] for v in range(seqs)]),
                (value_columns(h), [grad_values[h, v] for v in range(seqs)]),
            ):
                parts = [p.reshape(frames, patch, -1) for p in parts]
                total = jnp.concatenate(parts, axis=1).astype(bf16)
                for j in range(PARTS):
                    grad_vision[j][:, :, columns] = total[j * PARTS : (j + 1) * PARTS]
            total_rate = sum(sums[h, v, 1] for v in range(seqs))
            own_rate = jnp.sum(total_rate, axis=1, keepdims=True) * (-1.0 / scale)
            rate_row = jnp.where(lane == x * heads + h, own_rate, rate_row)
    gains = jnp.sum(raw_gain[...].T, axis=0, keepdims=True)
    row = lax.broadcasted_iota(jnp.int32, stats.shape[1:], 0)
    tile = jnp.where(row == 0, gains[:, :head_size], 0.0)
    tile = jnp.where(row == 1, gains[:, head_size:], tile)
    tile = jnp.where(row == 2, rate_row, tile)
    for i in range(stats.shape[0]):
        stats[i] = tile


def sum_vision_body(place, after, *refs):
    del after
    parts, outs, total, sems = (
        refs[:PARTS],
        refs[2 * PARTS : 3 * PARTS],
        refs[3 * PARTS],
        refs[3 * PARTS + 1],
    )
    rows, columns = total.shape[1] // 2, total.shape[2]
    copies = []
    for k in range(PARTS):
        x = wrap(place[1] - ORDER[k])
        value = parts[0][x].astype(f32)
        for part in parts[1:]:
            value = value + part[x].astype(f32)
        value = value.astype(bf16)
        total[k, :rows] = value[:, :columns]
        total[k, rows:] = value[:, columns:]
        base = outs[k].shape[0] - 2 * rows
        copies.append(
            pltpu.make_async_copy(total.at[k], outs[k].at[pl.ds(base, 2 * rows)], sems.at[k])
        )
        copies[k].start()
    for copy in copies:
        copy.wait()


def spread_sum_body(tiles, after, out):
    del after
    total = jnp.sum(tiles[...], axis=0)
    for i in range(out.shape[0]):
        out[i] = total


def finish_body(place, tiles, lambdas, norm_gain, gate, *refs):
    parts, grad_queries, grad_vision, grad_lambdas, grad_gain, grad_gate = (
        refs[:PARTS],
        *refs[PARTS:],
    )
    text_rows, rows = grad_queries.shape[0], grad_vision.shape[0]
    half = grad_queries.shape[1] // 2
    width = half // PARTS
    for k in range(PARTS):
        g = wrap(place[1] + ORDER[k])
        first = pl.multiple_of(g * width, width)
        second = pl.multiple_of(half + g * width, width)
        wide = pl.multiple_of(2 * half + 2 * g * width, 2 * width)
        own = parts[k]
        grad_queries[:, pl.ds(first, width)] = own[:text_rows, :width]
        grad_queries[:, pl.ds(second, width)] = own[:text_rows, width:]
        grad_vision[:, pl.ds(first, width)] = own[text_rows : text_rows + rows, :width]
        grad_vision[:, pl.ds(second, width)] = own[text_rows : text_rows + rows, width:]
        grad_vision[:, pl.ds(wide, 2 * width)] = own[text_rows + rows :, :]
    total = jnp.sum(tiles[...], axis=0)
    head_count, head_size = lambdas.shape[1:]
    gate_tanh = jnp.tanh(gate[...])
    grad_gain[...] = total[:2] * (gate_tanh * (1.0 - rate_offset))
    weighed = jnp.sum(total[:2] * norm_gain[...], axis=-1, keepdims=True)
    grad_gate[...] = (
        jnp.sum(weighed, axis=0, keepdims=True)
        * (1.0 - rate_offset)
        * (1.0 - gate_tanh * gate_tanh)
    )
    shape = (head_count, head_size)
    own = lax.broadcasted_iota(jnp.int32, shape, 0) == lax.broadcasted_iota(jnp.int32, shape, 1)
    grad_rate = jnp.sum(jnp.where(own, total[2:3], 0.0), axis=-1, keepdims=True)
    first_exp = jnp.exp(jnp.sum(lambdas[0] * lambdas[1], axis=-1, keepdims=True))
    second_exp = jnp.exp(jnp.sum(lambdas[2] * lambdas[3], axis=-1, keepdims=True))
    weight_one, weight_two = grad_rate * first_exp, grad_rate * second_exp
    grad_lambdas[0] = weight_one * lambdas[1]
    grad_lambdas[1] = weight_one * lambdas[0]
    grad_lambdas[2] = -weight_two * lambdas[3]
    grad_lambdas[3] = -weight_two * lambdas[2]


def shift_all(parts, axis, order, way):
    return [
        lax.ppermute(part, axis, [(i, (i + way * k) % PARTS) for i in range(PARTS)]) if k else part
        for part, k in zip(parts, order)
    ]


def kernel(body, out_shape, in_specs, out_specs, **more):
    return pl.pallas_call(
        body,
        out_shape=out_shape,
        in_specs=in_specs,
        out_specs=out_specs,
        compiler_params=LIMIT,
        **more,
    )


def shaped(shape, dtype=bf16):
    return jax.ShapeDtypeStruct(shape, dtype)


def exchange(value, axes):
    return lax.all_to_all(value, axes, 0, 0, tiled=True)


def attend_call(place, assignment, counts, lambdas, norm_gain, gate, text, vision):
    seqs, toks, columns = text[0].shape
    head_count, head_size = lambdas.shape[1:]
    heads = head_count // PARTS
    slab = vision[0].shape
    rows = slab[1]
    return kernel(
        functools.partial(
            attend_body, heads=heads, head_size=head_size, patch=rows // seqs
        ),
        [shaped((seqs * toks + 2 * rows, columns // 2))] * PARTS
        + [shaped(slab)] * PARTS
        + [shaped((FIRST, 4, head_size), f32)],
        [SMEM] * 3 + [VMEM] * (3 + 2 * PARTS),
        [VMEM] * (2 * PARTS + 1),
        scratch_shapes=[
            pltpu.VMEM((2 * head_size, PARTS * toks), f32),
            pltpu.VMEM((seqs, PARTS * PARTS * rows // seqs, PARTS * toks), f32),
            pltpu.VMEM((2 * head_size, head_size), f32),
        ],
    )(place, assignment, counts, lambdas, norm_gain, gate, *text, *vision)


def shards(queries, vision, cotangent, assignment, frame_counts, lambdas, norm_gain, gate_logit):
    seqs, toks, text_columns = queries.shape
    frames_dev, patch, vision_columns = vision.shape[1:]
    head_count, head_size = lambdas.shape[1:]
    heads = head_count // PARTS
    rows = seqs * frames_dev * patch
    place = jnp.stack([lax.axis_index("zl"), lax.axis_index("x")]).astype(jnp.int32)
    slab = shaped((PARTS, rows, vision_columns // PARTS))
    gain_rows = norm_gain.reshape(-1, head_size)
    gate = gate_logit.reshape(1, 1)

    sent_vision = kernel(pack_vision_body, slab, [VMEM], VMEM)(
        vision.reshape(rows, vision_columns)
    )
    row_vision = exchange(sent_vision, "x")
    sent_text = {}
    early = (row_vision, norm_gain.reshape(1, -1), assignment, frame_counts)
    for held, others in (((2,), ()), ((0, 1, 3), early)):
        packed = kernel(
            functools.partial(pack_text_body, shifts=held),
            [shaped((seqs, toks, 2 * text_columns // PARTS))] * len(held),
            [SMEM, ANY, ANY] + [ANY, VMEM, SMEM, SMEM][: len(others)],
            [ANY] * len(held),
            scratch_shapes=[pltpu.SemaphoreType.DMA((len(held), 3))],
        )(place, queries, cotangent, *others)
        sent_text.update(zip(held, packed))
    held_text = shift_all([sent_text[k] for k in ORDER], "x", ORDER, 1)
    held_vision = shift_all([row_vision] * PARTS, "zl", LATE, 1)

    grads = attend_call(
        place,
        assignment,
        frame_counts,
        lambdas,
        norm_gain.reshape(1, -1),
        gate,
        held_text,
        held_vision,
    )
    payload, grad_vision, stats = grads[:PARTS], grads[PARTS : 2 * PARTS], grads[2 * PARTS]

    back_vision = shift_all(grad_vision, "zl", range(PARTS), -1)
    stats = exchange(stats, ("y", "x"))
    payload = kernel(
        sum_vision_body,
        [shaped(payload[0].shape)] * PARTS,
        [SMEM, ANY] + [VMEM] * PARTS + [ANY] * PARTS,
        [ANY] * PARTS,
        scratch_shapes=[
            pltpu.VMEM((PARTS, 2 * rows, text_columns // PARTS), bf16),
            pltpu.SemaphoreType.DMA((PARTS,)),
        ],
        input_output_aliases={2 + PARTS + k: k for k in range(PARTS)},
    )(place, stats, *back_vision, *payload)
    back = shift_all(payload, "x", ORDER, -1)
    stats = kernel(spread_sum_body, shaped((SECOND, 4, head_size), f32), [VMEM, ANY], VMEM)(
        stats, payload[0]
    )
    stats = exchange(stats, ("zh", "core", "zl"))
    grad_queries, grad_vision, grad_lambdas, grad_gain, grad_gate = kernel(
        finish_body,
        [
            shaped((seqs * toks, text_columns)),
            shaped((rows, vision_columns)),
            shaped(lambdas.shape, f32),
            shaped(gain_rows.shape, f32),
            shaped((1, 1), f32),
        ],
        [SMEM] + [VMEM] * (4 + PARTS),
        [VMEM] * 5,
    )(place, stats, lambdas, gain_rows, gate, *back)
    return (
        grad_queries.reshape(queries.shape),
        grad_vision.reshape(vision.shape),
        grad_lambdas,
        grad_gain.reshape(norm_gain.shape),
        grad_gate.reshape(gate_logit.shape),
    )


def solution(mesh):
    fine = Mesh(mesh.devices.reshape(8, 2, 2, PARTS, PARTS), DP + IMAGE)
    placed = (
        P(DP, IMAGE, None),
        P(DP, IMAGE, None, None),
        P(DP, IMAGE, None),
        P(DP, None),
        P(DP),
        P(),
        P(),
        P(),
    )
    return jax.shard_map(
        shards,
        mesh=fine,
        in_specs=placed,
        out_specs=(P(DP, IMAGE, None), P(DP, IMAGE, None, None), P(), P(), P()),
        check_vma=False,
    )
```

```python
import functools

import jax
import jax.numpy as jnp
from jax import lax
from jax.experimental import pallas as pl
from jax.experimental.pallas import tpu as pltpu
from jax.sharding import Mesh, PartitionSpec as P

rate_offset = 0.8
epsilon = 1e-05
DP = ("y", "zh", "core")
IMAGE = ("zl", "x")
FIRST, SECOND = 32, 16
PARTS = 4
GROUP = 2
ORDER, LATE, BACK = (0, 2, 1, 3), (0, 3, 1, 2), (0, 1, 3, 2)
VMEM = pl.BlockSpec(memory_space=pltpu.VMEM)
SMEM = pl.BlockSpec(memory_space=pltpu.SMEM)
ANY = pl.BlockSpec(memory_space=pl.ANY)
LIMIT = pltpu.CompilerParams(vmem_limit_bytes=32 * 2**20)
f32, bf16 = jnp.float32, jnp.bfloat16


def dot(a, b, contract):
    return lax.dot_general(
        a, b, ((contract[:1], contract[1:]), ((), ())), preferred_element_type=f32
    )


def wrap(index):
    return lax.rem(index + PARTS, PARTS)


def pack_vision_body(vision, out):
    half = vision.shape[1] // 4
    width = half // PARTS
    for g in range(PARTS):
        out[g, :, :width] = vision[:, g * width : (g + 1) * width]
        out[g, :, width : 2 * width] = vision[:, half + g * width : half + (g + 1) * width]
        out[g, :, 2 * width :] = vision[
            :, 2 * half + 2 * g * width : 2 * half + 2 * (g + 1) * width
        ]


def pack_text_body(place, queries, cotangent, *refs, shifts):
    outs, sems = refs[-1 - len(shifts) : -1], refs[-1]
    half = queries.shape[2] // 2
    width = half // PARTS
    copies = []
    for n, shift in enumerate(shifts):
        g = wrap(place[1] + shift)
        first = pl.multiple_of(g * width, width)
        second = pl.multiple_of(half + g * width, width)
        wide = pl.multiple_of(2 * g * width, 2 * width)
        pieces = (
            (queries.at[:, :, pl.ds(first, width)], pl.ds(0, width)),
            (queries.at[:, :, pl.ds(second, width)], pl.ds(width, width)),
            (cotangent.at[:, :, pl.ds(wide, 2 * width)], pl.ds(2 * width, 2 * width)),
        )
        for i, (source, columns) in enumerate(pieces):
            copies.append(
                pltpu.make_async_copy(source, outs[n].at[:, :, columns], sems.at[n, i])
            )
    for copy in copies:
        copy.start()
    for copy in copies:
        copy.wait()


def attend_body(
    place, assignment, counts, lambdas, norm_gain, gate, *refs, heads, head_size, patch
):
    text, vision, grad_text, grad_vision = (refs[i * PARTS : (i + 1) * PARTS] for i in range(4))
    vision = [vision[LATE.index(k)] for k in range(PARTS)]
    stats, gain, bias, raw_gain = refs[4 * PARTS :]
    zl, x = place[0], place[1]
    seqs, toks = text[0].shape[:2]
    rows = PARTS * toks
    frames = PARTS * PARTS
    keys = frames * patch
    width = heads * head_size
    wide = 2 * head_size
    scale = head_size ** (-0.5)
    first_exp = jnp.exp(jnp.sum(lambdas[0] * lambdas[1], axis=-1, keepdims=True))
    second_exp = jnp.exp(jnp.sum(lambdas[2] * lambdas[3], axis=-1, keepdims=True))
    all_rates = first_exp - second_exp + rate_offset
    head_index = lax.broadcasted_iota(jnp.int32, all_rates.shape, 0)
    shape = (wide, wide)
    diagonal = lax.broadcasted_iota(jnp.int32, shape, 0) == lax.broadcasted_iota(
        jnp.int32, shape, 1
    )
    eye = jnp.where(diagonal, 1.0, 0.0).astype(bf16)
    gain_row = norm_gain[...] * (jnp.tanh(gate[...]) * (1.0 - rate_offset))
    gain[...] = jnp.broadcast_to(
        jnp.sum(jnp.where(diagonal, gain_row, 0.0), axis=1, keepdims=True), gain.shape
    )
    spot = lax.broadcasted_iota(jnp.int32, (keys, rows), 0) // patch
    part = spot // PARTS
    frame = wrap(zl - part) * PARTS + spot - part * PARTS
    for v in range(seqs):
        bias[v] = jnp.where(frame < counts[v], 0.0, -jnp.inf)
    lane = lax.broadcasted_iota(jnp.int32, (1, head_size), 1)
    rate_row = jnp.zeros((1, head_size), f32)

    def map_columns(h, m):
        return pl.ds(m * width + h * head_size, head_size)

    def value_columns(h):
        return pl.ds(2 * width + h * wide, wide)

    def block(columns):
        joined = jnp.concatenate([part[:, :, columns] for part in vision], axis=0)
        return joined.astype(f32).reshape(frames, seqs, patch, -1)

    def of_video(joined, v):
        return joined[:, v].reshape(keys, -1).astype(bf16)

    place_of = [jnp.where(assignment[0, 0] == v, 0, 1) for v in range(seqs)]
    for first in range(0, heads, GROUP):
        chains = [(h, v) for h in range(first, first + GROUP) for v in range(seqs)]
        both = [(h, v, m) for h, v in chains for m in range(2)]
        rates, joined = {}, {}
        for h in range(first, first + GROUP):
            rates[h] = jnp.sum(
                jnp.where(head_index == x * heads + h, all_rates, 0.0), axis=0, keepdims=True
            )
            joined[h] = block(value_columns(h))
            for m in range(2):
                joined[h, m] = block(map_columns(h, m))
        values = {(h, v): of_video(joined[h], v) for h, v in chains}
        key_rows = {(h, v, m): of_video(joined[h, m], v) for h, v, m in both}
        queries = {
            (h, v, m): jnp.concatenate(
                [part[place_of[v], :, map_columns(h, m)] for part in text], axis=0
            )
            for h, v, m in both
        }
        scores = {c: dot(key_rows[c], queries[c], (1, 1)) + bias[c[1]] for c in both}
        shifted = {
            c: jnp.exp((scores[c] - jnp.max(scores[c], axis=0, keepdims=True)) * scale)
            for c in both
        }
        probs = {
            c: shifted[c] * (1.0 / jnp.sum(shifted[c], axis=0, keepdims=True)) for c in both
        }
        rated = {c: rates[c[0]] * probs[(*c, 1)] for c in chains}
        mixed = {c: (probs[(*c, 0)] - rated[c]).astype(bf16) for c in chains}
        attended = {c: dot(values[c], mixed[c], (0, 0)) for c in chains}
        grad_out = {
            (h, v): dot(
                eye,
                jnp.concatenate(
                    [part[place_of[v], :, value_columns(h)] for part in text], axis=0
                ),
                (1, 1),
            )
            for h, v in chains
        }
        inverse_rms = {
            c: lax.rsqrt(jnp.mean(attended[c] * attended[c], axis=0, keepdims=True) + epsilon)
            for c in chains
        }
        grad_attended = {}
        for c in chains:
            normed = attended[c] * inverse_rms[c]
            product = grad_out[c] * normed
            halves = product[:, :head_size] + product[:, head_size:]
            raw_gain[...] = halves if c == (0, 0) else raw_gain[...] + halves
            middle = jnp.mean(product * gain[...], axis=0, keepdims=True)
            grad_attended[c] = (
                inverse_rms[c] * (grad_out[c] * gain[...] - normed * middle)
            ).astype(bf16)
        grad_mixed = {c: dot(values[c], grad_attended[c], (1, 0)) * scale for c in chains}
        grad_values = {c: dot(mixed[c], grad_attended[c], (1, 1)) for c in chains}
        sums = {
            c: jnp.sum(grad_mixed[c[:2]] * probs[c], axis=0, keepdims=True) for c in both
        }
        grad_scores = {}
        for c in chains:
            grad_scores[(*c, 0)] = (probs[(*c, 0)] * (grad_mixed[c] - sums[(*c, 0)])).astype(bf16)
            grad_scores[(*c, 1)] = (rated[c] * (sums[(*c, 1)] - grad_mixed[c])).astype(bf16)
        grad_keys = {c: dot(grad_scores[c], queries[c], (1, 0)) for c in both}
        for h, v, m in both:
            grad_query = dot(grad_scores[h, v, m], key_rows[h, v, m], (0, 0)).astype(bf16)
            own_rows = pl.ds(pl.multiple_of(place_of[v] * toks, toks), toks)
            for i in range(PARTS):
                grad_text[i][own_rows, map_columns(h, m)] = grad_query[i * toks : (i + 1) * toks]
        for h in range(first, first + GROUP):
            for columns, parts in (
                (map_columns(h, 0), [grad_keys[h, v, 0] for v in range(seqs)]),
                (map_columns(h, 1), [grad_keys[h, v, 1] for v in range(seqs)]),
                (value_columns(h), [grad_values[h, v] for v in range(seqs)]),
            ):
                parts = [p.reshape(frames, patch, -1) for p in parts]
                total = jnp.concatenate(parts, axis=1).astype(bf16)
                for j in range(PARTS):
                    grad_vision[j][:, :, columns] = total[j * PARTS : (j + 1) * PARTS]
            total_rate = sum(sums[h, v, 1] for v in range(seqs))
            own_rate = jnp.sum(total_rate, axis=1, keepdims=True) * (-1.0 / scale)
            rate_row = jnp.where(lane == x * heads + h, own_rate, rate_row)
    gains = jnp.sum(raw_gain[...].T, axis=0, keepdims=True)
    row = lax.broadcasted_iota(jnp.int32, stats.shape[1:], 0)
    tile = jnp.where(row == 0, gains[:, :head_size], 0.0)
    tile = jnp.where(row == 1, gains[:, head_size:], tile)
    tile = jnp.where(row == 2, rate_row, tile)
    for i in range(stats.shape[0]):
        stats[i] = tile


def sum_vision_body(place, after, *refs):
    del after
    parts, text, outs = (refs[i * PARTS : (i + 1) * PARTS] for i in range(3))
    for k, out in enumerate(outs):
        x = wrap(place[1] - ORDER[k])
        value = parts[0][x].astype(f32)
        for part in parts[1:]:
            value = value + part[x].astype(f32)
        value = value.astype(bf16)
        text_rows, columns = text[k].shape
        rows = value.shape[0]
        out[:text_rows] = text[k][...]
        out[text_rows : text_rows + rows] = value[:, :columns]
        out[text_rows + rows :] = value[:, columns:]


def spread_sum_body(tiles, after, out):
    del after
    total = jnp.sum(tiles[...], axis=0)
    for i in range(out.shape[0]):
        out[i] = total


def finish_body(place, tiles, lambdas, norm_gain, gate, *refs):
    parts, grad_queries, grad_vision, grad_lambdas, grad_gain, grad_gate = (
        refs[:PARTS],
        *refs[PARTS:],
    )
    text_rows, rows = grad_queries.shape[0], grad_vision.shape[0]
    half = grad_queries.shape[1] // 2
    width = half // PARTS
    for k in range(PARTS):
        g = wrap(place[1] + ORDER[k])
        first = pl.multiple_of(g * width, width)
        second = pl.multiple_of(half + g * width, width)
        wide = pl.multiple_of(2 * half + 2 * g * width, 2 * width)
        own = parts[k]
        grad_queries[:, pl.ds(first, width)] = own[:text_rows, :width]
        grad_queries[:, pl.ds(second, width)] = own[:text_rows, width:]
        grad_vision[:, pl.ds(first, width)] = own[text_rows : text_rows + rows, :width]
        grad_vision[:, pl.ds(second, width)] = own[text_rows : text_rows + rows, width:]
        grad_vision[:, pl.ds(wide, 2 * width)] = own[text_rows + rows :, :]
    total = jnp.sum(tiles[...], axis=0)
    head_count, head_size = lambdas.shape[1:]
    gate_tanh = jnp.tanh(gate[...])
    grad_gain[...] = total[:2] * (gate_tanh * (1.0 - rate_offset))
    weighed = jnp.sum(total[:2] * norm_gain[...], axis=-1, keepdims=True)
    grad_gate[...] = (
        jnp.sum(weighed, axis=0, keepdims=True)
        * (1.0 - rate_offset)
        * (1.0 - gate_tanh * gate_tanh)
    )
    shape = (head_count, head_size)
    own = lax.broadcasted_iota(jnp.int32, shape, 0) == lax.broadcasted_iota(jnp.int32, shape, 1)
    grad_rate = jnp.sum(jnp.where(own, total[2:3], 0.0), axis=-1, keepdims=True)
    first_exp = jnp.exp(jnp.sum(lambdas[0] * lambdas[1], axis=-1, keepdims=True))
    second_exp = jnp.exp(jnp.sum(lambdas[2] * lambdas[3], axis=-1, keepdims=True))
    weight_one, weight_two = grad_rate * first_exp, grad_rate * second_exp
    grad_lambdas[0] = weight_one * lambdas[1]
    grad_lambdas[1] = weight_one * lambdas[0]
    grad_lambdas[2] = -weight_two * lambdas[3]
    grad_lambdas[3] = -weight_two * lambdas[2]


def shift_all(parts, axis, order, way):
    return [
        lax.ppermute(part, axis, [(i, (i + way * k) % PARTS) for i in range(PARTS)]) if k else part
        for part, k in zip(parts, order)
    ]


def kernel(body, out_shape, in_specs, out_specs, **more):
    return pl.pallas_call(
        body,
        out_shape=out_shape,
        in_specs=in_specs,
        out_specs=out_specs,
        compiler_params=LIMIT,
        **more,
    )


def shaped(shape, dtype=bf16):
    return jax.ShapeDtypeStruct(shape, dtype)


def exchange(value, axes):
    return lax.all_to_all(value, axes, 0, 0, tiled=True)


def attend_call(place, assignment, counts, lambdas, norm_gain, gate, text, vision):
    seqs, toks, columns = text[0].shape
    head_count, head_size = lambdas.shape[1:]
    heads = head_count // PARTS
    slab = vision[0].shape
    rows = slab[1]
    return kernel(
        functools.partial(
            attend_body, heads=heads, head_size=head_size, patch=rows // seqs
        ),
        [shaped((seqs * toks, columns // 2))] * PARTS
        + [shaped(slab)] * PARTS
        + [shaped((FIRST, 4, head_size), f32)],
        [SMEM] * 3 + [VMEM] * (3 + 2 * PARTS),
        [VMEM] * (2 * PARTS + 1),
        scratch_shapes=[
            pltpu.VMEM((2 * head_size, PARTS * toks), f32),
            pltpu.VMEM((seqs, PARTS * PARTS * rows // seqs, PARTS * toks), f32),
            pltpu.VMEM((2 * head_size, head_size), f32),
        ],
    )(place, assignment, counts, lambdas, norm_gain, gate, *text, *vision)


def shards(queries, vision, cotangent, assignment, frame_counts, lambdas, norm_gain, gate_logit):
    seqs, toks, text_columns = queries.shape
    frames_dev, patch, vision_columns = vision.shape[1:]
    head_count, head_size = lambdas.shape[1:]
    heads = head_count // PARTS
    rows = seqs * frames_dev * patch
    place = jnp.stack([lax.axis_index("zl"), lax.axis_index("x")]).astype(jnp.int32)
    slab = shaped((PARTS, rows, vision_columns // PARTS))
    gain_rows = norm_gain.reshape(-1, head_size)
    gate = gate_logit.reshape(1, 1)

    sent_vision = kernel(pack_vision_body, slab, [VMEM], VMEM)(
        vision.reshape(rows, vision_columns)
    )
    row_vision = exchange(sent_vision, "x")
    sent_text = {}
    early = (row_vision, norm_gain.reshape(1, -1), assignment, frame_counts)
    for held, others in (((2,), ()), ((0, 1, 3), early)):
        packed = kernel(
            functools.partial(pack_text_body, shifts=held),
            [shaped((seqs, toks, 2 * text_columns // PARTS))] * len(held),
            [SMEM, ANY, ANY] + [ANY, VMEM, SMEM, SMEM][: len(others)],
            [ANY] * len(held),
            scratch_shapes=[pltpu.SemaphoreType.DMA((len(held), 3))],
        )(place, queries, cotangent, *others)
        sent_text.update(zip(held, packed))
    held_text = shift_all([sent_text[k] for k in ORDER], "x", ORDER, 1)
    held_vision = shift_all([row_vision] * PARTS, "zl", LATE, 1)

    grads = attend_call(
        place,
        assignment,
        frame_counts,
        lambdas,
        norm_gain.reshape(1, -1),
        gate,
        held_text,
        held_vision,
    )
    grad_text, grad_vision, stats = grads[:PARTS], grads[PARTS : 2 * PARTS], grads[2 * PARTS]

    back_vision = shift_all([grad_vision[k] for k in BACK], "zl", BACK, -1)
    stats = exchange(stats, ("y", "x"))
    payload = kernel(
        sum_vision_body,
        [shaped((seqs * toks + 2 * rows, text_columns // PARTS))] * PARTS,
        [SMEM, ANY] + [VMEM] * (2 * PARTS),
        [VMEM] * PARTS,
    )(place, stats, *back_vision, *grad_text)
    back = shift_all(payload, "x", ORDER, -1)
    stats = kernel(spread_sum_body, shaped((SECOND, 4, head_size), f32), [VMEM, ANY], VMEM)(
        stats, payload[0]
    )
    stats = exchange(stats, ("zh", "core", "zl"))
    grad_queries, grad_vision, grad_lambdas, grad_gain, grad_gate = kernel(
        finish_body,
        [
            shaped((seqs * toks, text_columns)),
            shaped((rows, vision_columns)),
            shaped(lambdas.shape, f32),
            shaped(gain_rows.shape, f32),
            shaped((1, 1), f32),
        ],
        [SMEM] + [VMEM] * (4 + PARTS),
        [VMEM] * 5,
    )(place, stats, lambdas, gain_rows, gate, *back)
    return (
        grad_queries.reshape(queries.shape),
        grad_vision.reshape(vision.shape),
        grad_lambdas,
        grad_gain.reshape(norm_gain.shape),
        grad_gate.reshape(gate_logit.shape),
    )


def solution(mesh):
    fine = Mesh(mesh.devices.reshape(8, 2, 2, PARTS, PARTS), DP + IMAGE)
    placed = (
        P(DP, IMAGE, None),
        P(DP, IMAGE, None, None),
        P(DP, IMAGE, None),
        P(DP, None),
        P(DP),
        P(),
        P(),
        P(),
    )
    return jax.shard_map(
        shards,
        mesh=fine,
        in_specs=placed,
        out_specs=(P(DP, IMAGE, None), P(DP, IMAGE, None, None), P(), P(), P()),
        check_vma=False,
    )
```

```python
import functools

import jax
import jax.numpy as jnp
from jax import lax
from jax.experimental import pallas as pl
from jax.experimental.pallas import tpu as pltpu
from jax.sharding import Mesh, PartitionSpec as P

rate_offset = 0.8
epsilon = 1e-05
DP = ("y", "zh", "core")
IMAGE = ("zl", "x")
FIRST, SECOND = 32, 16
PARTS = 4
GROUP = 2
ORDER, LATE, BACK = (0, 2, 1, 3), (0, 3, 1, 2), (0, 1, 2, 3)
VMEM = pl.BlockSpec(memory_space=pltpu.VMEM)
SMEM = pl.BlockSpec(memory_space=pltpu.SMEM)
ANY = pl.BlockSpec(memory_space=pl.ANY)
LIMIT = pltpu.CompilerParams(vmem_limit_bytes=32 * 2**20)
f32, bf16 = jnp.float32, jnp.bfloat16


def dot(a, b, contract):
    return lax.dot_general(
        a, b, ((contract[:1], contract[1:]), ((), ())), preferred_element_type=f32
    )


def wrap(index):
    return lax.rem(index + PARTS, PARTS)


def pack_vision_body(vision, out):
    half = vision.shape[1] // 4
    width = half // PARTS
    for g in range(PARTS):
        out[g, :, :width] = vision[:, g * width : (g + 1) * width]
        out[g, :, width : 2 * width] = vision[:, half + g * width : half + (g + 1) * width]
        out[g, :, 2 * width :] = vision[
            :, 2 * half + 2 * g * width : 2 * half + 2 * (g + 1) * width
        ]


def pack_text_body(place, queries, cotangent, *refs, shifts):
    outs, sems = refs[-1 - len(shifts) : -1], refs[-1]
    half = queries.shape[2] // 2
    width = half // PARTS
    copies = []
    for n, shift in enumerate(shifts):
        g = wrap(place[1] + shift)
        first = pl.multiple_of(g * width, width)
        second = pl.multiple_of(half + g * width, width)
        wide = pl.multiple_of(2 * g * width, 2 * width)
        pieces = (
            (queries.at[:, :, pl.ds(first, width)], pl.ds(0, width)),
            (queries.at[:, :, pl.ds(second, width)], pl.ds(width, width)),
            (cotangent.at[:, :, pl.ds(wide, 2 * width)], pl.ds(2 * width, 2 * width)),
        )
        for i, (source, columns) in enumerate(pieces):
            copies.append(
                pltpu.make_async_copy(source, outs[n].at[:, :, columns], sems.at[n, i])
            )
    for copy in copies:
        copy.start()
    for copy in copies:
        copy.wait()


def attend_body(
    place, assignment, counts, lambdas, norm_gain, gate, *refs, heads, head_size, patch
):
    text, vision, grad_text, grad_vision = (refs[i * PARTS : (i + 1) * PARTS] for i in range(4))
    vision = [vision[LATE.index(k)] for k in range(PARTS)]
    stats, gain, bias, raw_gain = refs[4 * PARTS :]
    zl, x = place[0], place[1]
    seqs, toks = text[0].shape[:2]
    rows = PARTS * toks
    frames = PARTS * PARTS
    keys = frames * patch
    width = heads * head_size
    wide = 2 * head_size
    scale = head_size ** (-0.5)
    first_exp = jnp.exp(jnp.sum(lambdas[0] * lambdas[1], axis=-1, keepdims=True))
    second_exp = jnp.exp(jnp.sum(lambdas[2] * lambdas[3], axis=-1, keepdims=True))
    all_rates = first_exp - second_exp + rate_offset
    head_index = lax.broadcasted_iota(jnp.int32, all_rates.shape, 0)
    shape = (wide, wide)
    diagonal = lax.broadcasted_iota(jnp.int32, shape, 0) == lax.broadcasted_iota(
        jnp.int32, shape, 1
    )
    eye = jnp.where(diagonal, 1.0, 0.0).astype(bf16)
    gain_row = norm_gain[...] * (jnp.tanh(gate[...]) * (1.0 - rate_offset))
    gain[...] = jnp.broadcast_to(
        jnp.sum(jnp.where(diagonal, gain_row, 0.0), axis=1, keepdims=True), gain.shape
    )
    spot = lax.broadcasted_iota(jnp.int32, (keys, rows), 0) // patch
    part = spot // PARTS
    frame = wrap(zl - part) * PARTS + spot - part * PARTS
    for v in range(seqs):
        bias[v] = jnp.where(frame < counts[v], 0.0, -jnp.inf)
    lane = lax.broadcasted_iota(jnp.int32, (1, head_size), 1)
    rate_row = jnp.zeros((1, head_size), f32)

    def map_columns(h, m):
        return pl.ds(m * width + h * head_size, head_size)

    def value_columns(h):
        return pl.ds(2 * width + h * wide, wide)

    def block(columns):
        joined = jnp.concatenate([part[:, :, columns] for part in vision], axis=0)
        return joined.astype(f32).reshape(frames, seqs, patch, -1)

    def of_video(joined, v):
        return joined[:, v].reshape(keys, -1).astype(bf16)

    place_of = [jnp.where(assignment[0, 0] == v, 0, 1) for v in range(seqs)]
    for first in range(0, heads, GROUP):
        chains = [(h, v) for h in range(first, first + GROUP) for v in range(seqs)]
        both = [(h, v, m) for h, v in chains for m in range(2)]
        rates, joined = {}, {}
        for h in range(first, first + GROUP):
            rates[h] = jnp.sum(
                jnp.where(head_index == x * heads + h, all_rates, 0.0), axis=0, keepdims=True
            )
            joined[h] = block(value_columns(h))
            for m in range(2):
                joined[h, m] = block(map_columns(h, m))
        values = {(h, v): of_video(joined[h], v) for h, v in chains}
        key_rows = {(h, v, m): of_video(joined[h, m], v) for h, v, m in both}
        queries = {
            (h, v, m): jnp.concatenate(
                [part[place_of[v], :, map_columns(h, m)] for part in text], axis=0
            )
            for h, v, m in both
        }
        scores = {c: dot(key_rows[c], queries[c], (1, 1)) + bias[c[1]] for c in both}
        shifted = {
            c: jnp.exp((scores[c] - jnp.max(scores[c], axis=0, keepdims=True)) * scale)
            for c in both
        }
        probs = {
            c: shifted[c] * (1.0 / jnp.sum(shifted[c], axis=0, keepdims=True)) for c in both
        }
        rated = {c: rates[c[0]] * probs[(*c, 1)] for c in chains}
        mixed = {c: (probs[(*c, 0)] - rated[c]).astype(bf16) for c in chains}
        attended = {c: dot(values[c], mixed[c], (0, 0)) for c in chains}
        grad_out = {
            (h, v): dot(
                eye,
                jnp.concatenate(
                    [part[place_of[v], :, value_columns(h)] for part in text], axis=0
                ),
                (1, 1),
            )
            for h, v in chains
        }
        inverse_rms = {
            c: lax.rsqrt(jnp.mean(attended[c] * attended[c], axis=0, keepdims=True) + epsilon)
            for c in chains
        }
        grad_attended = {}
        for c in chains:
            normed = attended[c] * inverse_rms[c]
            product = grad_out[c] * normed
            halves = product[:, :head_size] + product[:, head_size:]
            raw_gain[...] = halves if c == (0, 0) else raw_gain[...] + halves
            middle = jnp.mean(product * gain[...], axis=0, keepdims=True)
            grad_attended[c] = (
                inverse_rms[c] * (grad_out[c] * gain[...] - normed * middle)
            ).astype(bf16)
        grad_mixed = {c: dot(values[c], grad_attended[c], (1, 0)) * scale for c in chains}
        grad_values = {c: dot(mixed[c], grad_attended[c], (1, 1)) for c in chains}
        sums = {
            c: jnp.sum(grad_mixed[c[:2]] * probs[c], axis=0, keepdims=True) for c in both
        }
        grad_scores = {}
        for c in chains:
            grad_scores[(*c, 0)] = (probs[(*c, 0)] * (grad_mixed[c] - sums[(*c, 0)])).astype(bf16)
            grad_scores[(*c, 1)] = (rated[c] * (sums[(*c, 1)] - grad_mixed[c])).astype(bf16)
        grad_keys = {c: dot(grad_scores[c], queries[c], (1, 0)) for c in both}
        for h, v, m in both:
            grad_query = dot(grad_scores[h, v, m], key_rows[h, v, m], (0, 0)).astype(bf16)
            own_rows = pl.ds(pl.multiple_of(place_of[v] * toks, toks), toks)
            for i in range(PARTS):
                grad_text[i][own_rows, map_columns(h, m)] = grad_query[i * toks : (i + 1) * toks]
        for h in range(first, first + GROUP):
            for columns, parts in (
                (map_columns(h, 0), [grad_keys[h, v, 0] for v in range(seqs)]),
                (map_columns(h, 1), [grad_keys[h, v, 1] for v in range(seqs)]),
                (value_columns(h), [grad_values[h, v] for v in range(seqs)]),
            ):
                parts = [p.reshape(frames, patch, -1) for p in parts]
                total = jnp.concatenate(parts, axis=1).astype(bf16)
                for j in range(PARTS):
                    grad_vision[j][:, :, columns] = total[j * PARTS : (j + 1) * PARTS]
            total_rate = sum(sums[h, v, 1] for v in range(seqs))
            own_rate = jnp.sum(total_rate, axis=1, keepdims=True) * (-1.0 / scale)
            rate_row = jnp.where(lane == x * heads + h, own_rate, rate_row)
    gains = jnp.sum(raw_gain[...].T, axis=0, keepdims=True)
    row = lax.broadcasted_iota(jnp.int32, stats.shape[1:], 0)
    tile = jnp.where(row == 0, gains[:, :head_size], 0.0)
    tile = jnp.where(row == 1, gains[:, head_size:], tile)
    tile = jnp.where(row == 2, rate_row, tile)
    for i in range(stats.shape[0]):
        stats[i] = tile


def sum_vision_body(place, after, *refs):
    del after
    parts, text, outs = (refs[i * PARTS : (i + 1) * PARTS] for i in range(3))
    for k, out in enumerate(outs):
        x = wrap(place[1] - ORDER[k])
        value = parts[0][x].astype(f32)
        for part in parts[1:]:
            value = value + part[x].astype(f32)
        value = value.astype(bf16)
        text_rows, columns = text[k].shape
        rows = value.shape[0]
        out[:text_rows] = text[k][...]
        out[text_rows : text_rows + rows] = value[:, :columns]
        out[text_rows + rows :] = value[:, columns:]


def spread_sum_body(tiles, after, out):
    del after
    total = jnp.sum(tiles[...], axis=0)
    for i in range(out.shape[0]):
        out[i] = total


def finish_body(place, tiles, lambdas, norm_gain, gate, *refs):
    parts, grad_queries, grad_vision, grad_lambdas, grad_gain, grad_gate = (
        refs[:PARTS],
        *refs[PARTS:],
    )
    text_rows, rows = grad_queries.shape[0], grad_vision.shape[0]
    half = grad_queries.shape[1] // 2
    width = half // PARTS
    for k in range(PARTS):
        g = wrap(place[1] + ORDER[k])
        first = pl.multiple_of(g * width, width)
        second = pl.multiple_of(half + g * width, width)
        wide = pl.multiple_of(2 * half + 2 * g * width, 2 * width)
        own = parts[k]
        grad_queries[:, pl.ds(first, width)] = own[:text_rows, :width]
        grad_queries[:, pl.ds(second, width)] = own[:text_rows, width:]
        grad_vision[:, pl.ds(first, width)] = own[text_rows : text_rows + rows, :width]
        grad_vision[:, pl.ds(second, width)] = own[text_rows : text_rows + rows, width:]
        grad_vision[:, pl.ds(wide, 2 * width)] = own[text_rows + rows :, :]
    total = jnp.sum(tiles[...], axis=0)
    head_count, head_size = lambdas.shape[1:]
    gate_tanh = jnp.tanh(gate[...])
    grad_gain[...] = total[:2] * (gate_tanh * (1.0 - rate_offset))
    weighed = jnp.sum(total[:2] * norm_gain[...], axis=-1, keepdims=True)
    grad_gate[...] = (
        jnp.sum(weighed, axis=0, keepdims=True)
        * (1.0 - rate_offset)
        * (1.0 - gate_tanh * gate_tanh)
    )
    shape = (head_count, head_size)
    own = lax.broadcasted_iota(jnp.int32, shape, 0) == lax.broadcasted_iota(jnp.int32, shape, 1)
    grad_rate = jnp.sum(jnp.where(own, total[2:3], 0.0), axis=-1, keepdims=True)
    first_exp = jnp.exp(jnp.sum(lambdas[0] * lambdas[1], axis=-1, keepdims=True))
    second_exp = jnp.exp(jnp.sum(lambdas[2] * lambdas[3], axis=-1, keepdims=True))
    weight_one, weight_two = grad_rate * first_exp, grad_rate * second_exp
    grad_lambdas[0] = weight_one * lambdas[1]
    grad_lambdas[1] = weight_one * lambdas[0]
    grad_lambdas[2] = -weight_two * lambdas[3]
    grad_lambdas[3] = -weight_two * lambdas[2]


def shift_all(parts, axis, order, way):
    return [
        lax.ppermute(part, axis, [(i, (i + way * k) % PARTS) for i in range(PARTS)]) if k else part
        for part, k in zip(parts, order)
    ]


def kernel(body, out_shape, in_specs, out_specs, **more):
    return pl.pallas_call(
        body,
        out_shape=out_shape,
        in_specs=in_specs,
        out_specs=out_specs,
        compiler_params=LIMIT,
        **more,
    )


def shaped(shape, dtype=bf16):
    return jax.ShapeDtypeStruct(shape, dtype)


def exchange(value, axes):
    return lax.all_to_all(value, axes, 0, 0, tiled=True)


def attend_call(place, assignment, counts, lambdas, norm_gain, gate, text, vision):
    seqs, toks, columns = text[0].shape
    head_count, head_size = lambdas.shape[1:]
    heads = head_count // PARTS
    slab = vision[0].shape
    rows = slab[1]
    return kernel(
        functools.partial(
            attend_body, heads=heads, head_size=head_size, patch=rows // seqs
        ),
        [shaped((seqs * toks, columns // 2))] * PARTS
        + [shaped(slab)] * PARTS
        + [shaped((FIRST, 4, head_size), f32)],
        [SMEM] * 3 + [VMEM] * (3 + 2 * PARTS),
        [VMEM] * (2 * PARTS + 1),
        scratch_shapes=[
            pltpu.VMEM((2 * head_size, PARTS * toks), f32),
            pltpu.VMEM((seqs, PARTS * PARTS * rows // seqs, PARTS * toks), f32),
            pltpu.VMEM((2 * head_size, head_size), f32),
        ],
    )(place, assignment, counts, lambdas, norm_gain, gate, *text, *vision)


def shards(queries, vision, cotangent, assignment, frame_counts, lambdas, norm_gain, gate_logit):
    seqs, toks, text_columns = queries.shape
    frames_dev, patch, vision_columns = vision.shape[1:]
    head_count, head_size = lambdas.shape[1:]
    heads = head_count // PARTS
    rows = seqs * frames_dev * patch
    place = jnp.stack([lax.axis_index("zl"), lax.axis_index("x")]).astype(jnp.int32)
    slab = shaped((PARTS, rows, vision_columns // PARTS))
    gain_rows = norm_gain.reshape(-1, head_size)
    gate = gate_logit.reshape(1, 1)

    sent_vision = kernel(pack_vision_body, slab, [VMEM], VMEM)(
        vision.reshape(rows, vision_columns)
    )
    row_vision = exchange(sent_vision, "x")
    sent_text = {}
    early = (row_vision, norm_gain.reshape(1, -1), assignment, frame_counts)
    for held, others in (((2,), ()), ((0, 1, 3), early)):
        packed = kernel(
            functools.partial(pack_text_body, shifts=held),
            [shaped((seqs, toks, 2 * text_columns // PARTS))] * len(held),
            [SMEM, ANY, ANY] + [ANY, VMEM, SMEM, SMEM][: len(others)],
            [ANY] * len(held),
            scratch_shapes=[pltpu.SemaphoreType.DMA((len(held), 3))],
        )(place, queries, cotangent, *others)
        sent_text.update(zip(held, packed))
    held_text = shift_all([sent_text[k] for k in ORDER], "x", ORDER, 1)
    held_vision = shift_all([row_vision] * PARTS, "zl", LATE, 1)

    grads = attend_call(
        place,
        assignment,
        frame_counts,
        lambdas,
        norm_gain.reshape(1, -1),
        gate,
        held_text,
        held_vision,
    )
    grad_text, grad_vision, stats = grads[:PARTS], grads[PARTS : 2 * PARTS], grads[2 * PARTS]

    back_vision = shift_all([grad_vision[k] for k in BACK], "zl", BACK, -1)
    stats = exchange(stats, ("y", "x"))
    payload = kernel(
        sum_vision_body,
        [shaped((seqs * toks + 2 * rows, text_columns // PARTS))] * PARTS,
        [SMEM, ANY] + [VMEM] * (2 * PARTS),
        [VMEM] * PARTS,
    )(place, stats, *back_vision, *grad_text)
    back = shift_all(payload, "x", ORDER, -1)
    stats = kernel(spread_sum_body, shaped((SECOND, 4, head_size), f32), [VMEM, ANY], VMEM)(
        stats, payload[0]
    )
    stats = exchange(stats, ("zh", "core", "zl"))
    grad_queries, grad_vision, grad_lambdas, grad_gain, grad_gate = kernel(
        finish_body,
        [
            shaped((seqs * toks, text_columns)),
            shaped((rows, vision_columns)),
            shaped(lambdas.shape, f32),
            shaped(gain_rows.shape, f32),
            shaped((1, 1), f32),
        ],
        [SMEM] + [VMEM] * (4 + PARTS),
        [VMEM] * 5,
    )(place, stats, lambdas, gain_rows, gate, *back)
    return (
        grad_queries.reshape(queries.shape),
        grad_vision.reshape(vision.shape),
        grad_lambdas,
        grad_gain.reshape(norm_gain.shape),
        grad_gate.reshape(gate_logit.shape),
    )


def solution(mesh):
    fine = Mesh(mesh.devices.reshape(8, 2, 2, PARTS, PARTS), DP + IMAGE)
    placed = (
        P(DP, IMAGE, None),
        P(DP, IMAGE, None, None),
        P(DP, IMAGE, None),
        P(DP, None),
        P(DP),
        P(),
        P(),
        P(),
    )
    return jax.shard_map(
        shards,
        mesh=fine,
        in_specs=placed,
        out_specs=(P(DP, IMAGE, None), P(DP, IMAGE, None, None), P(), P(), P()),
        check_vma=False,
    )
```
